256 devices in a mesh: gx: 16 (over z, core), gy: 4 (over y), gz: 4 (over x).
Axes of the slice: x: 4, y: 4, z: 8, core: 2. Of those that a mesh axis runs over, the one named last changes fastest.
Arguments:
- facies: int32 [32, 256, 512], P('gz', 'gx', 'gy'), may hold values from 0 to 7
- boundary: int32 [32, 256, 512], P('gz', 'gx', 'gy'), may hold values from 0 to 2, as said below
- horizontal_conductivity: float32 [8], replicated, may hold values from 0.2 to 5
- vertical_conductivity: float32 [8], replicated, may hold values from 0.1 to 2
- source: float32 [32, 256, 512], P('gz', 'gx', 'gy'), may hold values from -20 to 20
- density: float32 [32, 256, 512], P('gz', 'gx', 'gy'), may hold values from 0 to 4
Outputs:
- pressure: float32 [32, 256, 512], P('gz', 'gx', 'gy')
- residual: float32 [32, 256, 512], P('gz', 'gx', 'gy')
The draws below stay inside these ranges and needn't reach their ends.
Inputs may be any that keep to these rules, and one draw needn't show every extreme that they name: 0 inland, 1 sea boundary, 2 river boundary; boundary cells are few.
All inputs are finite; a program needn't handle non-finite values.
Results may differ from the reference program's by a relative error of at most 0.0003.
Values sent between devices are 32-bit elements; how exact they have to be, the bound alone decides.
No kernel may reach another device: no remote copies, remote signals or barrier semaphores. Data moves between devices by JAX's collectives and lax.ppermute only.
A program may use at most 256 MiB of HBM per device.

```python
import math
import jax
import jax.numpy as jnp

NF = 8
LEVELS = 5
NU = 2
COARSE_SWEEPS = 8
NZ = 32
NX = 256
NY = 512


def smooth_part(key, level, swing):
    phases = jax.random.uniform(key, (3,), jnp.float32, 0.0, 2.0 * math.pi)
    xpos = jnp.arange(NX, dtype=jnp.float32)[None, :, None] / NX
    ypos = jnp.arange(NY, dtype=jnp.float32)[None, None, :] / NY
    zpos = jnp.arange(NZ, dtype=jnp.float32)[:, None, None] / NZ
    wave = jnp.cos(2.0 * math.pi * xpos + phases[0]) * jnp.cos(2.0 * math.pi * ypos + phases[1])
    tilt = jnp.cos(math.pi * zpos + phases[2])
    return level + swing * (0.7 * wave + 0.3 * tilt)


def draw_source(key, part):
    key = jax.random.fold_in(key, 3)
    first, second = jax.random.split(key)
    rough = jnp.clip(jax.random.normal(second, (NZ, NX, NY), jnp.float32), -5.0, 5.0)
    return smooth_part(first, 4.5, 3.0) + 2.0 * rough


def draw_boundary(key, part):
    key = jax.random.fold_in(key, 7)
    values = jax.random.randint(key, (NZ, NX, NY), 0, 64)
    return jnp.where(values == 0, 1, jnp.where(values == 1, 2, 0)).astype(jnp.int32)


def place_ends(array, rng, smallest, high):
    spot = [jax.random.randint(jax.random.fold_in(rng, axis), (), 0, length) for axis, length in enumerate(array.shape)]
    main_axis = array.shape.index(max(array.shape))
    next_to = spot[:main_axis] + [(spot[main_axis] + 1) % array.shape[main_axis]] + spot[main_axis + 1:]
    return array.at[tuple(spot)].set(smallest).at[tuple(next_to)].set(high)


def steps_of(stream_key, extent, cuts, least, top_value):
    def one(dim, parts):
        draws = jax.random.uniform(jax.random.fold_in(jax.random.fold_in(stream_key, 6), dim), (parts,), jnp.float32, least / len(cuts), top_value / len(cuts))
        return jnp.repeat(jnp.exp(draws), extent[dim] // parts).reshape((-1,) + (1,) * (len(extent) - dim - 1))

    gain = one(*cuts[0])
    for cut in cuts[1:]:
        gain = gain * one(*cut)
    return gain


def setup_inputs(seed: int = 0) -> dict:
    splits = jax.random.split(jax.random.key(seed), 7)
    facies = place_ends(jax.random.randint(splits[0], (NZ, NX, NY), 0, NF), jax.random.fold_in(splits[0], 1), 0, NF - 1).astype(jnp.int32)
    boundary = draw_boundary(jax.random.fold_in(splits[6], 71), 0)
    horizontal_conductivity = jnp.clip(jnp.exp(jax.random.uniform(splits[2], (NF,), jnp.float32, math.log(0.2), math.log(5.0))), 0.2, 5.0)
    vertical_conductivity = jnp.clip(jnp.exp(jax.random.uniform(splits[3], (NF,), jnp.float32, math.log(0.1), math.log(2.0))), 0.1, 2.0)
    source = draw_source(jax.random.fold_in(splits[6], 71), 0)
    density = jnp.clip(4.0 * jax.random.uniform(splits[5], (NZ, NX, NY), jnp.float32) ** steps_of(splits[5], (NZ, NX, NY), ((0, 4), (1, 16), (2, 4)), -0.2, 0.2), 0.0, 4.0)
    return dict(facies=facies, boundary=boundary, horizontal_conductivity=horizontal_conductivity, vertical_conductivity=vertical_conductivity, source=source, density=density)


relax_weight = 2.0 / 3.0


def lookup(indices, table):
    result = jnp.zeros(indices.shape, jnp.float32)
    for entry in range(table.shape[0]):
        result = jnp.where(indices == entry, table[entry], result)
    return result


def harmonic(center, beyond):
    return 2.0 * center * beyond / (center + beyond)


def material(horizontal, vertical, density, boundary, source, pad_h, pad_v, pad_rho):
    couplings = [harmonic(vertical, pad_v[:-2, 1:-1, 1:-1]), harmonic(vertical, pad_v[2:, 1:-1, 1:-1]),
                 harmonic(horizontal, pad_h[1:-1, :-2, 1:-1]), harmonic(horizontal, pad_h[1:-1, 2:, 1:-1]),
                 harmonic(horizontal, pad_h[1:-1, 1:-1, :-2]), harmonic(horizontal, pad_h[1:-1, 1:-1, 2:])]
    sink_term = jnp.where(boundary == 1, 2.0 * vertical, jnp.where(boundary == 2, 0.5 * horizontal, 0.0))
    forcing = source + 0.5 * couplings[1] * (density + pad_rho[2:, 1:-1, 1:-1]) - 0.5 * couplings[0] * (pad_rho[:-2, 1:-1, 1:-1] + density)
    return jnp.stack(couplings + [sink_term]), forcing


def blocks(values):
    depth_z, depth_x, depth_y = values.shape
    return values.reshape(depth_z // 2, 2, depth_x // 2, 2, depth_y // 2, 2)


def coarsen(operators):
    return jnp.stack([
        blocks(operators[0])[:, 0].sum(axis=(2, 4)), blocks(operators[1])[:, 1].sum(axis=(2, 4)),
        blocks(operators[2])[:, :, :, 0].sum(axis=(1, 4)), blocks(operators[3])[:, :, :, 1].sum(axis=(1, 4)),
        blocks(operators[4])[..., 0].sum(axis=(1, 3)), blocks(operators[5])[..., 1].sum(axis=(1, 3)),
        blocks(operators[6]).sum(axis=(1, 3, 5))])


def restrict(values):
    return blocks(values).sum(axis=(1, 3, 5))


def prolong(values):
    depth_z, depth_x, depth_y = values.shape
    spread_out = jnp.broadcast_to(values[:, None, :, None, :, None], (depth_z, 2, depth_x, 2, depth_y, 2))
    return spread_out.reshape(2 * depth_z, 2 * depth_x, 2 * depth_y)


def diagonal(operators):
    return operators[6] + operators[0] + operators[1] + operators[2] + operators[3] + operators[4] + operators[5]


def apply_operator(operators, diag, field, padded):
    beside = operators[0] * padded[:-2, 1:-1, 1:-1] + operators[1] * padded[2:, 1:-1, 1:-1]
    beside = beside + operators[2] * padded[1:-1, :-2, 1:-1] + operators[3] * padded[1:-1, 2:, 1:-1]
    beside = beside + operators[4] * padded[1:-1, 1:-1, :-2] + operators[5] * padded[1:-1, 1:-1, 2:]
    return diag * field - beside


def smooth(operators, diag, target, field, sweeps):
    for sweep_index in range(sweeps):
        field = field + relax_weight * (target - apply_operator(operators, diag, field, jnp.pad(field, 1))) / diag
    return field


def reference(facies, boundary, horizontal_conductivity, vertical_conductivity, source, density):
    horizontal = lookup(facies, horizontal_conductivity)
    vertical = lookup(facies, vertical_conductivity)
    first, forcing = material(horizontal, vertical, density, boundary, source,
                              jnp.pad(horizontal, 1), jnp.pad(vertical, 1), jnp.pad(density, 1))
    operators = [first]
    for this_level in range(LEVELS):
        operators.append(coarsen(operators[-1]))
    diagonals = [diagonal(item) for item in operators]

    def cycle(this_level, target):
        stencil, diag = operators[this_level], diagonals[this_level]
        field = relax_weight * target / diag
        if this_level == LEVELS:
            return smooth(stencil, diag, target, field, COARSE_SWEEPS - 1)
        field = smooth(stencil, diag, target, field, NU - 1)
        coarse = restrict(target - apply_operator(stencil, diag, field, jnp.pad(field, 1)))
        field = field + prolong(cycle(this_level + 1, coarse))
        return smooth(stencil, diag, target, field, NU)

    pressure = cycle(0, forcing)
    residual = forcing - apply_operator(operators[0], diagonals[0], pressure, jnp.pad(pressure, 1))
    return pressure, residual
```

```python
import jax
import jax.numpy as jnp
from jax import lax
from jax.experimental import pallas as pl
from jax.experimental.pallas import tpu as pltpu
from jax.sharding import PartitionSpec as P

COARSE_SWEEPS = 8
W = 2.0 / 3.0
F32 = jnp.float32
UX, UY, UZ, RD, C, V = range(6)
SINK = RD
H = 5
Z0 = 8 + 2 * H

VMEM = pl.BlockSpec(memory_space=pltpu.VMEM)
SMEM = pl.BlockSpec(memory_space=pltpu.SMEM)


def call(kernel, outs, *args, scratch=(), smem=0):
    specs = [SMEM] * smem + [VMEM] * (len(args) - smem)
    return pl.pallas_call(
        kernel,
        out_shape=[jax.ShapeDtypeStruct(s, F32) for s in outs],
        in_specs=specs,
        out_specs=[VMEM] * len(outs),
        scratch_shapes=[pltpu.VMEM(s, F32) for s in scratch],
        compiler_params=pltpu.CompilerParams(vmem_limit_bytes=50 * 2**20),
    )(*args)


def iota(shape, dim):
    return lax.broadcasted_iota(jnp.int32, shape, dim)


def dot(a, b):
    return lax.dot_general(
        a, b, (((1,), (0,)), ((), ())), precision=lax.Precision.HIGHEST, preferred_element_type=F32
    )


def dot_nt(a, b):
    return lax.dot_general(
        a, b, (((1,), (1,)), ((), ())), precision=lax.Precision.HIGHEST, preferred_element_type=F32
    )


def onehot(cond):
    return jnp.where(cond, 1.0, 0.0).astype(F32)


def up(a, dim):
    return pltpu.roll(a, a.shape[dim] - 1, dim)


def down(a, dim):
    return pltpu.roll(a, 1, dim)


def each(start, stop, body):
    def step(z, carry):
        body(z)
        return carry

    lax.fori_loop(start, stop, step, 0)


def wrap(z, n):
    return lax.rem(z + n, n)


def around(a, field, z, zm, zp):
    v = field(z)
    ux, uy = a[UX, z], a[UY, z]
    out = ux * up(v, 0) + down(ux * v, 0)
    out = out + (uy * up(v, 1) + down(uy * v, 1))
    return v, out + (a[UZ, z] * field(zp) + a[UZ, zm] * field(zm))


def smoothed(a, field, z, zm, zp):
    v, beside = around(a, field, z, zm, zp)
    return v * (1.0 / 3.0) + a[C, z] + a[RD, z] * beside


def finish(a, d, r, z, zm):
    ux, uy = a[UX, z], a[UY, z]
    diag = a[SINK, z] + a[UZ, z] + a[UZ, zm] + ux + down(ux, 0) + uy + down(uy, 1)
    d[z] = diag
    rd = jnp.where(diag > 0.0, W / jnp.where(diag > 0.0, diag, 1.0), 0.0)
    a[RD, z] = rd
    if r is not None:
        a[C, z] = rd * r[z]


def circ(n):
    return lambda z: (z, wrap(z - 1, n), wrap(z + 1, n))


def pre(a, d, r, res, n):
    c3 = circ(n)
    each(0, n, lambda z: finish(a, d, r, z, wrap(z - 1, n)))

    def one(z):
        a[V, z] = smoothed(a, lambda k: a[C, k], *c3(z))

    each(0, n, one)
    if res is not None:

        def two(z):
            v, beside = around(a, lambda k: a[V, k], *c3(z))
            res[z] = d[z] * (1.5 * a[C, z] - v) + beside

        each(0, n, two)


def pair_rows(t, n):
    return t[pl.ds(0, n, stride=2), :] + t[pl.ds(1, n, stride=2), :]


def halve(a, sink, r, t, store, n, rows):
    odd_row = iota((rows, 128), 0) % 2 == 1
    odd_lane = iota((rows, 128), 1) % 2 == 1

    def body(z):
        lo, hi = 2 * z, 2 * z + 1
        parts = (
            jnp.where(odd_row, a[UX, lo] + a[UX, hi], 0.0),
            jnp.where(odd_lane, a[UY, lo] + a[UY, hi], 0.0),
            a[UZ, hi],
            sink[lo] + sink[hi],
            r[lo] + r[hi],
        )
        for k, part in enumerate(parts):
            t[k] = part
        for k in range(5):
            store(k, z, pair_rows(t.at[k], rows // 2))

    each(0, n // 2, body)


def stretch(e, q, p):
    return dot(dot(q, e), p)


def pack_z(f, b, s, d, lo, hi):
    for k, ref in enumerate((f, b, s, d)):
        lo[k] = ref[0:H].astype(F32)
        hi[k] = ref[8 - H : 8].astype(F32)


def pack_x(f, b, s, d, above, below, lo, hi):
    for out, row in ((lo, 0), (hi, 8)):
        for k, ref in enumerate((f, b, s, d)):
            out[k, 0:H] = below[k, :, row : row + 8]
            out[k, H : H + 8] = ref[:, row : row + 8].astype(F32)
            out[k, H + 8 : Z0] = above[k, :, row : row + 8]


ROWS0 = 4 * Z0 * 32


def pack_y(xl, xh, rl, rh, lo, hi):
    whole = jnp.concatenate([xl[...], xh[...], rl[...], rh[...]], axis=2).reshape(ROWS0, 128)
    i, j = iota((16, 128), 0), iota((16, 128), 1)
    edges = dot_nt(onehot(j == jnp.where(i < 8, i, 112 + i)), whole)
    lo[...] = edges[0:8]
    hi[...] = edges[8:16]


def level0(pos, hc, vc, xl, xh, rl, rh, yl, yh, a, packed, raw, hs, vs, dd, res, sk, t, m):
    gx, gy, gz = pos[0], pos[1], pos[2]
    i, j = iota((16, 128), 0), iota((16, 128), 1)
    place = onehot(j == jnp.where(i < 8, i, 112 + i))
    sides = jnp.concatenate([yl[...], yh[...]], axis=0)
    beyond = dot(jnp.transpose(sides), place).reshape(4, Z0, 32, 128)
    raw[:, :, :, 128:256] = beyond
    for row, ref in ((0, xl), (8, xh), (16, rl), (24, rh)):
        raw[:, :, row : row + 8, 0:128] = ref[...]

    row, lane = iota((32, 256), 0), iota((32, 256), 1)
    x = gx * 16 + jnp.where(row < 24, row, row - 32)
    y = gy * 128 + jnp.where(lane < 192, lane, lane - 256)
    inside = (x >= 0) & (x < 256) & (y >= 0) & (y < 512)
    own = (jnp.where(row < 24, 1, 0) * jnp.where(lane < 192, 1, 0)) > 0
    del own

    def materials(z):
        zg = gz * 8 + z - H
        here = inside & ((zg >= 0) & (zg < 32))
        kind = raw[0, z]
        h = jnp.full((32, 256), hc[0], F32)
        v = jnp.full((32, 256), vc[0], F32)
        for n in range(1, 8):
            is_n = kind == float(n)
            h = jnp.where(is_n, hc[n], h)
            v = jnp.where(is_n, vc[n], v)
        hs[z] = jnp.where(here, h, 0.0)
        vs[z] = jnp.where(here, v, 0.0)

    each(0, Z0, materials)

    def harmonic(c, n):
        s = c + n
        return 2.0 * c * n / jnp.where(s > 0.0, s, 1.0)

    def couple(z):
        h = hs[z]
        a[UX, z] = harmonic(h, up(h, 0))
        a[UY, z] = harmonic(h, up(h, 1))
        a[UZ, z] = harmonic(vs[z], vs[z + 1])

    each(0, Z0 - 1, couple)

    odd_row, odd_lane = row % 2 == 1, lane % 2 == 1

    def setup(z):
        h, v = hs[z], vs[z]
        sink = jnp.where(raw[1, z] == 1.0, 2.0 * v, jnp.where(raw[1, z] == 2.0, 0.5 * h, 0.0))
        ux, uy, uz, lz = a[UX, z], a[UY, z], a[UZ, z], a[UZ, z - 1]
        lx, ly = down(ux, 0), down(uy, 1)
        diag = sink + lz + uz + lx + ux + ly + uy
        dens = raw[3, z]
        b = raw[2, z] + 0.5 * uz * (dens + raw[3, z + 1]) - 0.5 * lz * (raw[3, z - 1] + dens)
        rd = jnp.where(diag > 0.0, W / jnp.where(diag > 0.0, diag, 1.0), 0.0)
        a[RD, z] = rd
        a[C, z] = rd * b
        dd[z] = diag
        sk[z] = sink
        outer = sink + jnp.where(odd_row, ux, lx) + jnp.where(odd_lane, uy, ly)
        hs[z] = outer + jnp.where((z - H) % 2 == 1, uz, lz)

    each(1, Z0 - 1, setup)

    def first(z):
        a[V, z] = smoothed(a, lambda k: a[C, k], z, z - 1, z + 1)

    each(2, Z0 - 2, first)

    def residual(z):
        v, beside = around(a, lambda k: a[V, k], z, z - 1, z + 1)
        res[z - H] = (dd[z] * (1.5 * a[C, z] - v) + beside)[0:16, 0:128]

    each(H, H + 8, residual)

    o_row = iota((16, 128), 0) % 2 == 1
    o_lane = iota((16, 128), 1) % 2 == 1

    def coarsen(z):
        lo, hi = H + 2 * z, H + 2 * z + 1

        def both(ref):
            return ref[lo, 0:16, 0:128] + ref[hi, 0:16, 0:128]

        parts = (
            jnp.where(o_row, both(a.at[UX]), 0.0),
            jnp.where(o_lane, both(a.at[UY]), 0.0),
            a[UZ, hi, 0:16, 0:128],
            both(sk),
            res[2 * z] + res[2 * z + 1],
            both(hs),
        )
        for k, part in enumerate(parts):
            t[k] = part
        for k in range(6):
            m[lax.div(z, 2), k, lax.rem(z, 2)] = pair_rows(t.at[k], 8)

    each(0, 4, coarsen)
    i, j = iota((128, 128), 0), iota((128, 128), 1)
    out = dot(m[0].reshape(96, 128), onehot(j == i // 2))
    out = out + dot(m[1].reshape(96, 128), onehot(j == 64 + i // 2))
    out = out.reshape(6, 2, 8, 128)
    packed[0:4] = out[0:4]
    packed[4] = W * out[4] / out[5]


def pack_x1(own, b1, b2, b3, full, lo, hi):
    for n, ref in enumerate((own, b1, b2, b3)):
        full[:, 2 * n : 2 * n + 2] = ref[...]
        first, second = ref[:, 0], ref[:, 1]
        lo[:, n] = jnp.concatenate([first[:, 0:4], second[:, 0:4]], axis=1)
        hi[:, n] = jnp.concatenate([first[:, 4:8], second[:, 4:8]], axis=1)


def pack_y1(own, r1, l1, r2, l2, whole, lo, hi):
    whole[:, :, 0:8] = own[...]
    whole[:, :, 8:16] = r1[...]
    whole[:, :, 24:32] = l1[...]
    for n in range(4):
        for s in range(2):
            part = slice(4 * s, 4 * s + 4)
            whole[:, 2 * n + s, 16:24] = jnp.concatenate([r2[:, n, part], l2[:, n, part]], axis=1)
    i, j = iota((64, 128), 0), iota((64, 128), 1)
    half, k = (i // 16) % 2, i % 16
    lane = jnp.where(i < 32, k, 48 + k) + 64 * half
    edges = dot_nt(onehot(j == lane), whole[...].reshape(1280, 128))
    lo[...] = edges[0:32]
    hi[...] = edges[32:64]


def sums(n, width):
    i, j = iota((128, 128), 0), iota((128, 128), 1)
    return onehot((i < n) & (j % width == i // 2))


def level12(pos, whole, yl, yh, a, b, sent, d1, r1, t1, m1, d2, r2, s1, s2, q2, m2):
    gx, gy, gz = pos[0], pos[1], pos[2]
    sides = jnp.transpose(jnp.concatenate([yl[...], yh[...]], axis=0))
    i, j = iota((64, 128), 0), iota((64, 128), 1)
    side, half, k = i // 32, (i // 16) % 2, i % 16
    to = jnp.where(side == 0, 64 + k, 112 + k)
    row, lane = iota((32, 128), 0), iota((32, 128), 1)
    x = gx * 8 + jnp.where(row < 20, row, row - 32)
    y = gy * 64 + jnp.where(lane < 96, lane, lane - 128)
    inside = (x >= 0) & (x < 128) & (y >= 0) & (y < 256)
    for part in range(2):
        beyond = dot(sides, onehot((half == part) & (j == to))).reshape(5, 8, 32, 128)
        for n in range(4):
            for s in range(2):
                for k5 in range(5):
                    v = whole[k5, 2 * n + s]
                    if part:
                        v = pltpu.roll(v, 64, 1)
                    v = jnp.where(lane < 64, v, beyond[k5, 2 * n + s])
                    v = jnp.where(inside, v, 0.0)
                    z = 4 * n + 2 * part + s
                    a[k5, z] = v
                    if k5 == SINK:
                        s1[z] = v
    pre(a, d1, None, r1, 16)

    def keep1(k, z, value):
        m1[k, z] = value

    halve(a, s1, r1, t1, keep1, 16, 32)
    out = dot(m1[...].reshape(640, 128), sums(128, 64)).reshape(5, 8, 16, 128)
    b[0:4] = out[0:4]
    s2[...] = out[3]
    q2[...] = out[4]
    pre(b, d2, q2, r2, 8)

    def keep2(k, z, value):
        m2[z, k] = value[0:2]

    m2[...] = jnp.zeros((4, 8, 2, 128), F32)
    halve(b, s2, r2, t1.at[:, 0:16], keep2, 8, 16)
    i, j = iota((128, 128), 0), iota((128, 128), 1)
    total = jnp.zeros((8, 128), F32)
    for z in range(4):
        zg = lax.rem(z + gz, 4)
        for s in range(2):
            to = (zg * 2 + s) * 16 + i // 2
            total = total + dot(m2[z, :, s], onehot((i < 32) & (j == to)))
    sent[...] = jnp.broadcast_to(total[None], (64, 8, 128))


def finish_up(a, n):
    c3 = circ(n)

    def run(src, dst):
        def body(z):
            dst[z] = smoothed(a, lambda k: src[k], *c3(z))

        each(0, n, body)

    return run


def solve(
    pos, got, a0, a1, a2, pressure, left,
    a3, a4, a5, d3, d4, d5, r3, r4, s3, s4, t3, m3, m4, e1, e2, e3, e4, e5, w0,
):
    gx, gy, gz = pos[0], pos[1], pos[2]
    lane = iota((16, 128), 1)
    for k in range(5):
        rows = [got[pl.ds(g * 128 + k, 16, stride=8), :] for g in range(4)]
        for z in range(4):
            for s in range(2):
                at = (z * 2 + s) * 16
                value = jnp.zeros((16, 128), F32)
                for g in range(4):
                    shift = (16 * g - at) % 128
                    moved = pltpu.roll(rows[g], shift, 1) if shift else rows[g]
                    value = jnp.where(lane // 16 == g, moved, value)
                value = value + pltpu.roll(value, 64, 1)
                if k < 4:
                    a3[k, z, pl.ds(s, 16, stride=2), :] = value
                else:
                    r3[z, pl.ds(s, 16, stride=2), :] = value
    s3[...] = a3[SINK]
    pre(a3, d3, r3, e3, 4)

    def keep3(k, z, value):
        m3[k, z] = value

    halve(a3, s3, e3, t3, keep3, 4, 32)
    out = dot(m3[...].reshape(160, 128), sums(64, 32)).reshape(5, 2, 16, 128)
    a4[0:4] = out[0:4]
    s4[...] = out[3]
    r4[...] = out[4]
    pre(a4, d4, r4, e4, 2)

    def keep4(k, z, value):
        m4[k, z] = value

    halve(a4, s4, e4, t3.at[:, 0:16], keep4, 2, 16)
    out = dot(m4[...].reshape(40, 128), sums(32, 16)).reshape(5, 8, 128)
    ux, uy, uz, sink, r = out[0], out[1], out[2], out[3], out[4]
    diag = sink + uz + uz + ux + down(ux, 0) + uy + down(uy, 1)
    rd = W / diag
    c = rd * r
    v = c
    for _ in range(COARSE_SWEEPS - 1):
        beside = ux * up(v, 0) + down(ux * v, 0) + (uy * up(v, 1) + down(uy * v, 1))
        beside = beside + (uz * v + uz * v)
        v = v * (1.0 / 3.0) + c + rd * beside

    def double(rows):
        i, j = iota((rows, rows // 2), 0), iota((rows, rows // 2), 1)
        return onehot(j == i // 2)

    def lanes(width):
        i, j = iota((128, 128), 0), iota((128, 128), 1)
        return onehot((i < width // 2) & (i == (j % width) // 2))

    e = stretch(v, double(16), lanes(32))
    for z in range(2):
        a4[V, z] = a4[V, z] + e
    run = finish_up(a4, 2)
    run(a4.at[V], e4)
    run(e4, r4)
    q, p = double(32), lanes(64)
    for z in range(2):
        e = stretch(r4[z], q, p)
        a3[V, 2 * z] = a3[V, 2 * z] + e
        a3[V, 2 * z + 1] = a3[V, 2 * z + 1] + e
    run = finish_up(a3, 4)
    run(a3.at[V], e3)
    run(e3, r3)
    i, j = iota((128, 128), 0), iota((128, 128), 1)
    jj = j % 64
    at = jnp.where(jj < 40, jj // 2, jj // 2 - 32) + 16 * gy
    p = onehot((i < 64) & (i == lax.rem(at + 64, 64)))
    i, j = iota((16, 32), 0), iota((16, 32), 1)
    at = jnp.where(i < 10, i // 2, i // 2 - 8) + 2 * gx
    q = onehot(j == lax.rem(at + 32, 32))
    for z in range(4):
        e = stretch(r3[lax.rem(z + gz, 4)], q, p)
        e2[2 * z] = a2[V, 2 * z] + e
        e2[2 * z + 1] = a2[V, 2 * z + 1] + e
    run = finish_up(a2, 8)
    run(e2, e5)
    run(e5, e2)
    i, j = iota((128, 128), 0), iota((128, 128), 1)
    q, p = double(32), onehot((i < 64) & (i == j // 2))
    for z in range(8):
        e = stretch(e2[z], q, p)
        e1[0, 2 * z] = a1[V, 2 * z] + e
        e1[0, 2 * z + 1] = a1[V, 2 * z + 1] + e
    run = finish_up(a1, 16)
    run(e1.at[0], e1.at[1])
    run(e1.at[1], e1.at[0])
    i, j = iota((32, 32), 0), iota((32, 32), 1)
    q = onehot(j == jnp.where(i < 24, i // 2, i // 2 + 16))
    i, j = iota((128, 256), 0), iota((128, 256), 1)
    p = onehot(i == j // 2)
    for zc in range(-2, 6):
        e = stretch(e1[0, zc % 16], q, p)
        for z in (2 * zc, 2 * zc + 1):
            if -3 <= z <= 10:
                w0[0, z + H] = a0[V, z + H] + e

    def sweep0(src, dst):
        def body(z):
            w0[dst, z] = smoothed(a0, lambda k: w0[src, k], z, z - 1, z + 1)

        return body

    each(3, Z0 - 3, sweep0(0, 1))
    each(4, Z0 - 4, sweep0(1, 0))

    def last(z):
        v, beside = around(a0, lambda k: w0[0, k], z, z - 1, z + 1)
        r = W / a0[RD, z] * (1.5 * a0[C, z] - v) + beside
        pressure[z - H] = v[0:16, 0:128]
        left[z - H] = r[0:16, 0:128]

    each(H, H + 8, last)


def shift(value, axis, by):
    count = lax.axis_size(axis)
    return lax.ppermute(value, axis, [((i + by) % count, i) for i in range(count)])


def local(facies, boundary, hc, vc, source, density):
    pos = jnp.stack([lax.axis_index(n) for n in ("gx", "gy", "gz")]).astype(jnp.int32)
    raw = (facies, boundary, source, density)
    lo, hi = call(pack_z, [(4, H, 16, 128)] * 2, *raw)
    above, below = shift(lo, "gz", 1), shift(hi, "gz", -1)
    xl, xh = call(pack_x, [(4, Z0, 8, 128)] * 2, *raw, above, below)
    rl, rh = shift(xl, "gx", 1), shift(xh, "gx", -1)
    lo, hi = call(pack_y, [(8, ROWS0)] * 2, xl, xh, rl, rh)
    yl, yh = shift(lo, "gy", 1), shift(hi, "gy", -1)
    a0, packed = call(
        level0,
        [(6, Z0, 32, 256), (5, 2, 8, 128)],
        pos, hc, vc, xl, xh, rl, rh, yl, yh,
        smem=3,
        scratch=[
            (4, Z0, 32, 256), (Z0, 32, 256), (Z0, 32, 256), (Z0, 32, 256), (8, 16, 128),
            (Z0, 32, 256), (6, 16, 128), (2, 6, 2, 8, 128),
        ],
    )
    blocks = [shift(packed, "gz", n) for n in (1, 2, 3)]
    full, lo, hi = call(
        pack_x1, [(5, 8, 8, 128), (5, 4, 8, 128), (5, 4, 8, 128)], packed, *blocks
    )
    r1, l1 = shift(full, "gx", 1), shift(full, "gx", -1)
    r2, l2 = shift(lo, "gx", 2), shift(hi, "gx", -2)
    whole, lo, hi = call(
        pack_y1, [(5, 8, 32, 128), (32, 1280), (32, 1280)], full, r1, l1, r2, l2
    )
    yl, yh = shift(lo, "gy", 1), shift(hi, "gy", -1)
    a1, a2, sent = call(
        level12,
        [(6, 16, 32, 128), (6, 8, 16, 128), (64, 8, 128)],
        pos, whole, yl, yh,
        smem=1,
        scratch=[
            (16, 32, 128), (16, 32, 128), (5, 32, 128), (5, 8, 16, 128),
            (8, 16, 128), (8, 16, 128), (16, 32, 128), (8, 16, 128), (8, 16, 128), (4, 8, 2, 128),
        ],
    )
    got = lax.all_to_all(sent, ("gy", "gx"), 0, 0)
    return tuple(
        call(
            solve,
            [(8, 16, 128), (8, 16, 128)],
            pos, got.reshape(512, 128), a0, a1, a2,
            smem=1,
            scratch=[
                (6, 4, 32, 128), (6, 2, 16, 128), (6, 1, 8, 128),
                (4, 32, 128), (2, 16, 128), (1, 8, 128),
                (4, 32, 128), (2, 16, 128), (4, 32, 128), (2, 16, 128),
                (5, 32, 128), (5, 2, 16, 128), (5, 1, 8, 128),
                (2, 16, 32, 128), (8, 16, 128), (4, 32, 128), (2, 16, 128), (8, 16, 128),
                (2, Z0, 32, 256),
            ],
        )
    )


def solution(mesh):
    split = P("gz", "gx", "gy")
    return jax.shard_map(
        local,
        mesh=mesh,
        in_specs=(split, split, P(), P(), split, split),
        out_specs=(split, split),
        check_vma=False,
    )
```

```python
import jax
import jax.numpy as jnp
from jax import lax
from jax.experimental import pallas as pl
from jax.experimental.pallas import tpu as pltpu
from jax.sharding import PartitionSpec as P

COARSE_SWEEPS = 8
W = 2.0 / 3.0
F32 = jnp.float32
UX, UY, UZ, RD, C, V = range(6)
SINK = RD
H = 5
Z0 = 8 + 2 * H

VMEM = pl.BlockSpec(memory_space=pltpu.VMEM)
SMEM = pl.BlockSpec(memory_space=pltpu.SMEM)
ANY = pl.BlockSpec(memory_space=pl.ANY)


def call(kernel, outs, *args, scratch=(), spaces=None):
    return pl.pallas_call(
        kernel,
        out_shape=[jax.ShapeDtypeStruct(s, F32) for s in outs],
        in_specs=spaces or [VMEM] * len(args),
        out_specs=[VMEM] * len(outs),
        scratch_shapes=[pltpu.VMEM(s, F32) if isinstance(s, tuple) else s for s in scratch],
        compiler_params=pltpu.CompilerParams(vmem_limit_bytes=24 * 2**20),
    )(*args)


def iota(shape, dim):
    return lax.broadcasted_iota(jnp.int32, shape, dim)


def up(a, dim):
    return pltpu.roll(a, a.shape[dim] - 1, dim)


def down(a, dim):
    return pltpu.roll(a, 1, dim)


def turn(a, by):
    by %= 128
    return pltpu.roll(a, by, a.ndim - 1) if by else a


def pick(a, index):
    return jnp.take_along_axis(a, index, axis=1, mode="promise_in_bounds")


def fold_lanes(a):
    return pick(a + up(a, 1), (2 * iota(a.shape, 1)) % 128)


def spread_lanes(a, first=0):
    return pick(a, first + iota(a.shape, 1) // 2)


def each(start, stop, body, unroll=1):
    if unroll >= stop - start:
        for z in range(start, stop):
            body(z)
        return

    def step(z, carry):
        body(z)
        return carry

    lax.fori_loop(start, stop, step, 0, unroll=unroll)


def wrap(z, n):
    return z % n if isinstance(z, int) else lax.rem(z + n, n)


def around(a, field, z, zm, zp):
    v = field(z)
    ux, uy = a[UX, z], a[UY, z]
    out = ux * up(v, 0) + down(ux * v, 0)
    out = out + (uy * up(v, 1) + down(uy * v, 1))
    return v, out + (a[UZ, z] * field(zp) + a[UZ, zm] * field(zm))


def smoothed(a, field, z, zm, zp):
    v, beside = around(a, field, z, zm, zp)
    return v * (1.0 / 3.0) + a[C, z] + a[RD, z] * beside


def finish(a, d, r, z, zm):
    ux, uy = a[UX, z], a[UY, z]
    diag = a[SINK, z] + a[UZ, z] + a[UZ, zm] + ux + down(ux, 0) + uy + down(uy, 1)
    d[z] = diag
    rd = jnp.where(diag > 0.0, W / jnp.where(diag > 0.0, diag, 1.0), 0.0)
    a[RD, z] = rd
    if r is not None:
        a[C, z] = rd * r[z]


def circ(n):
    return lambda z: (z, wrap(z - 1, n), wrap(z + 1, n))


def pre(a, d, r, res, n, unroll):
    c3 = circ(n)
    each(0, n, lambda z: finish(a, d, r, z, wrap(z - 1, n)), unroll)

    def one(z):
        a[V, z] = smoothed(a, lambda k: a[C, k], *c3(z))

    each(0, n, one, unroll)

    def two(z):
        v, beside = around(a, lambda k: a[V, k], *c3(z))
        res[z] = d[z] * (1.5 * a[C, z] - v) + beside

    each(0, n, two, unroll)


def halve(a, sink, r, t, store, n, rows):
    odd_row = iota((rows, 128), 0) % 2 == 1
    odd_lane = iota((rows, 128), 1) % 2 == 1

    def body(z):
        lo, hi = 2 * z, 2 * z + 1
        parts = (
            jnp.where(odd_row, a[UX, lo] + a[UX, hi], 0.0),
            jnp.where(odd_lane, a[UY, lo] + a[UY, hi], 0.0),
            a[UZ, hi],
            sink[lo] + sink[hi],
            r[lo] + r[hi],
        )
        for k, part in enumerate(parts):
            t[k, z] = part
        for k in range(5):
            store(k, z, fold_rows(t.at[k, z], rows // 2))

    each(0, n // 2, body, n)


def fold_rows(t, n):
    return t[pl.ds(0, n, stride=2), :] + t[pl.ds(1, n, stride=2), :]


def spread_rows(t, value):
    n = value.shape[0]
    t[pl.ds(0, n, stride=2), :] = value
    t[pl.ds(1, n, stride=2), :] = value
    return t[...]


def pack_z(f, b, s, d, lo, hi, own, fi, bi, sems):
    copies = [
        pltpu.make_async_copy(f, fi, sems.at[0]),
        pltpu.make_async_copy(b, bi, sems.at[1]),
        pltpu.make_async_copy(s, own.at[2], sems.at[2]),
        pltpu.make_async_copy(d, own.at[3], sems.at[3]),
    ]
    for copy in copies:
        copy.start()
    for k, copy in enumerate(copies):
        copy.wait()
        if k < 2:
            own[k] = (fi, bi)[k][...].astype(F32)
        lo[k] = own[k, 0:H]
        hi[k] = own[k, 8 - H : 8]


def pack_x(own, above, below, lo, hi):
    for out, row in ((lo, 0), (hi, 8)):
        out[:, 0:H] = below[:, :, row : row + 8]
        out[:, H : H + 8] = own[:, :, row : row + 8]
        out[:, H + 8 : Z0] = above[:, :, row : row + 8]


GROUPS0 = 4 * Z0 // 4


def pack_y(xl, xh, rl, rh, lo, hi):
    block = iota((8, 128), 1) // 8
    for g in range(GROUPS0):
        left = right = None
        for n in range(4):
            k, z = divmod(4 * g + n, Z0)
            for tile, ref in enumerate((xl, xh, rl, rh)):
                at = 4 * n + tile
                v = ref[k, z]
                a, b = turn(v, 8 * at), turn(v, 8 * at + 8)
                left = a if at == 0 else jnp.where(block == at, a, left)
                right = b if at == 0 else jnp.where(block == at, b, right)
        lo[g] = left
        hi[g] = right


def level0(pos, tables, xl, xh, rl, rh, yl, yh, a, packed, raw, hs, vs, dd, res, sk, t, m):
    gx, gy, gz = pos[0], pos[1], pos[2]
    lane8 = iota((8, 128), 1)
    for g in range(GROUPS0):
        right, left = yl[g], yh[g]
        for n in range(4):
            k, z = divmod(4 * g + n, Z0)
            for tile in range(4):
                at = 8 * (4 * n + tile)
                raw[k, z, 8 * tile : 8 * tile + 8, 128:256] = jnp.where(
                    lane8 < 8,
                    turn(right, -at),
                    jnp.where(lane8 >= 120, turn(left, 120 - at), 0.0),
                )
    for row, ref in ((0, xl), (8, xh), (16, rl), (24, rh)):
        raw[:, :, row : row + 8, 0:128] = ref[...]

    row, lane = iota((32, 256), 0), iota((32, 256), 1)
    x = gx * 16 + jnp.where(row < 24, row, row - 32)
    y = gy * 128 + jnp.where(lane < 192, lane, lane - 256)
    inside = (x >= 0) & (x < 256) & (y >= 0) & (y < 512)

    def materials(z):
        zg = gz * 8 + z - H
        here = inside & ((zg >= 0) & (zg < 32))
        kind = raw[0, z]
        h = jnp.full((32, 256), tables[0], F32)
        v = jnp.full((32, 256), tables[8], F32)
        for n in range(1, 8):
            is_n = kind == float(n)
            h = jnp.where(is_n, tables[n], h)
            v = jnp.where(is_n, tables[8 + n], v)
        hs[z] = jnp.where(here, h, 0.0)
        vs[z] = jnp.where(here, v, 0.0)

    each(0, Z0, materials, 2)

    def harmonic(c, n):
        s = c + n
        return 2.0 * c * n / jnp.where(s > 0.0, s, 1.0)

    def couple(z):
        h = hs[z]
        a[UX, z] = harmonic(h, up(h, 0))
        a[UY, z] = harmonic(h, up(h, 1))
        a[UZ, z] = harmonic(vs[z], vs[z + 1])

    each(0, Z0 - 1, couple, 2)

    odd_row, odd_lane = row % 2 == 1, lane % 2 == 1

    def setup(z):
        h, v = hs[z], vs[z]
        sink = jnp.where(raw[1, z] == 1.0, 2.0 * v, jnp.where(raw[1, z] == 2.0, 0.5 * h, 0.0))
        ux, uy, uz, lz = a[UX, z], a[UY, z], a[UZ, z], a[UZ, z - 1]
        lx, ly = down(ux, 0), down(uy, 1)
        diag = sink + lz + uz + lx + ux + ly + uy
        dens = raw[3, z]
        b = raw[2, z] + 0.5 * uz * (dens + raw[3, z + 1]) - 0.5 * lz * (raw[3, z - 1] + dens)
        rd = jnp.where(diag > 0.0, W / jnp.where(diag > 0.0, diag, 1.0), 0.0)
        a[RD, z] = rd
        a[C, z] = rd * b
        dd[z] = diag
        sk[z] = sink
        outer = sink + jnp.where(odd_row, ux, lx) + jnp.where(odd_lane, uy, ly)
        hs[z] = outer + jnp.where((z - H) % 2 == 1, uz, lz)

    each(1, Z0 - 1, setup, 2)

    def first(z):
        a[V, z] = smoothed(a, lambda k: a[C, k], z, z - 1, z + 1)

    each(2, Z0 - 2, first, 2)

    def residual(z):
        v, beside = around(a, lambda k: a[V, k], z, z - 1, z + 1)
        res[z - H] = (dd[z] * (1.5 * a[C, z] - v) + beside)[0:16, 0:128]

    each(H, H + 8, residual, 2)

    o_row = iota((16, 128), 0) % 2 == 1
    o_lane = iota((16, 128), 1) % 2 == 1

    def coarsen(z):
        lo, hi = H + 2 * z, H + 2 * z + 1

        def both(ref):
            return ref[lo, 0:16, 0:128] + ref[hi, 0:16, 0:128]

        parts = (
            jnp.where(o_row, both(a.at[UX]), 0.0),
            jnp.where(o_lane, both(a.at[UY]), 0.0),
            a[UZ, hi, 0:16, 0:128],
            both(sk),
            res[2 * z] + res[2 * z + 1],
            both(hs),
        )
        for k, part in enumerate(parts):
            t[k, z] = part
        for k in range(6):
            m[k, z] = fold_rows(t.at[k, z], 8)

    each(0, 4, coarsen, 4)
    lower = lane8 < 64
    for s in range(2):
        parts = [jnp.where(lower, fold_lanes(m[k, s]), fold_lanes(m[k, 2 + s])) for k in range(6)]
        for k in range(4):
            packed[k, s] = parts[k]
        packed[4, s] = W * parts[4] / parts[5]


def pack_x1(own, b1, b2, b3, full, lo, hi):
    for n, ref in enumerate((own, b1, b2, b3)):
        full[:, 2 * n : 2 * n + 2] = ref[...]
        first, second = ref[:, 0], ref[:, 1]
        lo[:, n] = jnp.concatenate([first[:, 0:4], second[:, 0:4]], axis=1)
        hi[:, n] = jnp.concatenate([first[:, 4:8], second[:, 4:8]], axis=1)


def pack_y1(own, r1, l1, r2, l2, whole, lo, hi):
    whole[:, :, 0:8] = own[...]
    whole[:, :, 8:16] = r1[...]
    whole[:, :, 24:32] = l1[...]
    for n in range(4):
        for s in range(2):
            part = slice(4 * s, 4 * s + 4)
            whole[:, 2 * n + s, 16:24] = jnp.concatenate([r2[:, n, part], l2[:, n, part]], axis=1)
    block = (iota((8, 128), 1) // 16) % 4
    for k in range(5):
        for n in range(8):
            left = right = None
            for tile in range(4):
                v = whole[k, n, 8 * tile : 8 * tile + 8]
                a, b = turn(v, 16 * tile), turn(v, 16 * tile + 80)
                left = a if tile == 0 else jnp.where(block == tile, a, left)
                right = b if tile == 0 else jnp.where(block == tile, b, right)
            lo[k, n] = left
            hi[k, n] = right


def level12(pos, whole, yl, yh, a, b, sent, d1, r1, t1, m1, d2, r2, s1, s2, q2):
    gx, gy, gz = pos[0], pos[1], pos[2]
    row, lane = iota((8, 128), 0), iota((8, 128), 1)
    y = gy * 64 + jnp.where(lane < 96, lane, lane - 128)
    in_y = (y >= 0) & (y < 256)
    for tile in range(4):
        x = gx * 8 + jnp.where(8 * tile + row < 20, 8 * tile + row, 8 * tile + row - 32)
        inside = in_y & (x >= 0) & (x < 128)
        rows = slice(8 * tile, 8 * tile + 8)
        for k in range(5):
            for n in range(8):
                v, right, left = whole[k, n, rows], yl[k, n], yh[k, n]
                for part in range(2):
                    own = turn(v, 64 * part)
                    beyond = jnp.where(
                        lane < 80,
                        turn(right, 64 - 64 * part - 16 * tile),
                        jnp.where(lane >= 112, turn(left, 112 - 64 * part - 16 * tile), 0.0),
                    )
                    value = jnp.where(inside, jnp.where(lane < 64, own, beyond), 0.0)
                    z = 4 * (n // 2) + 2 * part + n % 2
                    a[k, z, rows] = value
                    if k == SINK:
                        s1[z, rows] = value
    pre(a, d1, None, r1, 16, 4)

    def keep1(k, z, value):
        value = fold_lanes(value)
        if k < 4:
            b[k, z] = value
        if k == SINK:
            s2[z] = value
        if k == 4:
            q2[z] = value

    halve(a, s1, r1, t1, keep1, 16, 32)
    pre(b, d2, q2, r2, 8, 8)

    def keep2(k, z, value):
        m1[z, 0, k : k + 1] = value[0:1]
        m1[z, 1, k : k + 1] = value[1:2]

    m1[...] = jnp.zeros((4, 2, 8, 128), F32)
    halve(b, s2, r2, t1.at[:, :, 0:16], keep2, 8, 16)
    total = jnp.zeros((8, 128), F32)
    for z in range(4):
        zg = lax.rem(z + gz, 4)
        for s in range(2):
            v = m1[z, s]
            v = pick(v + up(v, 1), 2 * (lane % 16))
            total = jnp.where(lane // 16 == 2 * zg + s, v, total)
    sent[...] = jnp.broadcast_to(total[None], (64, 8, 128))


def sweep(a, src, dst, n, unroll):
    c3 = circ(n)

    def body(z):
        dst[z] = smoothed(a, lambda k: src[k], *c3(z))

    each(0, n, body, unroll)


def solve(
    pos, got, a0, a1, a2, pressure, left,
    a3, a4, d3, d4, r3, r4, s3, s4, t3, q5, e1, e2, e3, e4, f2, g4, g3, g2, g1, g0, b3, w0,
):
    gx, gy, gz = pos[0], pos[1], pos[2]
    lane = iota((16, 128), 1)
    for k in range(5):
        rows = [got[pl.ds(g * 128 + k, 16, stride=8), :] for g in range(4)]
        for z in range(4):
            for s in range(2):
                at = (z * 2 + s) * 16
                value = turn(rows[0], -at)
                for g in range(1, 4):
                    value = jnp.where(lane // 16 == g, turn(rows[g], 16 * g - at), value)
                value = jnp.where(lane < 64, value, turn(value, 64))
                if k < 4:
                    a3[k, z, pl.ds(s, 16, stride=2), :] = value
                else:
                    r3[z, pl.ds(s, 16, stride=2), :] = value
    s3[...] = a3[SINK]
    pre(a3, d3, r3, e3, 4, 4)

    def keep3(k, z, value):
        value = fold_lanes(value)
        if k < 4:
            a4[k, z] = value
        if k == SINK:
            s4[z] = value
        if k == 4:
            r4[z] = value

    halve(a3, s3, e3, t3, keep3, 4, 32)
    pre(a4, d4, r4, e4, 2, 2)

    def keep4(k, z, value):
        q5[k] = fold_lanes(value)

    halve(a4, s4, e4, t3.at[:, :, 0:16], keep4, 2, 16)
    ux, uy, uz, sink, r = q5[0], q5[1], q5[2], q5[3], q5[4]
    lx, ly = down(ux, 0), down(uy, 1)
    diag = sink + uz + uz + ux + lx + uy + ly
    rd = W / diag
    c = rd * r
    ux, lx, uy, ly = rd * ux, rd * lx, rd * uy, rd * ly
    v = c
    for _ in range(COARSE_SWEEPS - 1):
        beside = (ux * up(v, 0) + lx * down(v, 0)) + (uy * up(v, 1) + ly * down(v, 1))
        v = (v * (1.0 / 3.0) + c) + beside

    e = spread_rows(g4, spread_lanes(v))
    for z in range(2):
        a4[V, z] = a4[V, z] + e
    sweep(a4, a4.at[V], e4, 2, 2)
    sweep(a4, e4, r4, 2, 2)
    for z in range(2):
        e = spread_rows(g3.at[z], spread_lanes(r4[z]))
        a3[V, 2 * z] = a3[V, 2 * z] + e
        a3[V, 2 * z + 1] = a3[V, 2 * z + 1] + e
    sweep(a3, a3.at[V], e3, 4, 4)
    sweep(a3, e3, r3, 4, 4)
    b3[:, 8:40] = r3[...]
    b3[:, 0:8] = r3[:, 24:32]
    b3[:, 40:48] = r3[:, 0:8]
    lane = iota((8, 128), 1) % 64
    index = jnp.where(lane < 40, lane // 2, lane // 2 - 32) + 16 * gy
    index = lax.rem(index + 64, 64)
    for z in range(4):
        e = b3[lax.rem(z + gz, 4), pl.ds(2 * gx + 5, 8), :]
        e = pick(pltpu.roll(e, 5, 0), index)
        e = spread_rows(g2.at[z], e)
        e2[2 * z] = a2[V, 2 * z] + e
        e2[2 * z + 1] = a2[V, 2 * z + 1] + e
    sweep(a2, e2, f2, 8, 8)
    sweep(a2, f2, e2, 8, 8)
    for z in range(8):
        e = spread_rows(g1.at[z], spread_lanes(e2[z]))
        e1[0, 2 * z] = a1[V, 2 * z] + e
        e1[0, 2 * z + 1] = a1[V, 2 * z + 1] + e
    sweep(a1, e1.at[0], e1.at[1], 16, 4)
    sweep(a1, e1.at[1], e1.at[0], 16, 4)
    upper = iota((8, 128), 0) < 4
    for zc in range(-2, 6):
        v = e1[0, zc % 16]
        v = jnp.concatenate([v[0:8], jnp.where(upper, v[8:16], v[24:32])], axis=0)
        for half in range(2):
            e = spread_rows(g0.at[half, zc + 2], spread_lanes(v, 64 * half))
            lanes = slice(128 * half, 128 * half + 128)
            for z in (2 * zc, 2 * zc + 1):
                if -3 <= z <= 10:
                    w0[0, z + H, :, lanes] = a0[V, z + H, :, lanes] + e

    def sweep0(src, dst):
        def body(z):
            w0[dst, z] = smoothed(a0, lambda k: w0[src, k], z, z - 1, z + 1)

        return body

    each(3, Z0 - 3, sweep0(0, 1), 2)
    each(4, Z0 - 4, sweep0(1, 0), 2)

    def last(z):
        v, beside = around(a0, lambda k: w0[0, k], z, z - 1, z + 1)
        r = W / a0[RD, z] * (1.5 * a0[C, z] - v) + beside
        pressure[z - H] = v[0:16, 0:128]
        left[z - H] = r[0:16, 0:128]

    each(H, H + 8, last, 2)


def shift(value, axis, by):
    count = lax.axis_size(axis)
    return lax.ppermute(value, axis, [((i + by) % count, i) for i in range(count)])


def local(facies, boundary, hc, vc, source, density):
    pos = jnp.stack([lax.axis_index(n) for n in ("gx", "gy", "gz")]).astype(jnp.int32)
    tables = jnp.concatenate([hc, vc])
    lo, hi, own = call(
        pack_z,
        [(4, H, 16, 128)] * 2 + [(4, 8, 16, 128)],
        facies, boundary, source, density,
        spaces=[ANY] * 4,
        scratch=[
            pltpu.VMEM((8, 16, 128), jnp.int32), pltpu.VMEM((8, 16, 128), jnp.int32),
            pltpu.SemaphoreType.DMA((4,)),
        ],
    )
    above, below = shift(lo, "gz", 1), shift(hi, "gz", -1)
    xl, xh = call(pack_x, [(4, Z0, 8, 128)] * 2, own, above, below)
    rl, rh = shift(xl, "gx", 1), shift(xh, "gx", -1)
    lo, hi = call(pack_y, [(GROUPS0, 8, 128)] * 2, xl, xh, rl, rh)
    yl, yh = shift(lo, "gy", 1), shift(hi, "gy", -1)
    a0, packed = call(
        level0,
        [(6, Z0, 32, 256), (5, 2, 8, 128)],
        pos, tables, xl, xh, rl, rh, yl, yh,
        spaces=[SMEM] * 2 + [VMEM] * 6,
        scratch=[
            (4, Z0, 32, 256), (Z0, 32, 256), (Z0, 32, 256), (Z0, 32, 256), (8, 16, 128),
            (Z0, 32, 256), (6, 4, 16, 128), (6, 4, 8, 128),
        ],
    )
    blocks = [shift(packed, "gz", n) for n in (1, 2, 3)]
    full, lo, hi = call(
        pack_x1, [(5, 8, 8, 128), (5, 4, 8, 128), (5, 4, 8, 128)], packed, *blocks
    )
    r1, l1 = shift(full, "gx", 1), shift(full, "gx", -1)
    r2, l2 = shift(lo, "gx", 2), shift(hi, "gx", -2)
    whole, lo, hi = call(
        pack_y1, [(5, 8, 32, 128), (5, 8, 8, 128), (5, 8, 8, 128)], full, r1, l1, r2, l2
    )
    yl, yh = shift(lo, "gy", 1), shift(hi, "gy", -1)
    a1, a2, sent = call(
        level12,
        [(6, 16, 32, 128), (6, 8, 16, 128), (64, 8, 128)],
        pos, whole, yl, yh,
        spaces=[SMEM] + [VMEM] * 3,
        scratch=[
            (16, 32, 128), (16, 32, 128), (5, 8, 32, 128), (4, 2, 8, 128),
            (8, 16, 128), (8, 16, 128), (16, 32, 128), (8, 16, 128), (8, 16, 128),
        ],
    )
    got = lax.all_to_all(sent, ("gy", "gx"), 0, 0)
    return tuple(
        call(
            solve,
            [(8, 16, 128), (8, 16, 128)],
            pos, got.reshape(512, 128), a0, a1, a2,
            spaces=[SMEM] + [VMEM] * 4,
            scratch=[
                (6, 4, 32, 128), (6, 2, 16, 128),
                (4, 32, 128), (2, 16, 128),
                (4, 32, 128), (2, 16, 128), (4, 32, 128), (2, 16, 128),
                (5, 2, 32, 128), (5, 8, 128),
                (2, 16, 32, 128), (8, 16, 128), (4, 32, 128), (2, 16, 128), (8, 16, 128),
                (16, 128), (2, 32, 128), (4, 16, 128), (8, 32, 128), (2, 8, 32, 128),
                (4, 48, 128), (2, Z0, 32, 256),
            ],
        )
    )


def solution(mesh):
    split = P("gz", "gx", "gy")
    return jax.shard_map(
        local,
        mesh=mesh,
        in_specs=(split, split, P(), P(), split, split),
        out_specs=(split, split),
        check_vma=False,
    )
```

```python
import jax
import jax.numpy as jnp
from jax import lax
from jax.experimental import pallas as pl
from jax.experimental.pallas import tpu as pltpu
from jax.sharding import PartitionSpec as P

COARSE_SWEEPS = 8
W = 2.0 / 3.0
F32 = jnp.float32
UX, UY, UZ, RD, C, V = range(6)
SINK = RD
H = 5
Z0 = 8 + 2 * H

VMEM = pl.BlockSpec(memory_space=pltpu.VMEM)
SMEM = pl.BlockSpec(memory_space=pltpu.SMEM)
HBM = pl.BlockSpec(memory_space=pltpu.HBM)


def call(kernel, outs, *args, scratch=(), spaces=None):
    return pl.pallas_call(
        kernel,
        out_shape=[jax.ShapeDtypeStruct(s, F32) for s in outs],
        in_specs=spaces or [VMEM] * len(args),
        out_specs=[VMEM] * len(outs),
        scratch_shapes=[pltpu.VMEM(s, F32) if isinstance(s, tuple) else s for s in scratch],
        compiler_params=pltpu.CompilerParams(vmem_limit_bytes=24 * 2**20),
    )(*args)


def iota(shape, dim):
    return lax.broadcasted_iota(jnp.int32, shape, dim)


def up(a, dim):
    return pltpu.roll(a, a.shape[dim] - 1, dim)


def down(a, dim):
    return pltpu.roll(a, 1, dim)


def turn(a, by):
    by %= 128
    return pltpu.roll(a, by, a.ndim - 1) if by else a


def pick(a, index):
    return jnp.take_along_axis(a, index, axis=1, mode="promise_in_bounds")


def fold_lanes(a):
    return pick(a + up(a, 1), (2 * iota(a.shape, 1)) % 128)


def spread_lanes(a, first=0):
    return pick(a, first + iota(a.shape, 1) // 2)


def each(start, stop, body, unroll=1):
    if unroll >= stop - start:
        for z in range(start, stop):
            body(z)
        return

    def step(z, carry):
        body(z)
        return carry

    lax.fori_loop(start, stop, step, 0, unroll=unroll)


def wrap(z, n):
    return z % n if isinstance(z, int) else lax.rem(z + n, n)


def around(a, field, z, zm, zp):
    v = field(z)
    ux, uy = a[UX, z], a[UY, z]
    out = ux * up(v, 0) + down(ux * v, 0)
    out = out + (uy * up(v, 1) + down(uy * v, 1))
    return v, out + (a[UZ, z] * field(zp) + a[UZ, zm] * field(zm))


def smoothed(a, field, z, zm, zp):
    v, beside = around(a, field, z, zm, zp)
    return v * (1.0 / 3.0) + a[C, z] + a[RD, z] * beside


def finish(a, d, r, z, zm):
    ux, uy = a[UX, z], a[UY, z]
    diag = a[SINK, z] + a[UZ, z] + a[UZ, zm] + ux + down(ux, 0) + uy + down(uy, 1)
    d[z] = diag
    rd = jnp.where(diag > 0.0, W / jnp.where(diag > 0.0, diag, 1.0), 0.0)
    a[RD, z] = rd
    if r is not None:
        a[C, z] = rd * r[z]


def circ(n):
    return lambda z: (z, wrap(z - 1, n), wrap(z + 1, n))


def pre(a, d, r, res, n, unroll):
    c3 = circ(n)
    each(0, n, lambda z: finish(a, d, r, z, wrap(z - 1, n)), unroll)

    def one(z):
        a[V, z] = smoothed(a, lambda k: a[C, k], *c3(z))

    each(0, n, one, unroll)

    def two(z):
        v, beside = around(a, lambda k: a[V, k], *c3(z))
        res[z] = d[z] * (1.5 * a[C, z] - v) + beside

    each(0, n, two, unroll)


def halve(a, sink, r, t, store, n, rows):
    odd_row = iota((rows, 128), 0) % 2 == 1
    odd_lane = iota((rows, 128), 1) % 2 == 1

    def body(z):
        lo, hi = 2 * z, 2 * z + 1
        parts = (
            jnp.where(odd_row, a[UX, lo] + a[UX, hi], 0.0),
            jnp.where(odd_lane, a[UY, lo] + a[UY, hi], 0.0),
            a[UZ, hi],
            sink[lo] + sink[hi],
            r[lo] + r[hi],
        )
        for k, part in enumerate(parts):
            t[k, z] = part
        for k in range(5):
            store(k, z, fold_rows(t.at[k, z], rows // 2))

    each(0, n // 2, body, n)


def fold_rows(t, n):
    return t[pl.ds(0, n, stride=2), :] + t[pl.ds(1, n, stride=2), :]


def spread_rows(t, value):
    n = value.shape[0]
    t[pl.ds(0, n, stride=2), :] = value
    t[pl.ds(1, n, stride=2), :] = value
    return t[...]


def pack_z(f, b, s, d, lo, hi, own, fi, bi, sems):
    copies = [
        pltpu.make_async_copy(f, fi, sems.at[0]),
        pltpu.make_async_copy(b, bi, sems.at[1]),
        pltpu.make_async_copy(s, own.at[2], sems.at[2]),
        pltpu.make_async_copy(d, own.at[3], sems.at[3]),
    ]
    for copy in copies:
        copy.start()
    for k, copy in enumerate(copies):
        copy.wait()
        if k < 2:
            own[k] = (fi, bi)[k][...].astype(F32)
        lo[k] = own[k, 0:H]
        hi[k] = own[k, 8 - H : 8]


FACIES, BOUNDARY, SOURCE, DENSITY = range(4)
XTILES = 2 * Z0 + 3


def pack_x(own, above, below, xl, xh, lo, hi):
    for out, row in ((xl, 0), (xh, 8)):
        out[:, 0:H] = below[:, :, row : row + 8]
        out[:, H : H + 8] = own[:, :, row : row + 8]
        out[:, H + 8 : Z0] = above[:, :, row : row + 8]
    first = iota((8, 128), 0) < 4
    lo[XTILES - 1] = hi[XTILES - 1] = jnp.zeros((8, 128), F32)
    for z in range(Z0):
        fifth = 2 * Z0 + z // 8, slice(z % 8, z % 8 + 1)
        f, b, s, d = (xl[k, z] for k in range(4))
        lo[2 * z] = jnp.where(first, b, pltpu.roll(s, 4, 0))
        lo[2 * z + 1] = jnp.where(first, d, pltpu.roll(f, 4, 0))
        lo[fifth] = f[4:5]
        f, b, s, d = (xh[k, z] for k in range(4))
        hi[2 * z] = jnp.where(first, pltpu.roll(b, 4, 0), s)
        hi[2 * z + 1] = jnp.where(first, pltpu.roll(d, 4, 0), f)
        hi[fifth] = f[3:4]


SMALL = 7
YTILES = SMALL + 5


def block_of(k, z, tile):
    if k == FACIES:
        return SMALL + z // 4, 8 * (4 * (z % 4) + tile), 8
    layer = (k - 1) * Z0 + z
    return layer // 8, 4 * (4 * (layer % 8) + tile), 4


def pack_y(xl, xh, ml, mh, rl, rh, lo, hi):
    row, lane = iota((8, 128), 0), iota((8, 128), 1)
    for z in range(Z0):
        fifth = 2 * Z0 + z // 8, slice(z % 8, z % 8 + 1)
        bs, df = ml[2 * z], ml[2 * z + 1]
        rl[BOUNDARY, z] = bs
        rl[SOURCE, z] = pltpu.roll(bs, 4, 0)
        rl[DENSITY, z] = df
        rl[FACIES, z] = jnp.where(row == 4, ml[fifth], pltpu.roll(df, 4, 0))
        bs, df = mh[2 * z], mh[2 * z + 1]
        rh[BOUNDARY, z] = pltpu.roll(bs, 4, 0)
        rh[SOURCE, z] = bs
        rh[DENSITY, z] = pltpu.roll(df, 4, 0)
        rh[FACIES, z] = jnp.where(row == 3, mh[fifth], df)
    left, right = [None] * YTILES, [None] * YTILES
    for k in range(4):
        for z in range(Z0):
            for tile, ref in enumerate((xl, xh, rl, rh)):
                g, at, width = block_of(k, z, tile)
                v = ref[k, z]
                here = lane // width == at // width
                a, b = turn(v, at), turn(v, at + width)
                left[g] = a if at == 0 else jnp.where(here, a, left[g])
                right[g] = b if at == 0 else jnp.where(here, b, right[g])
    for g in range(YTILES):
        lo[g] = left[g]
        hi[g] = right[g]


def level0(pos, tables, xl, xh, rl, rh, yl, yh, a, packed, raw, hs, vs, dd, res, sk, t, m):
    gx, gy, gz = pos[0], pos[1], pos[2]
    lane8 = iota((8, 128), 1)
    for k in range(4):
        for z in range(Z0):
            for tile in range(4):
                g, at, width = block_of(k, z, tile)
                raw[k, z, 8 * tile : 8 * tile + 8, 128:256] = jnp.where(
                    lane8 < width,
                    turn(yl[g], -at),
                    jnp.where(lane8 >= 128 - width, turn(yh[g], -at - width), 0.0),
                )
    for row, ref in ((0, xl), (8, xh), (16, rl), (24, rh)):
        raw[:, :, row : row + 8, 0:128] = ref[...]

    row, lane = iota((32, 256), 0), iota((32, 256), 1)
    x = gx * 16 + jnp.where(row < 24, row, row - 32)
    y = gy * 128 + jnp.where(lane < 192, lane, lane - 256)
    inside = (x >= 0) & (x < 256) & (y >= 0) & (y < 512)

    def materials(z):
        zg = gz * 8 + z - H
        here = inside & ((zg >= 0) & (zg < 32))
        kind = raw[0, z]
        h = jnp.full((32, 256), tables[0], F32)
        v = jnp.full((32, 256), tables[8], F32)
        for n in range(1, 8):
            is_n = kind == float(n)
            h = jnp.where(is_n, tables[n], h)
            v = jnp.where(is_n, tables[8 + n], v)
        hs[z] = jnp.where(here, h, 0.0)
        vs[z] = jnp.where(here, v, 0.0)

    each(0, Z0, materials, 2)

    def harmonic(c, n):
        s = c + n
        return 2.0 * c * n / jnp.where(s > 0.0, s, 1.0)

    def couple(z):
        h = hs[z]
        a[UX, z] = harmonic(h, up(h, 0))
        a[UY, z] = harmonic(h, up(h, 1))
        a[UZ, z] = harmonic(vs[z], vs[z + 1])

    each(0, Z0 - 1, couple, 2)

    odd_row, odd_lane = row % 2 == 1, lane % 2 == 1

    def setup(z):
        h, v = hs[z], vs[z]
        sink = jnp.where(raw[1, z] == 1.0, 2.0 * v, jnp.where(raw[1, z] == 2.0, 0.5 * h, 0.0))
        ux, uy, uz, lz = a[UX, z], a[UY, z], a[UZ, z], a[UZ, z - 1]
        lx, ly = down(ux, 0), down(uy, 1)
        diag = sink + lz + uz + lx + ux + ly + uy
        dens = raw[3, z]
        b = raw[2, z] + 0.5 * uz * (dens + raw[3, z + 1]) - 0.5 * lz * (raw[3, z - 1] + dens)
        rd = jnp.where(diag > 0.0, W / jnp.where(diag > 0.0, diag, 1.0), 0.0)
        a[RD, z] = rd
        a[C, z] = rd * b
        dd[z] = diag
        sk[z] = sink
        outer = sink + jnp.where(odd_row, ux, lx) + jnp.where(odd_lane, uy, ly)
        hs[z] = outer + jnp.where((z - H) % 2 == 1, uz, lz)

    each(1, Z0 - 1, setup, 2)

    def first(z):
        a[V, z] = smoothed(a, lambda k: a[C, k], z, z - 1, z + 1)

    each(2, Z0 - 2, first, 2)

    def residual(z):
        v, beside = around(a, lambda k: a[V, k], z, z - 1, z + 1)
        res[z - H] = (dd[z] * (1.5 * a[C, z] - v) + beside)[0:16, 0:128]

    each(H, H + 8, residual, 2)

    o_row = iota((16, 128), 0) % 2 == 1
    o_lane = iota((16, 128), 1) % 2 == 1

    def coarsen(z):
        lo, hi = H + 2 * z, H + 2 * z + 1

        def both(ref):
            return ref[lo, 0:16, 0:128] + ref[hi, 0:16, 0:128]

        parts = (
            jnp.where(o_row, both(a.at[UX]), 0.0),
            jnp.where(o_lane, both(a.at[UY]), 0.0),
            a[UZ, hi, 0:16, 0:128],
            both(sk),
            res[2 * z] + res[2 * z + 1],
            both(hs),
        )
        for k, part in enumerate(parts):
            t[k, z] = part
        for k in range(6):
            m[k, z] = fold_rows(t.at[k, z], 8)

    each(0, 4, coarsen, 4)
    lower = lane8 < 64
    for s in range(2):
        parts = [jnp.where(lower, fold_lanes(m[k, s]), fold_lanes(m[k, 2 + s])) for k in range(6)]
        for k in range(4):
            packed[k, s] = parts[k]
        packed[4, s] = W * parts[4] / parts[5]


def pack_x1(own, b1, b2, b3, full, lo, hi):
    for n, ref in enumerate((own, b1, b2, b3)):
        full[:, 2 * n : 2 * n + 2] = ref[...]
        first, second = ref[:, 0], ref[:, 1]
        lo[:, n] = jnp.concatenate([first[:, 0:4], second[:, 0:4]], axis=1)
        hi[:, n] = jnp.concatenate([first[:, 4:8], second[:, 4:8]], axis=1)


def pack_y1(own, r1, l1, r2, l2, whole, lo, hi):
    whole[:, :, 0:8] = own[...]
    whole[:, :, 8:16] = r1[...]
    whole[:, :, 24:32] = l1[...]
    for n in range(4):
        for s in range(2):
            part = slice(4 * s, 4 * s + 4)
            whole[:, 2 * n + s, 16:24] = jnp.concatenate([r2[:, n, part], l2[:, n, part]], axis=1)
    block = (iota((8, 128), 1) % 64) // 12
    for g in range(32):
        left = right = None
        for at in range(5):
            layer, tile = divmod(5 * g + at, 4)
            v = whole[layer // 8, layer % 8, 8 * tile : 8 * tile + 8]
            a, b = turn(v, 12 * at), turn(v, 12 * at - 52)
            left = a if at == 0 else jnp.where(block == at, a, left)
            right = b if at == 0 else jnp.where(block == at, b, right)
        lo[g] = left
        hi[g] = right


def level12(pos, whole, yl, yh, a, b, sent, d1, r1, t1, m1, d2, r2, s1, s2, q2):
    gx, gy, gz = pos[0], pos[1], pos[2]
    row, lane = iota((8, 128), 0), iota((8, 128), 1)
    y = gy * 64 + jnp.where(lane < 96, lane, lane - 128)
    in_y = (y >= 0) & (y < 256)
    for tile in range(4):
        x = gx * 8 + jnp.where(8 * tile + row < 20, 8 * tile + row, 8 * tile + row - 32)
        inside = in_y & (x >= 0) & (x < 128)
        rows = slice(8 * tile, 8 * tile + 8)
        for k in range(5):
            for n in range(8):
                g, at = divmod(4 * (8 * k + n) + tile, 5)
                v, right, left = whole[k, n, rows], yl[g], yh[g]
                for part in range(2):
                    own = turn(v, 64 * part)
                    beyond = jnp.where(
                        lane < 76,
                        turn(right, 64 - 64 * part - 12 * at),
                        jnp.where(lane >= 116, turn(left, 116 - 64 * part - 12 * at), 0.0),
                    )
                    value = jnp.where(inside, jnp.where(lane < 64, own, beyond), 0.0)
                    z = 4 * (n // 2) + 2 * part + n % 2
                    a[k, z, rows] = value
                    if k == SINK:
                        s1[z, rows] = value
    pre(a, d1, None, r1, 16, 4)

    def keep1(k, z, value):
        value = fold_lanes(value)
        if k < 4:
            b[k, z] = value
        if k == SINK:
            s2[z] = value
        if k == 4:
            q2[z] = value

    halve(a, s1, r1, t1, keep1, 16, 32)
    pre(b, d2, q2, r2, 8, 8)

    def keep2(k, z, value):
        m1[z, 0, k : k + 1] = value[0:1]
        m1[z, 1, k : k + 1] = value[1:2]

    m1[...] = jnp.zeros((4, 2, 8, 128), F32)
    halve(b, s2, r2, t1.at[:, :, 0:16], keep2, 8, 16)
    total = jnp.zeros((8, 128), F32)
    for z in range(4):
        zg = lax.rem(z + gz, 4)
        for s in range(2):
            v = m1[z, s]
            v = pick(v + up(v, 1), 2 * (lane % 16))
            total = jnp.where(lane // 16 == 2 * zg + s, v, total)
    for k in range(5):
        sent[:, :, 128 * k : 128 * k + 128] = jnp.broadcast_to(total[k : k + 1][None], (64, 1, 128))


def sweep(a, src, dst, n, unroll):
    c3 = circ(n)

    def body(z):
        dst[z] = smoothed(a, lambda k: src[k], *c3(z))

    each(0, n, body, unroll)


def solve(
    pos, got, a0, a1, a2, pressure, left,
    a3, a4, d3, d4, r3, r4, s3, s4, t3, q5, e1, e2, e3, e4, f2, g4, g3, g2, g1, g0, b3, w0,
):
    gx, gy, gz = pos[0], pos[1], pos[2]
    lane = iota((16, 128), 1)
    for k in range(5):
        rows = [got[16 * g : 16 * g + 16, 0, 128 * k : 128 * k + 128] for g in range(4)]
        for z in range(4):
            for s in range(2):
                at = (z * 2 + s) * 16
                value = turn(rows[0], -at)
                for g in range(1, 4):
                    value = jnp.where(lane // 16 == g, turn(rows[g], 16 * g - at), value)
                value = jnp.where(lane < 64, value, turn(value, 64))
                if k < 4:
                    a3[k, z, pl.ds(s, 16, stride=2), :] = value
                else:
                    r3[z, pl.ds(s, 16, stride=2), :] = value
    s3[...] = a3[SINK]
    pre(a3, d3, r3, e3, 4, 4)

    def keep3(k, z, value):
        value = fold_lanes(value)
        if k < 4:
            a4[k, z] = value
        if k == SINK:
            s4[z] = value
        if k == 4:
            r4[z] = value

    halve(a3, s3, e3, t3, keep3, 4, 32)
    pre(a4, d4, r4, e4, 2, 2)

    def keep4(k, z, value):
        q5[k] = fold_lanes(value)

    halve(a4, s4, e4, t3.at[:, :, 0:16], keep4, 2, 16)
    ux, uy, uz, sink, r = q5[0], q5[1], q5[2], q5[3], q5[4]
    lx, ly = down(ux, 0), down(uy, 1)
    diag = sink + uz + uz + ux + lx + uy + ly
    rd = W / diag
    c = rd * r
    ux, lx, uy, ly = rd * ux, rd * lx, rd * uy, rd * ly
    v = c
    for _ in range(COARSE_SWEEPS - 1):
        beside = (ux * up(v, 0) + lx * down(v, 0)) + (uy * up(v, 1) + ly * down(v, 1))
        v = (v * (1.0 / 3.0) + c) + beside

    e = spread_rows(g4, spread_lanes(v))
    for z in range(2):
        a4[V, z] = a4[V, z] + e
    sweep(a4, a4.at[V], e4, 2, 2)
    sweep(a4, e4, r4, 2, 2)
    for z in range(2):
        e = spread_rows(g3.at[z], spread_lanes(r4[z]))
        a3[V, 2 * z] = a3[V, 2 * z] + e
        a3[V, 2 * z + 1] = a3[V, 2 * z + 1] + e
    sweep(a3, a3.at[V], e3, 4, 4)
    sweep(a3, e3, r3, 4, 4)
    b3[:, 8:40] = r3[...]
    b3[:, 0:8] = r3[:, 24:32]
    b3[:, 40:48] = r3[:, 0:8]
    lane = iota((8, 128), 1) % 64
    index = jnp.where(lane < 40, lane // 2, lane // 2 - 32) + 16 * gy
    index = lax.rem(index + 64, 64)
    for z in range(4):
        e = b3[lax.rem(z + gz, 4), pl.ds(2 * gx + 5, 8), :]
        e = pick(pltpu.roll(e, 5, 0), index)
        e = spread_rows(g2.at[z], e)
        e2[2 * z] = a2[V, 2 * z] + e
        e2[2 * z + 1] = a2[V, 2 * z + 1] + e
    sweep(a2, e2, f2, 8, 8)
    sweep(a2, f2, e2, 8, 8)
    for z in range(8):
        e = spread_rows(g1.at[z], spread_lanes(e2[z]))
        e1[0, 2 * z] = a1[V, 2 * z] + e
        e1[0, 2 * z + 1] = a1[V, 2 * z + 1] + e
    sweep(a1, e1.at[0], e1.at[1], 16, 4)
    sweep(a1, e1.at[1], e1.at[0], 16, 4)
    upper = iota((8, 128), 0) < 4
    for zc in range(-2, 6):
        v = e1[0, zc % 16]
        v = jnp.concatenate([v[0:8], jnp.where(upper, v[8:16], v[24:32])], axis=0)
        for half in range(2):
            e = spread_rows(g0.at[half, zc + 2], spread_lanes(v, 64 * half))
            lanes = slice(128 * half, 128 * half + 128)
            for z in (2 * zc, 2 * zc + 1):
                if -3 <= z <= 10:
                    w0[0, z + H, :, lanes] = a0[V, z + H, :, lanes] + e

    def sweep0(src, dst):
        def body(z):
            w0[dst, z] = smoothed(a0, lambda k: w0[src, k], z, z - 1, z + 1)

        return body

    each(3, Z0 - 3, sweep0(0, 1), 2)
    each(4, Z0 - 4, sweep0(1, 0), 2)

    def last(z):
        v, beside = around(a0, lambda k: w0[0, k], z, z - 1, z + 1)
        r = W / a0[RD, z] * (1.5 * a0[C, z] - v) + beside
        pressure[z - H] = v[0:16, 0:128]
        left[z - H] = r[0:16, 0:128]

    each(H, H + 8, last, 2)


def shift(value, axis, by):
    count = lax.axis_size(axis)
    return lax.ppermute(value, axis, [((i + by) % count, i) for i in range(count)])


def local(facies, boundary, hc, vc, source, density):
    pos = jnp.stack([lax.axis_index(n) for n in ("gx", "gy", "gz")]).astype(jnp.int32)
    tables = jnp.concatenate([hc, vc])
    lo, hi, own = call(
        pack_z,
        [(4, H, 16, 128)] * 2 + [(4, 8, 16, 128)],
        facies, boundary, source, density,
        spaces=[HBM] * 4,
        scratch=[
            pltpu.VMEM((8, 16, 128), jnp.int32), pltpu.VMEM((8, 16, 128), jnp.int32),
            pltpu.SemaphoreType.DMA((4,)),
        ],
    )
    above, below = shift(lo, "gz", 1), shift(hi, "gz", -1)
    xl, xh, lo, hi = call(
        pack_x, [(4, Z0, 8, 128)] * 2 + [(XTILES, 8, 128)] * 2, own, above, below
    )
    ml, mh = shift(lo, "gx", 1), shift(hi, "gx", -1)
    rl, rh, lo, hi = call(
        pack_y, [(4, Z0, 8, 128)] * 2 + [(YTILES, 8, 128)] * 2, xl, xh, ml, mh
    )
    yl, yh = shift(lo, "gy", 1), shift(hi, "gy", -1)
    a0, packed = call(
        level0,
        [(6, Z0, 32, 256), (5, 2, 8, 128)],
        pos, tables, xl, xh, rl, rh, yl, yh,
        spaces=[SMEM] * 2 + [VMEM] * 6,
        scratch=[
            (4, Z0, 32, 256), (Z0, 32, 256), (Z0, 32, 256), (Z0, 32, 256), (8, 16, 128),
            (Z0, 32, 256), (6, 4, 16, 128), (6, 4, 8, 128),
        ],
    )
    blocks = [shift(packed, "gz", n) for n in (1, 2, 3)]
    full, lo, hi = call(
        pack_x1, [(5, 8, 8, 128), (5, 4, 8, 128), (5, 4, 8, 128)], packed, *blocks
    )
    r1, l1 = shift(full, "gx", 1), shift(full, "gx", -1)
    r2, l2 = shift(lo, "gx", 2), shift(hi, "gx", -2)
    whole, lo, hi = call(
        pack_y1, [(5, 8, 32, 128), (32, 8, 128), (32, 8, 128)], full, r1, l1, r2, l2
    )
    yl, yh = shift(lo, "gy", 1), shift(hi, "gy", -1)
    a1, a2, sent = call(
        level12,
        [(6, 16, 32, 128), (6, 8, 16, 128), (64, 1, 640)],
        pos, whole, yl, yh,
        spaces=[SMEM] + [VMEM] * 3,
        scratch=[
            (16, 32, 128), (16, 32, 128), (5, 8, 32, 128), (4, 2, 8, 128),
            (8, 16, 128), (8, 16, 128), (16, 32, 128), (8, 16, 128), (8, 16, 128),
        ],
    )
    got = lax.all_to_all(sent, ("gy", "gx"), 0, 0)
    return tuple(
        call(
            solve,
            [(8, 16, 128), (8, 16, 128)],
            pos, got, a0, a1, a2,
            spaces=[SMEM] + [VMEM] * 4,
            scratch=[
                (6, 4, 32, 128), (6, 2, 16, 128),
                (4, 32, 128), (2, 16, 128),
                (4, 32, 128), (2, 16, 128), (4, 32, 128), (2, 16, 128),
                (5, 2, 32, 128), (5, 8, 128),
                (2, 16, 32, 128), (8, 16, 128), (4, 32, 128), (2, 16, 128), (8, 16, 128),
                (16, 128), (2, 32, 128), (4, 16, 128), (8, 32, 128), (2, 8, 32, 128),
                (4, 48, 128), (2, Z0, 32, 256),
            ],
        )
    )


def solution(mesh):
    split = P("gz", "gx", "gy")
    return jax.shard_map(
        local,
        mesh=mesh,
        in_specs=(split, split, P(), P(), split, split),
        out_specs=(split, split),
        check_vma=False,
    )
```

```python
import jax
import jax.numpy as jnp
from jax import lax
from jax.experimental import pallas as pl
from jax.experimental.pallas import tpu as pltpu
from jax.sharding import PartitionSpec as P

COARSE_SWEEPS = 8
W = 2.0 / 3.0
F32 = jnp.float32
UX, UY, UZ, RD, C, V = range(6)
SINK = RD
H = 5
Z0 = 8 + 2 * H

VMEM = pl.BlockSpec(memory_space=pltpu.VMEM)
SMEM = pl.BlockSpec(memory_space=pltpu.SMEM)
HBM = pl.BlockSpec(memory_space=pltpu.HBM)


def call(kernel, outs, *args, scratch=(), spaces=None, limit=24):
    return pl.pallas_call(
        kernel,
        out_shape=[jax.ShapeDtypeStruct(s, F32) for s in outs],
        in_specs=spaces or [VMEM] * len(args),
        out_specs=[VMEM] * len(outs),
        scratch_shapes=[pltpu.VMEM(s, F32) if isinstance(s, tuple) else s for s in scratch],
        compiler_params=pltpu.CompilerParams(vmem_limit_bytes=limit * 2**20),
    )(*args)


def iota(shape, dim):
    return lax.broadcasted_iota(jnp.int32, shape, dim)


def up(a, dim):
    return pltpu.roll(a, a.shape[dim] - 1, dim)


def down(a, dim):
    return pltpu.roll(a, 1, dim)


def turn(a, by):
    by %= 128
    return pltpu.roll(a, by, a.ndim - 1) if by else a


def pick(a, index):
    return jnp.take_along_axis(a, index, axis=1, mode="promise_in_bounds")


def fold_lanes(a):
    return pick(a + up(a, 1), (2 * iota(a.shape, 1)) % 128)


def spread_lanes(a, first=0):
    return pick(a, first + iota(a.shape, 1) // 2)


def each(start, stop, body, unroll=1):
    if unroll >= stop - start:
        for z in range(start, stop):
            body(z)
        return

    def step(z, carry):
        body(z)
        return carry

    lax.fori_loop(start, stop, step, 0, unroll=unroll)


def wrap(z, n):
    return z % n if isinstance(z, int) else lax.rem(z + n, n)


def around(a, field, z, zm, zp):
    v = field(z)
    ux, uy = a[UX, z], a[UY, z]
    out = ux * up(v, 0) + down(ux * v, 0)
    out = out + (uy * up(v, 1) + down(uy * v, 1))
    return v, out + (a[UZ, z] * field(zp) + a[UZ, zm] * field(zm))


def smoothed(a, field, z, zm, zp):
    v, beside = around(a, field, z, zm, zp)
    return v * (1.0 / 3.0) + a[C, z] + a[RD, z] * beside


def finish(a, d, r, z, zm):
    ux, uy = a[UX, z], a[UY, z]
    diag = a[SINK, z] + a[UZ, z] + a[UZ, zm] + ux + down(ux, 0) + uy + down(uy, 1)
    d[z] = diag
    rd = jnp.where(diag > 0.0, W / jnp.where(diag > 0.0, diag, 1.0), 0.0)
    a[RD, z] = rd
    if r is not None:
        a[C, z] = rd * r[z]


def circ(n):
    return lambda z: (z, wrap(z - 1, n), wrap(z + 1, n))


def pre(a, d, r, res, n, unroll):
    c3 = circ(n)
    each(0, n, lambda z: finish(a, d, r, z, wrap(z - 1, n)), unroll)

    def one(z):
        a[V, z] = smoothed(a, lambda k: a[C, k], *c3(z))

    each(0, n, one, unroll)

    def two(z):
        v, beside = around(a, lambda k: a[V, k], *c3(z))
        res[z] = d[z] * (1.5 * a[C, z] - v) + beside

    each(0, n, two, unroll)


def halve(a, sink, r, t, store, n, rows):
    odd_row = iota((rows, 128), 0) % 2 == 1
    odd_lane = iota((rows, 128), 1) % 2 == 1

    def body(z):
        lo, hi = 2 * z, 2 * z + 1
        parts = (
            jnp.where(odd_row, a[UX, lo] + a[UX, hi], 0.0),
            jnp.where(odd_lane, a[UY, lo] + a[UY, hi], 0.0),
            a[UZ, hi],
            sink[lo] + sink[hi],
            r[lo] + r[hi],
        )
        for k, part in enumerate(parts):
            t[k, z] = part
        for k in range(5):
            store(k, z, fold_rows(t.at[k, z], rows // 2))

    each(0, n // 2, body, n)


def fold_rows(t, n):
    return t[pl.ds(0, n, stride=2), :] + t[pl.ds(1, n, stride=2), :]


def spread_rows(t, value):
    n = value.shape[0]
    t[pl.ds(0, n, stride=2), :] = value
    t[pl.ds(1, n, stride=2), :] = value
    return t[...]


def pack_z(f, b, s, d, lo, hi, own, fi, bi, sems):
    copies = [
        pltpu.make_async_copy(f, fi, sems.at[0]),
        pltpu.make_async_copy(b, bi, sems.at[1]),
        pltpu.make_async_copy(s, own.at[2], sems.at[2]),
        pltpu.make_async_copy(d, own.at[3], sems.at[3]),
    ]
    for copy in copies:
        copy.start()
    for k, copy in enumerate(copies):
        copy.wait()
        if k < 2:
            own[k] = (fi, bi)[k][...].astype(F32)
        lo[k] = own[k, 0:H]
        hi[k] = own[k, 8 - H : 8]


FACIES, BOUNDARY, SOURCE, DENSITY = range(4)
XTILES = 2 * Z0 + 3


def pack_x(own, above, below, xl, xh, lo, hi):
    for out, row in ((xl, 0), (xh, 8)):
        out[:, 0:H] = below[:, :, row : row + 8]
        out[:, H : H + 8] = own[:, :, row : row + 8]
        out[:, H + 8 : Z0] = above[:, :, row : row + 8]
    first = iota((8, 128), 0) < 4
    lo[XTILES - 1] = hi[XTILES - 1] = jnp.zeros((8, 128), F32)
    for z in range(Z0):
        fifth = 2 * Z0 + z // 8, slice(z % 8, z % 8 + 1)
        f, b, s, d = (xl[k, z] for k in range(4))
        lo[2 * z] = jnp.where(first, b, pltpu.roll(s, 4, 0))
        lo[2 * z + 1] = jnp.where(first, d, pltpu.roll(f, 4, 0))
        lo[fifth] = f[4:5]
        f, b, s, d = (xh[k, z] for k in range(4))
        hi[2 * z] = jnp.where(first, pltpu.roll(b, 4, 0), s)
        hi[2 * z + 1] = jnp.where(first, pltpu.roll(d, 4, 0), f)
        hi[fifth] = f[3:4]


SMALL = 7
YTILES = SMALL + 5


def block_of(k, z, tile):
    if k == FACIES:
        return SMALL + z // 4, 8 * (4 * (z % 4) + tile), 8
    layer = (k - 1) * Z0 + z
    return layer // 8, 4 * (4 * (layer % 8) + tile), 4


def pack_y(xl, xh, ml, mh, rl, rh, lo, hi):
    row, lane = iota((8, 128), 0), iota((8, 128), 1)
    for z in range(Z0):
        fifth = 2 * Z0 + z // 8, slice(z % 8, z % 8 + 1)
        bs, df = ml[2 * z], ml[2 * z + 1]
        rl[BOUNDARY, z] = bs
        rl[SOURCE, z] = pltpu.roll(bs, 4, 0)
        rl[DENSITY, z] = df
        rl[FACIES, z] = jnp.where(row == 4, ml[fifth], pltpu.roll(df, 4, 0))
        bs, df = mh[2 * z], mh[2 * z + 1]
        rh[BOUNDARY, z] = pltpu.roll(bs, 4, 0)
        rh[SOURCE, z] = bs
        rh[DENSITY, z] = pltpu.roll(df, 4, 0)
        rh[FACIES, z] = jnp.where(row == 3, mh[fifth], df)
    left, right = [None] * YTILES, [None] * YTILES
    for k in range(4):
        for z in range(Z0):
            for tile, ref in enumerate((xl, xh, rl, rh)):
                g, at, width = block_of(k, z, tile)
                v = ref[k, z]
                here = lane // width == at // width
                a, b = turn(v, at), turn(v, at + width)
                left[g] = a if at == 0 else jnp.where(here, a, left[g])
                right[g] = b if at == 0 else jnp.where(here, b, right[g])
    for g in range(YTILES):
        lo[g] = left[g]
        hi[g] = right[g]


def level0(pos, tables, xl, xh, rl, rh, yl, yh, a, packed, raw, hs, vs, dd, res, sk, t, m):
    gx, gy, gz = pos[0], pos[1], pos[2]
    lane8 = iota((8, 128), 1)
    for k in range(4):
        for z in range(Z0):
            for tile in range(4):
                g, at, width = block_of(k, z, tile)
                raw[k, z, 8 * tile : 8 * tile + 8, 128:256] = jnp.where(
                    lane8 < width,
                    turn(yl[g], -at),
                    jnp.where(lane8 >= 128 - width, turn(yh[g], -at - width), 0.0),
                )
    for row, ref in ((0, xl), (8, xh), (16, rl), (24, rh)):
        raw[:, :, row : row + 8, 0:128] = ref[...]

    row, lane = iota((32, 256), 0), iota((32, 256), 1)
    x = gx * 16 + jnp.where(row < 24, row, row - 32)
    y = gy * 128 + jnp.where(lane < 192, lane, lane - 256)
    inside = (x >= 0) & (x < 256) & (y >= 0) & (y < 512)

    def materials(z):
        zg = gz * 8 + z - H
        here = inside & ((zg >= 0) & (zg < 32))
        kind = raw[0, z]
        h = jnp.full((32, 256), tables[0], F32)
        v = jnp.full((32, 256), tables[8], F32)
        for n in range(1, 8):
            is_n = kind == float(n)
            h = jnp.where(is_n, tables[n], h)
            v = jnp.where(is_n, tables[8 + n], v)
        hs[z] = jnp.where(here, h, 0.0)
        vs[z] = jnp.where(here, v, 0.0)

    each(0, Z0, materials, 2)

    def harmonic(c, n):
        s = c + n
        return 2.0 * c * n / jnp.where(s > 0.0, s, 1.0)

    def couple(z):
        h = hs[z]
        a[UX, z] = harmonic(h, up(h, 0))
        a[UY, z] = harmonic(h, up(h, 1))
        a[UZ, z] = harmonic(vs[z], vs[z + 1])

    each(0, Z0 - 1, couple, 2)

    odd_row, odd_lane = row % 2 == 1, lane % 2 == 1

    def setup(z):
        h, v = hs[z], vs[z]
        sink = jnp.where(raw[1, z] == 1.0, 2.0 * v, jnp.where(raw[1, z] == 2.0, 0.5 * h, 0.0))
        ux, uy, uz, lz = a[UX, z], a[UY, z], a[UZ, z], a[UZ, z - 1]
        lx, ly = down(ux, 0), down(uy, 1)
        diag = sink + lz + uz + lx + ux + ly + uy
        dens = raw[3, z]
        b = raw[2, z] + 0.5 * uz * (dens + raw[3, z + 1]) - 0.5 * lz * (raw[3, z - 1] + dens)
        rd = jnp.where(diag > 0.0, W / jnp.where(diag > 0.0, diag, 1.0), 0.0)
        a[RD, z] = rd
        a[C, z] = rd * b
        dd[z] = diag
        sk[z] = sink
        outer = sink + jnp.where(odd_row, ux, lx) + jnp.where(odd_lane, uy, ly)
        hs[z] = outer + jnp.where((z - H) % 2 == 1, uz, lz)

    each(1, Z0 - 1, setup, 2)

    def first(z):
        a[V, z] = smoothed(a, lambda k: a[C, k], z, z - 1, z + 1)

    each(2, Z0 - 2, first, 2)

    def residual(z):
        v, beside = around(a, lambda k: a[V, k], z, z - 1, z + 1)
        res[z - H] = (dd[z] * (1.5 * a[C, z] - v) + beside)[0:16, 0:128]

    each(H, H + 8, residual, 2)

    o_row = iota((16, 128), 0) % 2 == 1
    o_lane = iota((16, 128), 1) % 2 == 1

    def coarsen(z):
        lo, hi = H + 2 * z, H + 2 * z + 1

        def both(ref):
            return ref[lo, 0:16, 0:128] + ref[hi, 0:16, 0:128]

        parts = (
            jnp.where(o_row, both(a.at[UX]), 0.0),
            jnp.where(o_lane, both(a.at[UY]), 0.0),
            a[UZ, hi, 0:16, 0:128],
            both(sk),
            res[2 * z] + res[2 * z + 1],
            both(hs),
        )
        for k, part in enumerate(parts):
            t[k, z] = part
        for k in range(6):
            m[k, z] = fold_rows(t.at[k, z], 8)

    each(0, 4, coarsen, 4)
    lower = lane8 < 64
    for s in range(2):
        parts = [jnp.where(lower, fold_lanes(m[k, s]), fold_lanes(m[k, 2 + s])) for k in range(6)]
        for k in range(4):
            packed[k, s] = parts[k]
        packed[4, s] = W * parts[4] / parts[5]


def pack_x1(own, b1, b2, b3, full, lo, hi):
    for n, ref in enumerate((own, b1, b2, b3)):
        full[:, 2 * n : 2 * n + 2] = ref[...]
        first, second = ref[:, 0], ref[:, 1]
        lo[:, n] = jnp.concatenate([first[:, 0:4], second[:, 0:4]], axis=1)
        hi[:, n] = jnp.concatenate([first[:, 4:8], second[:, 4:8]], axis=1)


def pack_y1(own, r1, l1, r2, l2, whole, lo, hi):
    whole[:, :, 0:8] = own[...]
    whole[:, :, 8:16] = r1[...]
    whole[:, :, 24:32] = l1[...]
    for n in range(4):
        for s in range(2):
            part = slice(4 * s, 4 * s + 4)
            whole[:, 2 * n + s, 16:24] = jnp.concatenate([r2[:, n, part], l2[:, n, part]], axis=1)
    block = (iota((8, 128), 1) % 64) // 12
    for g in range(32):
        left = right = None
        for at in range(5):
            layer, tile = divmod(5 * g + at, 4)
            v = whole[layer // 8, layer % 8, 8 * tile : 8 * tile + 8]
            a, b = turn(v, 12 * at), turn(v, 12 * at - 52)
            left = a if at == 0 else jnp.where(block == at, a, left)
            right = b if at == 0 else jnp.where(block == at, b, right)
        lo[g] = left
        hi[g] = right


def level12(pos, whole, yl, yh, a, b, sent, d1, r1, t1, m1, d2, r2, s1, s2, q2):
    gx, gy, gz = pos[0], pos[1], pos[2]
    row, lane = iota((8, 128), 0), iota((8, 128), 1)
    y = gy * 64 + jnp.where(lane < 96, lane, lane - 128)
    in_y = (y >= 0) & (y < 256)
    for tile in range(4):
        x = gx * 8 + jnp.where(8 * tile + row < 20, 8 * tile + row, 8 * tile + row - 32)
        inside = in_y & (x >= 0) & (x < 128)
        rows = slice(8 * tile, 8 * tile + 8)
        for k in range(5):
            for n in range(8):
                g, at = divmod(4 * (8 * k + n) + tile, 5)
                v, right, left = whole[k, n, rows], yl[g], yh[g]
                for part in range(2):
                    own = turn(v, 64 * part)
                    beyond = jnp.where(
                        lane < 76,
                        turn(right, 64 - 64 * part - 12 * at),
                        jnp.where(lane >= 116, turn(left, 116 - 64 * part - 12 * at), 0.0),
                    )
                    value = jnp.where(inside, jnp.where(lane < 64, own, beyond), 0.0)
                    z = 4 * (n // 2) + 2 * part + n % 2
                    a[k, z, rows] = value
                    if k == SINK:
                        s1[z, rows] = value
    pre(a, d1, None, r1, 16, 4)

    def keep1(k, z, value):
        value = fold_lanes(value)
        if k < 4:
            b[k, z] = value
        if k == SINK:
            s2[z] = value
        if k == 4:
            q2[z] = value

    halve(a, s1, r1, t1, keep1, 16, 32)
    pre(b, d2, q2, r2, 8, 8)

    def keep2(k, z, value):
        m1[z, 0, k : k + 1] = value[0:1]
        m1[z, 1, k : k + 1] = value[1:2]

    m1[...] = jnp.zeros((4, 2, 8, 128), F32)
    halve(b, s2, r2, t1.at[:, :, 0:16], keep2, 8, 16)
    total = jnp.zeros((8, 128), F32)
    for z in range(4):
        zg = lax.rem(z + gz, 4)
        for s in range(2):
            v = m1[z, s]
            v = pick(v + up(v, 1), 2 * (lane % 16))
            total = jnp.where(lane // 16 == 2 * zg + s, v, total)
    for k in range(5):
        sent[:, :, 128 * k : 128 * k + 128] = jnp.broadcast_to(total[k : k + 1][None], (64, 1, 128))


def sweep(a, src, dst, n, unroll):
    c3 = circ(n)

    def body(z):
        dst[z] = smoothed(a, lambda k: src[k], *c3(z))

    each(0, n, body, unroll)


def solve(
    pos, got, a0, a1, a2, pressure, left,
    a3, a4, d3, d4, r3, r4, s3, s4, t3, q5, e1, e2, e3, e4, f2, g4, g3, g2, g1, g0, b3, w0,
):
    gx, gy, gz = pos[0], pos[1], pos[2]
    lane = iota((16, 128), 1)
    for k in range(5):
        rows = [got[16 * g : 16 * g + 16, 0, 128 * k : 128 * k + 128] for g in range(4)]
        for z in range(4):
            for s in range(2):
                at = (z * 2 + s) * 16
                value = turn(rows[0], -at)
                for g in range(1, 4):
                    value = jnp.where(lane // 16 == g, turn(rows[g], 16 * g - at), value)
                value = jnp.where(lane < 64, value, turn(value, 64))
                if k < 4:
                    a3[k, z, pl.ds(s, 16, stride=2), :] = value
                else:
                    r3[z, pl.ds(s, 16, stride=2), :] = value
    s3[...] = a3[SINK]
    pre(a3, d3, r3, e3, 4, 4)

    def keep3(k, z, value):
        value = fold_lanes(value)
        if k < 4:
            a4[k, z] = value
        if k == SINK:
            s4[z] = value
        if k == 4:
            r4[z] = value

    halve(a3, s3, e3, t3, keep3, 4, 32)
    pre(a4, d4, r4, e4, 2, 2)

    def keep4(k, z, value):
        q5[k] = fold_lanes(value)

    halve(a4, s4, e4, t3.at[:, :, 0:16], keep4, 2, 16)
    ux, uy, uz, sink, r = q5[0], q5[1], q5[2], q5[3], q5[4]
    lx, ly = down(ux, 0), down(uy, 1)
    diag = sink + uz + uz + ux + lx + uy + ly
    rd = W / diag
    c = rd * r
    ux, lx, uy, ly = rd * ux, rd * lx, rd * uy, rd * ly
    v = c
    for _ in range(COARSE_SWEEPS - 1):
        beside = (ux * up(v, 0) + lx * down(v, 0)) + (uy * up(v, 1) + ly * down(v, 1))
        v = (v * (1.0 / 3.0) + c) + beside

    e = spread_rows(g4, spread_lanes(v))
    for z in range(2):
        a4[V, z] = a4[V, z] + e
    sweep(a4, a4.at[V], e4, 2, 2)
    sweep(a4, e4, r4, 2, 2)
    for z in range(2):
        e = spread_rows(g3.at[z], spread_lanes(r4[z]))
        a3[V, 2 * z] = a3[V, 2 * z] + e
        a3[V, 2 * z + 1] = a3[V, 2 * z + 1] + e
    sweep(a3, a3.at[V], e3, 4, 4)
    sweep(a3, e3, r3, 4, 4)
    b3[:, 8:40] = r3[...]
    b3[:, 0:8] = r3[:, 24:32]
    b3[:, 40:48] = r3[:, 0:8]
    lane = iota((8, 128), 1) % 64
    index = jnp.where(lane < 40, lane // 2, lane // 2 - 32) + 16 * gy
    index = lax.rem(index + 64, 64)
    for z in range(4):
        e = b3[lax.rem(z + gz, 4), pl.ds(2 * gx + 5, 8), :]
        e = pick(pltpu.roll(e, 5, 0), index)
        e = spread_rows(g2.at[z], e)
        e2[2 * z] = a2[V, 2 * z] + e
        e2[2 * z + 1] = a2[V, 2 * z + 1] + e
    sweep(a2, e2, f2, 8, 8)
    sweep(a2, f2, e2, 8, 8)
    for z in range(8):
        e = spread_rows(g1.at[z], spread_lanes(e2[z]))
        e1[0, 2 * z] = a1[V, 2 * z] + e
        e1[0, 2 * z + 1] = a1[V, 2 * z + 1] + e
    sweep(a1, e1.at[0], e1.at[1], 16, 4)
    sweep(a1, e1.at[1], e1.at[0], 16, 4)
    upper = iota((8, 128), 0) < 4
    for zc in range(-2, 6):
        v = e1[0, zc % 16]
        v = jnp.concatenate([v[0:8], jnp.where(upper, v[8:16], v[24:32])], axis=0)
        for half in range(2):
            e = spread_rows(g0.at[half, zc + 2], spread_lanes(v, 64 * half))
            lanes = slice(128 * half, 128 * half + 128)
            for z in (2 * zc, 2 * zc + 1):
                if -3 <= z <= 10:
                    w0[0, z + H, :, lanes] = a0[V, z + H, :, lanes] + e

    def sweep0(src, dst):
        def body(z):
            w0[dst, z] = smoothed(a0, lambda k: w0[src, k], z, z - 1, z + 1)

        return body

    each(3, Z0 - 3, sweep0(0, 1), 2)
    each(4, Z0 - 4, sweep0(1, 0), 2)

    def last(z):
        v, beside = around(a0, lambda k: w0[0, k], z, z - 1, z + 1)
        r = W / a0[RD, z] * (1.5 * a0[C, z] - v) + beside
        pressure[z - H] = v[0:16, 0:128]
        left[z - H] = r[0:16, 0:128]

    each(H, H + 8, last, 2)


def shift(value, axis, by):
    count = lax.axis_size(axis)
    return lax.ppermute(value, axis, [((i + by) % count, i) for i in range(count)])


def local(facies, boundary, hc, vc, source, density):
    pos = jnp.stack([lax.axis_index(n) for n in ("gx", "gy", "gz")]).astype(jnp.int32)
    tables = jnp.concatenate([hc, vc])
    lo, hi, own = call(
        pack_z,
        [(4, H, 16, 128)] * 2 + [(4, 8, 16, 128)],
        facies, boundary, source, density,
        spaces=[HBM] * 4,
        limit=60,
        scratch=[
            pltpu.VMEM((8, 16, 128), jnp.int32), pltpu.VMEM((8, 16, 128), jnp.int32),
            pltpu.SemaphoreType.DMA((4,)),
        ],
    )
    above, below = shift(lo, "gz", 1), shift(hi, "gz", -1)
    xl, xh, lo, hi = call(
        pack_x, [(4, Z0, 8, 128)] * 2 + [(XTILES, 8, 128)] * 2, own, above, below
    )
    ml, mh = shift(lo, "gx", 1), shift(hi, "gx", -1)
    rl, rh, lo, hi = call(
        pack_y, [(4, Z0, 8, 128)] * 2 + [(YTILES, 8, 128)] * 2, xl, xh, ml, mh
    )
    yl, yh = shift(lo, "gy", 1), shift(hi, "gy", -1)
    a0, packed = call(
        level0,
        [(6, Z0, 32, 256), (5, 2, 8, 128)],
        pos, tables, xl, xh, rl, rh, yl, yh,
        spaces=[SMEM] * 2 + [VMEM] * 6,
        scratch=[
            (4, Z0, 32, 256), (Z0, 32, 256), (Z0, 32, 256), (Z0, 32, 256), (8, 16, 128),
            (Z0, 32, 256), (6, 4, 16, 128), (6, 4, 8, 128),
        ],
    )
    blocks = [shift(packed, "gz", n) for n in (1, 2, 3)]
    full, lo, hi = call(
        pack_x1, [(5, 8, 8, 128), (5, 4, 8, 128), (5, 4, 8, 128)], packed, *blocks
    )
    r1, l1 = shift(full, "gx", 1), shift(full, "gx", -1)
    r2, l2 = shift(lo, "gx", 2), shift(hi, "gx", -2)
    whole, lo, hi = call(
        pack_y1, [(5, 8, 32, 128), (32, 8, 128), (32, 8, 128)], full, r1, l1, r2, l2
    )
    yl, yh = shift(lo, "gy", 1), shift(hi, "gy", -1)
    a1, a2, sent = call(
        level12,
        [(6, 16, 32, 128), (6, 8, 16, 128), (64, 1, 640)],
        pos, whole, yl, yh,
        spaces=[SMEM] + [VMEM] * 3,
        scratch=[
            (16, 32, 128), (16, 32, 128), (5, 8, 32, 128), (4, 2, 8, 128),
            (8, 16, 128), (8, 16, 128), (16, 32, 128), (8, 16, 128), (8, 16, 128),
        ],
    )
    got = lax.all_to_all(sent, ("gy", "gx"), 0, 0)
    return tuple(
        call(
            solve,
            [(8, 16, 128), (8, 16, 128)],
            pos, got, a0, a1, a2,
            spaces=[SMEM] + [VMEM] * 4,
            scratch=[
                (6, 4, 32, 128), (6, 2, 16, 128),
                (4, 32, 128), (2, 16, 128),
                (4, 32, 128), (2, 16, 128), (4, 32, 128), (2, 16, 128),
                (5, 2, 32, 128), (5, 8, 128),
                (2, 16, 32, 128), (8, 16, 128), (4, 32, 128), (2, 16, 128), (8, 16, 128),
                (16, 128), (2, 32, 128), (4, 16, 128), (8, 32, 128), (2, 8, 32, 128),
                (4, 48, 128), (2, Z0, 32, 256),
            ],
        )
    )


def solution(mesh):
    split = P("gz", "gx", "gy")
    return jax.shard_map(
        local,
        mesh=mesh,
        in_specs=(split, split, P(), P(), split, split),
        out_specs=(split, split),
        check_vma=False,
    )
```

```python
import jax
import jax.numpy as jnp
from jax import lax
from jax.experimental import pallas as pl
from jax.experimental.pallas import tpu as pltpu
from jax.sharding import PartitionSpec as P

COARSE_SWEEPS = 8
W = 2.0 / 3.0
F32 = jnp.float32
UX, UY, UZ, RD, C, V = range(6)
SINK = RD
H = 5
Z0 = 8 + 2 * H

VMEM = pl.BlockSpec(memory_space=pltpu.VMEM)
SMEM = pl.BlockSpec(memory_space=pltpu.SMEM)
HBM = pl.BlockSpec(memory_space=pltpu.HBM)


def call(kernel, outs, *args, scratch=(), spaces=None, limit=24):
    return pl.pallas_call(
        kernel,
        out_shape=[jax.ShapeDtypeStruct(s, F32) for s in outs],
        in_specs=spaces or [VMEM] * len(args),
        out_specs=[VMEM] * len(outs),
        scratch_shapes=[pltpu.VMEM(s, F32) if isinstance(s, tuple) else s for s in scratch],
        compiler_params=pltpu.CompilerParams(vmem_limit_bytes=limit * 2**20),
    )(*args)


def iota(shape, dim):
    return lax.broadcasted_iota(jnp.int32, shape, dim)


def up(a, dim):
    return pltpu.roll(a, a.shape[dim] - 1, dim)


def down(a, dim):
    return pltpu.roll(a, 1, dim)


def turn(a, by):
    by %= 128
    return pltpu.roll(a, by, a.ndim - 1) if by else a


def pick(a, index):
    return jnp.take_along_axis(a, index, axis=1, mode="promise_in_bounds")


def fold_lanes(a):
    return pick(a + up(a, 1), (2 * iota(a.shape, 1)) % 128)


def spread_lanes(a, first=0):
    return pick(a, first + iota(a.shape, 1) // 2)


def each(start, stop, body):
    for z in range(start, stop):
        body(z)


def wrap(z, n):
    return z % n


def around(a, field, z, zm, zp):
    v = field(z)
    ux, uy = a[UX, z], a[UY, z]
    out = ux * up(v, 0) + down(ux * v, 0)
    out = out + (uy * up(v, 1) + down(uy * v, 1))
    return v, out + (a[UZ, z] * field(zp) + a[UZ, zm] * field(zm))


def smoothed(a, field, z, zm, zp):
    v, beside = around(a, field, z, zm, zp)
    return v * (1.0 / 3.0) + a[C, z] + a[RD, z] * beside


def finish(a, d, r, z, zm):
    ux, uy = a[UX, z], a[UY, z]
    diag = a[SINK, z] + a[UZ, z] + a[UZ, zm] + ux + down(ux, 0) + uy + down(uy, 1)
    d[z] = diag
    rd = jnp.where(diag > 0.0, W / jnp.where(diag > 0.0, diag, 1.0), 0.0)
    a[RD, z] = rd
    if r is not None:
        a[C, z] = rd * r[z]


def circ(n):
    return lambda z: (z, wrap(z - 1, n), wrap(z + 1, n))


def pre(a, d, r, res, n):
    c3 = circ(n)
    each(0, n, lambda z: finish(a, d, r, z, wrap(z - 1, n)))

    def one(z):
        a[V, z] = smoothed(a, lambda k: a[C, k], *c3(z))

    each(0, n, one)

    def two(z):
        v, beside = around(a, lambda k: a[V, k], *c3(z))
        res[z] = d[z] * (1.5 * a[C, z] - v) + beside

    each(0, n, two)


def halve(a, sink, r, t, store, n, rows):
    odd_row = iota((rows, 128), 0) % 2 == 1
    odd_lane = iota((rows, 128), 1) % 2 == 1

    def body(z):
        lo, hi = 2 * z, 2 * z + 1
        parts = (
            jnp.where(odd_row, a[UX, lo] + a[UX, hi], 0.0),
            jnp.where(odd_lane, a[UY, lo] + a[UY, hi], 0.0),
            a[UZ, hi],
            sink[lo] + sink[hi],
            r[lo] + r[hi],
        )
        for k, part in enumerate(parts):
            t[k, z] = part
        for k in range(5):
            store(k, z, fold_rows(t.at[k, z], rows // 2))

    each(0, n // 2, body)


def fold_rows(t, n):
    return t[pl.ds(0, n, stride=2), :] + t[pl.ds(1, n, stride=2), :]


def spread_rows(t, value):
    n = value.shape[0]
    t[pl.ds(0, n, stride=2), :] = value
    t[pl.ds(1, n, stride=2), :] = value
    return t[...]


def fetch(f, b, s, d, fi, bi, sf, df, sems):
    copies = [
        pltpu.make_async_copy(src, dst, sems.at[k])
        for k, (src, dst) in enumerate(((f, fi), (b, bi), (s, sf), (d, df)))
    ]
    for copy in copies:
        copy.start()
    for copy in copies:
        copy.wait()
    return [fi[...].astype(F32), bi[...].astype(F32), sf[...], df[...]]


def pack_z(f, b, s, d, lo, hi, *scratch):
    for k, value in enumerate(fetch(f, b, s, d, *scratch)):
        lo[k] = value[0:H]
        hi[k] = value[8 - H : 8]


def fetch_own(f, b, s, d, own, *scratch):
    for k, value in enumerate(fetch(f, b, s, d, *scratch)):
        own[k] = value


FACIES, BOUNDARY, SOURCE, DENSITY = range(4)
XTILES = 2 * Z0 + 3


def pack_x(own, above, below, xl, xh, lo, hi):
    for out, row in ((xl, 0), (xh, 8)):
        out[:, 0:H] = below[:, :, row : row + 8]
        out[:, H : H + 8] = own[:, :, row : row + 8]
        out[:, H + 8 : Z0] = above[:, :, row : row + 8]
    first = iota((8, 128), 0) < 4
    lo[XTILES - 1] = hi[XTILES - 1] = jnp.zeros((8, 128), F32)
    for z in range(Z0):
        fifth = 2 * Z0 + z // 8, slice(z % 8, z % 8 + 1)
        f, b, s, d = (xl[k, z] for k in range(4))
        lo[2 * z] = jnp.where(first, b, pltpu.roll(s, 4, 0))
        lo[2 * z + 1] = jnp.where(first, d, pltpu.roll(f, 4, 0))
        lo[fifth] = f[4:5]
        f, b, s, d = (xh[k, z] for k in range(4))
        hi[2 * z] = jnp.where(first, pltpu.roll(b, 4, 0), s)
        hi[2 * z + 1] = jnp.where(first, pltpu.roll(d, 4, 0), f)
        hi[fifth] = f[3:4]


SMALL = 7
YTILES = SMALL + 5


def block_of(k, z, tile):
    if k == FACIES:
        return SMALL + z // 4, 8 * (4 * (z % 4) + tile), 8
    layer = (k - 1) * Z0 + z
    return layer // 8, 4 * (4 * (layer % 8) + tile), 4


def pack_y(xl, xh, ml, mh, rl, rh, lo, hi):
    row, lane = iota((8, 128), 0), iota((8, 128), 1)
    for z in range(Z0):
        fifth = 2 * Z0 + z // 8, slice(z % 8, z % 8 + 1)
        bs, df = ml[2 * z], ml[2 * z + 1]
        rl[BOUNDARY, z] = bs
        rl[SOURCE, z] = pltpu.roll(bs, 4, 0)
        rl[DENSITY, z] = df
        rl[FACIES, z] = jnp.where(row == 4, ml[fifth], pltpu.roll(df, 4, 0))
        bs, df = mh[2 * z], mh[2 * z + 1]
        rh[BOUNDARY, z] = pltpu.roll(bs, 4, 0)
        rh[SOURCE, z] = bs
        rh[DENSITY, z] = pltpu.roll(df, 4, 0)
        rh[FACIES, z] = jnp.where(row == 3, mh[fifth], df)
    left, right = [None] * YTILES, [None] * YTILES
    for k in range(4):
        for z in range(Z0):
            for tile, ref in enumerate((xl, xh, rl, rh)):
                g, at, width = block_of(k, z, tile)
                v = ref[k, z]
                v = turn(v, at)
                left[g] = v if at == 0 else jnp.where(lane // width == at // width, v, left[g])
                before = (at // width - 1) % (128 // width)
                right[g] = v if at == 0 else jnp.where(lane // width == before, v, right[g])
    for g in range(YTILES):
        lo[g] = left[g]
        hi[g] = right[g]


PART = PUX, PUZ, PSINK, PB, PH = range(5)


def tile0(pos, tables, raw, first_lane, part, vs):
    row, lane = iota((32, 128), 0), iota((32, 128), 1)
    x = pos[0] * 16 + jnp.where(row < 24, row, row - 32)
    y = pos[1] * 128 + first_lane + (lane if first_lane == 0 else jnp.where(lane < 64, lane, lane - 256))
    inside = (x >= 0) & (x < 256) & (y >= 0) & (y < 512)
    for z in range(Z0):
        zg = pos[2] * 8 + z - H
        here = inside & ((zg >= 0) & (zg < 32))
        kind = raw(FACIES, z)
        h = jnp.full((32, 128), tables[0], F32)
        v = jnp.full((32, 128), tables[8], F32)
        for n in range(1, 8):
            is_n = kind == float(n)
            h = jnp.where(is_n, tables[n], h)
            v = jnp.where(is_n, tables[8 + n], v)
        part[PH, z] = jnp.where(here, h, 0.0)
        vs[z] = jnp.where(here, v, 0.0)
    for z in range(Z0 - 1):
        h, v = part[PH, z], vs[z]
        hn, vn = up(h, 0), vs[z + 1]
        hsum, vsum = h + hn, v + vn
        hsum = jnp.where(hsum > 0.0, hsum, 1.0)
        vsum = jnp.where(vsum > 0.0, vsum, 1.0)
        twice = 2.0 / (hsum * vsum)
        part[PUX, z] = (h * hn) * (twice * vsum)
        part[PUZ, z] = (v * vn) * (twice * hsum)
    for z in range(1, Z0 - 1):
        kind = raw(BOUNDARY, z)
        part[PSINK, z] = jnp.where(
            kind == 1.0, 2.0 * vs[z], jnp.where(kind == 2.0, 0.5 * part[PH, z], 0.0)
        )
        dens = raw(DENSITY, z)
        part[PB, z] = (
            raw(SOURCE, z)
            + 0.5 * part[PUZ, z] * (dens + raw(DENSITY, z + 1))
            - 0.5 * part[PUZ, z - 1] * (raw(DENSITY, z - 1) + dens)
        )


def main0(pos, tables, xl, xh, rl, rh, part, vs):
    def raw(k, z):
        return jnp.concatenate([ref[k, z] for ref in (xl, xh, rl, rh)], axis=0)

    tile0(pos, tables, raw, 0, part, vs)


def level0(pos, tables, main, yl, yh, a, packed, raw, side, vs, hs, dd, res, t, m):
    lane8 = iota((8, 128), 1)
    for k in range(4):
        for z in range(Z0):
            for tile in range(4):
                g, at, width = block_of(k, z, tile)
                both = jnp.where(lane8 // width == at // width, yl[g], yh[g])
                raw[k, z, 8 * tile : 8 * tile + 8] = turn(both, -at)
    tile0(pos, tables, lambda k, z: raw[k, z], 128, side, vs)

    def both(k, z):
        return jnp.concatenate([main[k, z], side[k, z]], axis=1)

    row, lane = iota((32, 256), 0), iota((32, 256), 1)
    odd_row, odd_lane = row % 2 == 1, lane % 2 == 1
    a[UZ, 0] = both(PUZ, 0)
    for z in range(1, Z0 - 1):
        h, sink, ux, uz, lz = both(PH, z), both(PSINK, z), both(PUX, z), both(PUZ, z), a[UZ, z - 1]
        hn = up(h, 1)
        hsum = h + hn
        uy = 2.0 * h * hn / jnp.where(hsum > 0.0, hsum, 1.0)
        a[UX, z], a[UY, z], a[UZ, z] = ux, uy, uz
        lx, ly = down(ux, 0), down(uy, 1)
        diag = sink + lz + uz + lx + ux + ly + uy
        rd = jnp.where(diag > 0.0, W / jnp.where(diag > 0.0, diag, 1.0), 0.0)
        a[RD, z] = rd
        a[C, z] = rd * both(PB, z)
        dd[z] = diag
        outer = sink + jnp.where(odd_row, ux, lx) + jnp.where(odd_lane, uy, ly)
        hs[z] = (outer + (uz if (z - H) % 2 == 1 else lz))[0:16, 0:128]

    def first(z):
        a[V, z] = smoothed(a, lambda k: a[C, k], z, z - 1, z + 1)

    each(2, Z0 - 2, first)

    def residual(z):
        v, beside = around(a, lambda k: a[V, k], z, z - 1, z + 1)
        res[z - H] = (dd[z] * (1.5 * a[C, z] - v) + beside)[0:16, 0:128]

    each(H, H + 8, residual)

    o_row = iota((16, 128), 0) % 2 == 1
    o_lane = iota((16, 128), 1) % 2 == 1

    def coarsen(z):
        lo, hi = H + 2 * z, H + 2 * z + 1

        def pair(ref):
            return ref[lo, 0:16, 0:128] + ref[hi, 0:16, 0:128]

        parts = (
            jnp.where(o_row, pair(a.at[UX]), 0.0),
            jnp.where(o_lane, pair(a.at[UY]), 0.0),
            a[UZ, hi, 0:16, 0:128],
            pair(main.at[PSINK]),
            res[2 * z] + res[2 * z + 1],
            hs[lo] + hs[hi],
        )
        for k, part in enumerate(parts):
            t[k, z] = part
        for k in range(6):
            m[k, z] = fold_rows(t.at[k, z], 8)

    each(0, 4, coarsen)
    lower = lane8 < 64
    for s in range(2):
        parts = [jnp.where(lower, fold_lanes(m[k, s]), fold_lanes(m[k, 2 + s])) for k in range(6)]
        for k in range(4):
            packed[k, s] = parts[k]
        packed[4, s] = W * parts[4] / parts[5]


def pack_x1(own, b1, b2, b3, full, lo, hi):
    for n, ref in enumerate((own, b1, b2, b3)):
        full[:, 2 * n : 2 * n + 2] = ref[...]
        first, second = ref[:, 0], ref[:, 1]
        lo[:, n] = jnp.concatenate([first[:, 0:4], second[:, 0:4]], axis=1)
        hi[:, n] = jnp.concatenate([first[:, 4:8], second[:, 4:8]], axis=1)


def pack_y1(own, r1, l1, r2, l2, whole, lo, hi):
    whole[:, :, 0:8] = own[...]
    whole[:, :, 8:16] = r1[...]
    whole[:, :, 24:32] = l1[...]
    for n in range(4):
        for s in range(2):
            part = slice(4 * s, 4 * s + 4)
            whole[:, 2 * n + s, 16:24] = jnp.concatenate([r2[:, n, part], l2[:, n, part]], axis=1)
    lane = iota((8, 128), 1)
    block, last = (lane % 64) // 12, ((lane + 12) % 64) // 12
    for g in range(32):
        left = right = None
        for at in range(5):
            layer, tile = divmod(5 * g + at, 4)
            v = whole[layer // 8, layer % 8, 8 * tile : 8 * tile + 8]
            v = turn(v, 12 * at)
            left = v if at == 0 else jnp.where(block == at, v, left)
            right = v if at == 0 else jnp.where(last == at, v, right)
        lo[g] = left
        hi[g] = right


def level12(pos, whole, yl, yh, a, b, sent, d1, r1, t1, m1, d2, r2, s1, s2, q2):
    gx, gy, gz = pos[0], pos[1], pos[2]
    row, lane = iota((8, 128), 0), iota((8, 128), 1)
    y = gy * 64 + jnp.where(lane < 96, lane, lane - 128)
    in_y = (y >= 0) & (y < 256)
    for tile in range(4):
        x = gx * 8 + jnp.where(8 * tile + row < 20, 8 * tile + row, 8 * tile + row - 32)
        inside = in_y & (x >= 0) & (x < 128)
        rows = slice(8 * tile, 8 * tile + 8)
        for k in range(5):
            for n in range(8):
                g, at = divmod(4 * (8 * k + n) + tile, 5)
                v = whole[k, n, rows]
                near = jnp.where((lane % 64) // 12 == at, yl[g], yh[g])
                for part in range(2):
                    own = turn(v, 64 * part)
                    beyond = turn(near, 64 - 64 * part - 12 * at)
                    value = jnp.where(inside, jnp.where(lane < 64, own, beyond), 0.0)
                    z = 4 * (n // 2) + 2 * part + n % 2
                    a[k, z, rows] = value
                    if k == SINK:
                        s1[z, rows] = value
    pre(a, d1, None, r1, 16)

    def keep1(k, z, value):
        value = fold_lanes(value)
        if k < 4:
            b[k, z] = value
        if k == SINK:
            s2[z] = value
        if k == 4:
            q2[z] = value

    halve(a, s1, r1, t1, keep1, 16, 32)
    pre(b, d2, q2, r2, 8)

    def keep2(k, z, value):
        m1[z, 0, k : k + 1] = value[0:1]
        m1[z, 1, k : k + 1] = value[1:2]

    m1[...] = jnp.zeros((4, 2, 8, 128), F32)
    halve(b, s2, r2, t1.at[:, :, 0:16], keep2, 8, 16)
    total = jnp.zeros((8, 128), F32)
    for z in range(4):
        zg = lax.rem(z + gz, 4)
        for s in range(2):
            v = m1[z, s]
            v = pick(v + up(v, 1), 2 * (lane % 16))
            total = jnp.where(lane // 16 == 2 * zg + s, v, total)
    for k in range(5):
        sent[:, :, 128 * k : 128 * k + 128] = jnp.broadcast_to(total[k : k + 1][None], (64, 1, 128))


def sweep(a, src, dst, n, layers=None):
    for z in layers or range(n):
        dst[z % n] = smoothed(a, lambda k: src[k], z % n, (z - 1) % n, (z + 1) % n)


def solve(
    pos, got, a0, a1, a2, pressure, left,
    a3, a4, d3, d4, r3, r4, s3, s4, t3, q5, e1, e2, e3, e4, f2, g4, g3, g2, g1, g0, b3, w0,
):
    gx, gy, gz = pos[0], pos[1], pos[2]
    lane = iota((16, 128), 1)
    for k in range(5):
        rows = [got[16 * g : 16 * g + 16, 0, 128 * k : 128 * k + 128] for g in range(4)]
        for z in range(4):
            for s in range(2):
                at = (z * 2 + s) * 16
                value = turn(rows[0], -at)
                for g in range(1, 4):
                    value = jnp.where(lane // 16 == g, turn(rows[g], 16 * g - at), value)
                value = jnp.where(lane < 64, value, turn(value, 64))
                if k < 4:
                    a3[k, z, pl.ds(s, 16, stride=2), :] = value
                else:
                    r3[z, pl.ds(s, 16, stride=2), :] = value
    s3[...] = a3[SINK]
    pre(a3, d3, r3, e3, 4)

    def keep3(k, z, value):
        value = fold_lanes(value)
        if k < 4:
            a4[k, z] = value
        if k == SINK:
            s4[z] = value
        if k == 4:
            r4[z] = value

    halve(a3, s3, e3, t3, keep3, 4, 32)
    pre(a4, d4, r4, e4, 2)

    def keep4(k, z, value):
        q5[k] = fold_lanes(value)

    halve(a4, s4, e4, t3.at[:, :, 0:16], keep4, 2, 16)
    ux, uy, uz, sink, r = q5[0], q5[1], q5[2], q5[3], q5[4]
    lx, ly = down(ux, 0), down(uy, 1)
    diag = sink + uz + uz + ux + lx + uy + ly
    rd = W / diag
    c = rd * r
    ux, lx, uy, ly = rd * ux, rd * lx, rd * uy, rd * ly
    v = c
    for _ in range(COARSE_SWEEPS - 1):
        beside = (ux * up(v, 0) + lx * down(v, 0)) + (uy * up(v, 1) + ly * down(v, 1))
        v = (v * (1.0 / 3.0) + c) + beside

    e = spread_rows(g4, spread_lanes(v))
    for z in range(2):
        a4[V, z] = a4[V, z] + e
    sweep(a4, a4.at[V], e4, 2)
    sweep(a4, e4, r4, 2)
    for z in range(2):
        e = spread_rows(g3.at[z], spread_lanes(r4[z]))
        a3[V, 2 * z] = a3[V, 2 * z] + e
        a3[V, 2 * z + 1] = a3[V, 2 * z + 1] + e
    sweep(a3, a3.at[V], e3, 4)
    sweep(a3, e3, r3, 4)
    b3[:, 8:40] = r3[...]
    b3[:, 0:8] = r3[:, 24:32]
    b3[:, 40:48] = r3[:, 0:8]
    lane = iota((8, 128), 1) % 64
    index = jnp.where(lane < 40, lane // 2, lane // 2 - 32) + 16 * gy
    index = lax.rem(index + 64, 64)
    for z in range(4):
        e = b3[lax.rem(z + gz, 4), pl.ds(2 * gx + 5, 8), :]
        e = pick(pltpu.roll(e, 5, 0), index)
        e = spread_rows(g2.at[z], e)
        e2[2 * z] = a2[V, 2 * z] + e
        e2[2 * z + 1] = a2[V, 2 * z + 1] + e
    sweep(a2, e2, f2, 8)
    sweep(a2, f2, e2, 8, range(-2, 4))
    for z in range(-2, 4):
        e = spread_rows(g1.at[z % 8], spread_lanes(e2[z % 8]))
        for zf in (2 * z % 16, 2 * z % 16 + 1):
            e1[0, zf] = a1[V, zf] + e
    sweep(a1, e1.at[0], e1.at[1], 16, range(-3, 7))
    sweep(a1, e1.at[1], e1.at[0], 16, range(-2, 6))
    upper = iota((8, 128), 0) < 4
    for zc in range(-2, 6):
        v = e1[0, zc % 16]
        v = jnp.concatenate([v[0:8], jnp.where(upper, v[8:16], v[24:32])], axis=0)
        for half in range(2):
            e = spread_rows(g0.at[half, zc + 2], spread_lanes(v, 64 * half))
            lanes = slice(128 * half, 128 * half + 128)
            for z in (2 * zc, 2 * zc + 1):
                if -3 <= z <= 10:
                    w0[0, z + H, :, lanes] = a0[V, z + H, :, lanes] + e

    def sweep0(src, dst):
        def body(z):
            w0[dst, z] = smoothed(a0, lambda k: w0[src, k], z, z - 1, z + 1)

        return body

    each(3, Z0 - 3, sweep0(0, 1))
    each(4, Z0 - 4, sweep0(1, 0))

    def last(z):
        v, beside = around(a0, lambda k: w0[0, k], z, z - 1, z + 1)
        r = W / a0[RD, z] * (1.5 * a0[C, z] - v) + beside
        pressure[z - H] = v[0:16, 0:128]
        left[z - H] = r[0:16, 0:128]

    each(H, H + 8, last)


def shift(value, axis, by):
    count = lax.axis_size(axis)
    return lax.ppermute(value, axis, [((i + by) % count, i) for i in range(count)])


def local(facies, boundary, hc, vc, source, density):
    pos = jnp.stack([lax.axis_index(n) for n in ("gx", "gy", "gz")]).astype(jnp.int32)
    tables = jnp.concatenate([hc, vc])
    raw = (facies, boundary, source, density)
    landing = [
        pltpu.VMEM((8, 16, 128), jnp.int32), pltpu.VMEM((8, 16, 128), jnp.int32),
        (8, 16, 128), (8, 16, 128), pltpu.SemaphoreType.DMA((4,)),
    ]
    plan = dict(spaces=[HBM] * 4, scratch=landing, limit=60)
    lo, hi = call(pack_z, [(4, H, 16, 128)] * 2, *raw, **plan)
    above, below = shift(lo, "gz", 1), shift(hi, "gz", -1)
    (own,) = call(fetch_own, [(4, 8, 16, 128)], *raw, **plan)
    xl, xh, lo, hi = call(
        pack_x, [(4, Z0, 8, 128)] * 2 + [(XTILES, 8, 128)] * 2, own, above, below
    )
    ml, mh = shift(lo, "gx", 1), shift(hi, "gx", -1)
    rl, rh, lo, hi = call(
        pack_y, [(4, Z0, 8, 128)] * 2 + [(YTILES, 8, 128)] * 2, xl, xh, ml, mh
    )
    yl, yh = shift(lo, "gy", 1), shift(hi, "gy", -1)
    (main,) = call(
        main0, [(5, Z0, 32, 128)], pos, tables, xl, xh, rl, rh,
        spaces=[SMEM] * 2 + [VMEM] * 4, scratch=[(Z0, 32, 128)],
    )
    a0, packed = call(
        level0,
        [(6, Z0, 32, 256), (5, 2, 8, 128)],
        pos, tables, main, yl, yh,
        spaces=[SMEM] * 2 + [VMEM] * 3,
        scratch=[
            (4, Z0, 32, 128), (5, Z0, 32, 128), (Z0, 32, 128), (Z0, 16, 128), (Z0, 32, 256),
            (8, 16, 128), (6, 4, 16, 128), (6, 4, 8, 128),
        ],
    )
    blocks = [shift(packed, "gz", n) for n in (1, 2, 3)]
    full, lo, hi = call(
        pack_x1, [(5, 8, 8, 128), (5, 4, 8, 128), (5, 4, 8, 128)], packed, *blocks
    )
    r1, l1 = shift(full, "gx", 1), shift(full, "gx", -1)
    r2, l2 = shift(lo, "gx", 2), shift(hi, "gx", -2)
    whole, lo, hi = call(
        pack_y1, [(5, 8, 32, 128), (32, 8, 128), (32, 8, 128)], full, r1, l1, r2, l2
    )
    yl, yh = shift(lo, "gy", 1), shift(hi, "gy", -1)
    a1, a2, sent = call(
        level12,
        [(6, 16, 32, 128), (6, 8, 16, 128), (64, 1, 640)],
        pos, whole, yl, yh,
        spaces=[SMEM] + [VMEM] * 3,
        scratch=[
            (16, 32, 128), (16, 32, 128), (5, 8, 32, 128), (4, 2, 8, 128),
            (8, 16, 128), (8, 16, 128), (16, 32, 128), (8, 16, 128), (8, 16, 128),
        ],
    )
    got = lax.all_to_all(sent, ("gy", "gx"), 0, 0)
    return tuple(
        call(
            solve,
            [(8, 16, 128), (8, 16, 128)],
            pos, got, a0, a1, a2,
            spaces=[SMEM] + [VMEM] * 4,
            scratch=[
                (6, 4, 32, 128), (6, 2, 16, 128),
                (4, 32, 128), (2, 16, 128),
                (4, 32, 128), (2, 16, 128), (4, 32, 128), (2, 16, 128),
                (5, 2, 32, 128), (5, 8, 128),
                (2, 16, 32, 128), (8, 16, 128), (4, 32, 128), (2, 16, 128), (8, 16, 128),
                (16, 128), (2, 32, 128), (4, 16, 128), (8, 32, 128), (2, 8, 32, 128),
                (4, 48, 128), (2, Z0, 32, 256),
            ],
        )
    )


def solution(mesh):
    split = P("gz", "gx", "gy")
    return jax.shard_map(
        local,
        mesh=mesh,
        in_specs=(split, split, P(), P(), split, split),
        out_specs=(split, split),
        check_vma=False,
    )
```

```python
import jax
import jax.numpy as jnp
from jax import lax
from jax.experimental import pallas as pl
from jax.experimental.pallas import tpu as pltpu
from jax.sharding import PartitionSpec as P

COARSE_SWEEPS = 8
W = 2.0 / 3.0
F32 = jnp.float32
UX, UY, UZ, RD, C, V = range(6)
SINK = RD
H = 5
Z0 = 8 + 2 * H

VMEM = pl.BlockSpec(memory_space=pltpu.VMEM)
SMEM = pl.BlockSpec(memory_space=pltpu.SMEM)
HBM = pl.BlockSpec(memory_space=pltpu.HBM)


def call(kernel, outs, *args, scratch=(), spaces=None, limit=24):
    return pl.pallas_call(
        kernel,
        out_shape=[jax.ShapeDtypeStruct(s, F32) for s in outs],
        in_specs=spaces or [VMEM] * len(args),
        out_specs=[VMEM] * len(outs),
        scratch_shapes=[pltpu.VMEM(s, F32) if isinstance(s, tuple) else s for s in scratch],
        compiler_params=pltpu.CompilerParams(vmem_limit_bytes=limit * 2**20),
    )(*args)


def iota(shape, dim):
    return lax.broadcasted_iota(jnp.int32, shape, dim)


def up(a, dim):
    return pltpu.roll(a, a.shape[dim] - 1, dim)


def down(a, dim):
    return pltpu.roll(a, 1, dim)


def turn(a, by):
    by %= 128
    return pltpu.roll(a, by, a.ndim - 1) if by else a


def pick(a, index):
    return jnp.take_along_axis(a, index, axis=1, mode="promise_in_bounds")


def fold_lanes(a):
    return pick(a + up(a, 1), (2 * iota(a.shape, 1)) % 128)


def spread_lanes(a, first=0):
    return pick(a, first + iota(a.shape, 1) // 2)


def each(start, stop, body):
    for z in range(start, stop):
        body(z)


def wrap(z, n):
    return z % n


def around(a, field, z, zm, zp):
    v = field(z)
    ux, uy = a[UX, z], a[UY, z]
    out = ux * up(v, 0) + down(ux * v, 0)
    out = out + (uy * up(v, 1) + down(uy * v, 1))
    return v, out + (a[UZ, z] * field(zp) + a[UZ, zm] * field(zm))


def smoothed(a, field, z, zm, zp):
    v, beside = around(a, field, z, zm, zp)
    return v * (1.0 / 3.0) + a[C, z] + a[RD, z] * beside


def finish(a, d, r, z, zm):
    ux, uy = a[UX, z], a[UY, z]
    diag = a[SINK, z] + a[UZ, z] + a[UZ, zm] + ux + down(ux, 0) + uy + down(uy, 1)
    d[z] = diag
    rd = jnp.where(diag > 0.0, W / jnp.where(diag > 0.0, diag, 1.0), 0.0)
    a[RD, z] = rd
    if r is not None:
        a[C, z] = rd * r[z]


def circ(n):
    return lambda z: (z, wrap(z - 1, n), wrap(z + 1, n))


def pre(a, d, r, res, n):
    c3 = circ(n)
    each(0, n, lambda z: finish(a, d, r, z, wrap(z - 1, n)))

    def one(z):
        a[V, z] = smoothed(a, lambda k: a[C, k], *c3(z))

    each(0, n, one)

    def two(z):
        v, beside = around(a, lambda k: a[V, k], *c3(z))
        res[z] = d[z] * (1.5 * a[C, z] - v) + beside

    each(0, n, two)


def halve(a, sink, r, t, store, n, rows):
    odd_row = iota((rows, 128), 0) % 2 == 1
    odd_lane = iota((rows, 128), 1) % 2 == 1

    def body(z):
        lo, hi = 2 * z, 2 * z + 1
        parts = (
            jnp.where(odd_row, a[UX, lo] + a[UX, hi], 0.0),
            jnp.where(odd_lane, a[UY, lo] + a[UY, hi], 0.0),
            a[UZ, hi],
            sink[lo] + sink[hi],
            r[lo] + r[hi],
        )
        for k, part in enumerate(parts):
            t[k, z] = part
        for k in range(5):
            store(k, z, fold_rows(t.at[k, z], rows // 2))

    each(0, n // 2, body)


def fold_rows(t, n):
    return t[pl.ds(0, n, stride=2), :] + t[pl.ds(1, n, stride=2), :]


def spread_rows(t, value):
    n = value.shape[0]
    t[pl.ds(0, n, stride=2), :] = value
    t[pl.ds(1, n, stride=2), :] = value
    return t[...]


def fetch(f, b, s, d, fi, bi, sf, df, sems):
    copies = [
        pltpu.make_async_copy(src, dst, sems.at[k])
        for k, (src, dst) in enumerate(((f, fi), (b, bi), (s, sf), (d, df)))
    ]
    for copy in copies:
        copy.start()
    for copy in copies:
        copy.wait()
    return [fi[...].astype(F32), bi[...].astype(F32), sf[...], df[...]]


def pack_z(f, b, s, d, lo, hi, *scratch):
    f, b, s, d = fetch(f, b, s, d, *scratch)
    for value, at, n in ((f, 0, H), (d, H, H), (b, 2 * H, H - 1), (s, 3 * H - 1, H - 1)):
        lo[at : at + n] = value[0:n]
        hi[at : at + n] = value[8 - n : 8]


def fetch_own(f, b, s, d, own, *scratch):
    for k, value in enumerate(fetch(f, b, s, d, *scratch)):
        own[k] = value


FACIES, BOUNDARY, SOURCE, DENSITY = range(4)
XTILES = 2 * Z0 + 3


def pack_x(own, above, below, xl, xh, lo, hi):
    for out, row in ((xl, 0), (xh, 8)):
        rows = slice(row, row + 8)
        out[:, H : H + 8] = own[:, :, rows]
        for k, at in ((FACIES, 0), (DENSITY, H)):
            out[k, 0:H] = below[at : at + H, rows]
            out[k, H + 8 : Z0] = above[at : at + H, rows]
        for k, at in ((BOUNDARY, 2 * H), (SOURCE, 3 * H - 1)):
            out[k, 1:H] = below[at : at + H - 1, rows]
            out[k, H + 8 : Z0 - 1] = above[at : at + H - 1, rows]
            out[k, 0] = out[k, Z0 - 1] = jnp.zeros((8, 128), F32)
    first = iota((8, 128), 0) < 4
    lo[XTILES - 1] = hi[XTILES - 1] = jnp.zeros((8, 128), F32)
    for z in range(Z0):
        fifth = 2 * Z0 + z // 8, slice(z % 8, z % 8 + 1)
        f, b, s, d = (xl[k, z] for k in range(4))
        lo[2 * z] = jnp.where(first, b, pltpu.roll(s, 4, 0))
        lo[2 * z + 1] = jnp.where(first, d, pltpu.roll(f, 4, 0))
        lo[fifth] = f[4:5]
        f, b, s, d = (xh[k, z] for k in range(4))
        hi[2 * z] = jnp.where(first, pltpu.roll(b, 4, 0), s)
        hi[2 * z + 1] = jnp.where(first, pltpu.roll(d, 4, 0), f)
        hi[fifth] = f[3:4]


SMALL = 7
YTILES = SMALL + 5


def block_of(k, z, tile):
    if k == FACIES:
        return SMALL + z // 4, 8 * (4 * (z % 4) + tile), 8
    layer = (k - 1) * Z0 + z
    return layer // 8, 4 * (4 * (layer % 8) + tile), 4


def pack_y(xl, xh, ml, mh, rl, rh, lo, hi):
    row, lane = iota((8, 128), 0), iota((8, 128), 1)
    for z in range(Z0):
        fifth = 2 * Z0 + z // 8, slice(z % 8, z % 8 + 1)
        bs, df = ml[2 * z], ml[2 * z + 1]
        rl[BOUNDARY, z] = bs
        rl[SOURCE, z] = pltpu.roll(bs, 4, 0)
        rl[DENSITY, z] = df
        rl[FACIES, z] = jnp.where(row == 4, ml[fifth], pltpu.roll(df, 4, 0))
        bs, df = mh[2 * z], mh[2 * z + 1]
        rh[BOUNDARY, z] = pltpu.roll(bs, 4, 0)
        rh[SOURCE, z] = bs
        rh[DENSITY, z] = pltpu.roll(df, 4, 0)
        rh[FACIES, z] = jnp.where(row == 3, mh[fifth], df)
    left, right = [None] * YTILES, [None] * YTILES
    for k in range(4):
        for z in range(Z0):
            for tile, ref in enumerate((xl, xh, rl, rh)):
                g, at, width = block_of(k, z, tile)
                v = ref[k, z]
                v = turn(v, at)
                left[g] = v if at == 0 else jnp.where(lane // width == at // width, v, left[g])
                before = (at // width - 1) % (128 // width)
                right[g] = v if at == 0 else jnp.where(lane // width == before, v, right[g])
    for g in range(YTILES):
        lo[g] = left[g]
        hi[g] = right[g]


PART = PUX, PUZ, PSINK, PB, PH = range(5)


def tile0(pos, tables, raw, first_lane, part, vs):
    row, lane = iota((32, 128), 0), iota((32, 128), 1)
    x = pos[0] * 16 + jnp.where(row < 24, row, row - 32)
    y = pos[1] * 128 + first_lane + (lane if first_lane == 0 else jnp.where(lane < 64, lane, lane - 256))
    inside = (x >= 0) & (x < 256) & (y >= 0) & (y < 512)
    for z in range(Z0):
        zg = pos[2] * 8 + z - H
        here = inside & ((zg >= 0) & (zg < 32))
        kind = raw(FACIES, z)
        h = jnp.full((32, 128), tables[0], F32)
        v = jnp.full((32, 128), tables[8], F32)
        for n in range(1, 8):
            is_n = kind == float(n)
            h = jnp.where(is_n, tables[n], h)
            v = jnp.where(is_n, tables[8 + n], v)
        part[PH, z] = jnp.where(here, h, 0.0)
        vs[z] = jnp.where(here, v, 0.0)
    for z in range(Z0 - 1):
        h, v = part[PH, z], vs[z]
        hn, vn = up(h, 0), vs[z + 1]
        hsum, vsum = h + hn, v + vn
        hsum = jnp.where(hsum > 0.0, hsum, 1.0)
        vsum = jnp.where(vsum > 0.0, vsum, 1.0)
        twice = 2.0 / (hsum * vsum)
        part[PUX, z] = (h * hn) * (twice * vsum)
        part[PUZ, z] = (v * vn) * (twice * hsum)
    for z in range(1, Z0 - 1):
        kind = raw(BOUNDARY, z)
        part[PSINK, z] = jnp.where(
            kind == 1.0, 2.0 * vs[z], jnp.where(kind == 2.0, 0.5 * part[PH, z], 0.0)
        )
        dens = raw(DENSITY, z)
        part[PB, z] = (
            raw(SOURCE, z)
            + 0.5 * part[PUZ, z] * (dens + raw(DENSITY, z + 1))
            - 0.5 * part[PUZ, z - 1] * (raw(DENSITY, z - 1) + dens)
        )


def main0(pos, tables, xl, xh, rl, rh, part, vs):
    def raw(k, z):
        return jnp.concatenate([ref[k, z] for ref in (xl, xh, rl, rh)], axis=0)

    tile0(pos, tables, raw, 0, part, vs)


def level0(pos, tables, main, yl, yh, a, packed, raw, side, vs, hs, dd, res, t, m):
    lane8 = iota((8, 128), 1)
    for k in range(4):
        for z in range(Z0):
            for tile in range(4):
                g, at, width = block_of(k, z, tile)
                both = jnp.where(lane8 // width == at // width, yl[g], yh[g])
                raw[k, z, 8 * tile : 8 * tile + 8] = turn(both, -at)
    tile0(pos, tables, lambda k, z: raw[k, z], 128, side, vs)

    def both(k, z):
        return jnp.concatenate([main[k, z], side[k, z]], axis=1)

    row, lane = iota((32, 256), 0), iota((32, 256), 1)
    odd_row, odd_lane = row % 2 == 1, lane % 2 == 1
    a[UZ, 0] = both(PUZ, 0)
    for z in range(1, Z0 - 1):
        h, sink, ux, uz, lz = both(PH, z), both(PSINK, z), both(PUX, z), both(PUZ, z), a[UZ, z - 1]
        hn = up(h, 1)
        hsum = h + hn
        uy = 2.0 * h * hn / jnp.where(hsum > 0.0, hsum, 1.0)
        a[UX, z], a[UY, z], a[UZ, z] = ux, uy, uz
        lx, ly = down(ux, 0), down(uy, 1)
        diag = sink + lz + uz + lx + ux + ly + uy
        rd = jnp.where(diag > 0.0, W / jnp.where(diag > 0.0, diag, 1.0), 0.0)
        a[RD, z] = rd
        a[C, z] = rd * both(PB, z)
        dd[z] = diag
        outer = sink + jnp.where(odd_row, ux, lx) + jnp.where(odd_lane, uy, ly)
        hs[z] = (outer + (uz if (z - H) % 2 == 1 else lz))[0:16, 0:128]

    def first(z):
        a[V, z] = smoothed(a, lambda k: a[C, k], z, z - 1, z + 1)

    each(2, Z0 - 2, first)

    def residual(z):
        v, beside = around(a, lambda k: a[V, k], z, z - 1, z + 1)
        res[z - H] = (dd[z] * (1.5 * a[C, z] - v) + beside)[0:16, 0:128]

    each(H, H + 8, residual)

    o_row = iota((16, 128), 0) % 2 == 1
    o_lane = iota((16, 128), 1) % 2 == 1

    def coarsen(z):
        lo, hi = H + 2 * z, H + 2 * z + 1

        def pair(ref):
            return ref[lo, 0:16, 0:128] + ref[hi, 0:16, 0:128]

        parts = (
            jnp.where(o_row, pair(a.at[UX]), 0.0),
            jnp.where(o_lane, pair(a.at[UY]), 0.0),
            a[UZ, hi, 0:16, 0:128],
            pair(main.at[PSINK]),
            res[2 * z] + res[2 * z + 1],
            hs[lo] + hs[hi],
        )
        for k, part in enumerate(parts):
            t[k, z] = part
        for k in range(6):
            m[k, z] = fold_rows(t.at[k, z], 8)

    each(0, 4, coarsen)
    lower = lane8 < 64
    for s in range(2):
        parts = [jnp.where(lower, fold_lanes(m[k, s]), fold_lanes(m[k, 2 + s])) for k in range(6)]
        for k in range(4):
            packed[k, s] = parts[k]
        packed[4, s] = W * parts[4] / parts[5]


def pack_y1(own, b1, b2, b3, stack, lo, hi):
    lane = iota((8, 128), 1)
    block, last = (lane % 64) // 12, ((lane + 12) % 64) // 12
    blocks = (own, b1, b2, b3)
    for g in range(8):
        left = right = None
        for at in range(5):
            k, n = divmod(5 * g + at, 8)
            v = blocks[n // 2][k, n % 2]
            stack[5 * g + at] = v
            v = turn(v, 12 * at)
            left = v if at == 0 else jnp.where(block == at, v, left)
            right = v if at == 0 else jnp.where(last == at, v, right)
        lo[g] = left
        hi[g] = right


def pack_x1(stack, right, left, full, lo, hi):
    first = iota((8, 128), 0) < 4
    full[0:40] = stack[...]
    full[40:48] = right[...]
    full[48:56] = left[...]
    for n in range(28):
        a, b = full[2 * n], pltpu.roll(full[2 * n + 1], 4, 0)
        lo[n] = jnp.where(first, a, b)
        hi[n] = jnp.where(first, b, a)


def level12(pos, full, xr, xl, xr2, xl2, a, b, sent, d1, r1, t1, m1, d2, r2, s1, s2, q2):
    gx, gy, gz = pos[0], pos[1], pos[2]
    row, lane = iota((8, 128), 0), iota((8, 128), 1)
    y = gy * 64 + jnp.where(lane < 96, lane, lane - 128)
    in_y = (y >= 0) & (y < 256)
    first = row < 4

    def middle(i):
        near, far = xr2[i // 2], xl2[i // 2]
        if i % 2 == 0:
            return jnp.where(first, near, far)
        return pltpu.roll(jnp.where(first, far, near), 4, 0)

    for tile, tiles in enumerate((full, xr, None, xl)):
        of = middle if tiles is None else lambda i, tiles=tiles: tiles[i]
        edges = [(of(40 + g), of(48 + g)) for g in range(8)]
        x = gx * 8 + jnp.where(8 * tile + row < 20, 8 * tile + row, 8 * tile + row - 32)
        inside = in_y & (x >= 0) & (x < 128)
        rows = slice(8 * tile, 8 * tile + 8)
        for k in range(5):
            for n in range(8):
                g, at = divmod(8 * k + n, 5)
                v = of(8 * k + n)
                near = jnp.where((lane % 64) // 12 == at, *edges[g])
                for part in range(2):
                    own = turn(v, 64 * part)
                    beyond = turn(near, 64 - 64 * part - 12 * at)
                    value = jnp.where(inside, jnp.where(lane < 64, own, beyond), 0.0)
                    z = 4 * (n // 2) + 2 * part + n % 2
                    a[k, z, rows] = value
                    if k == SINK:
                        s1[z, rows] = value
    pre(a, d1, None, r1, 16)

    def keep1(k, z, value):
        value = fold_lanes(value)
        if k < 4:
            b[k, z] = value
        if k == SINK:
            s2[z] = value
        if k == 4:
            q2[z] = value

    halve(a, s1, r1, t1, keep1, 16, 32)
    pre(b, d2, q2, r2, 8)

    def keep2(k, z, value):
        m1[z, 0, k : k + 1] = value[0:1]
        m1[z, 1, k : k + 1] = value[1:2]

    m1[...] = jnp.zeros((4, 2, 8, 128), F32)
    halve(b, s2, r2, t1.at[:, :, 0:16], keep2, 8, 16)
    total = jnp.zeros((8, 128), F32)
    for z in range(4):
        zg = lax.rem(z + gz, 4)
        for s in range(2):
            v = m1[z, s]
            v = pick(v + up(v, 1), 2 * (lane % 16))
            total = jnp.where(lane // 16 == 2 * zg + s, v, total)
    for k in range(5):
        sent[:, :, 128 * k : 128 * k + 128] = jnp.broadcast_to(total[k : k + 1][None], (64, 1, 128))


def sweep(a, src, dst, n, layers=None):
    for z in layers or range(n):
        dst[z % n] = smoothed(a, lambda k: src[k], z % n, (z - 1) % n, (z + 1) % n)


def solve(
    pos, got, a0, a1, a2, pressure, left,
    a3, a4, d3, d4, r3, r4, s3, s4, t3, q5, e1, e2, e3, e4, f2, g4, g3, g2, g1, g0, b3, w0,
):
    gx, gy, gz = pos[0], pos[1], pos[2]
    lane = iota((16, 128), 1)
    for k in range(5):
        rows = [got[16 * g : 16 * g + 16, 0, 128 * k : 128 * k + 128] for g in range(4)]
        for z in range(4):
            for s in range(2):
                at = (z * 2 + s) * 16
                value = turn(rows[0], -at)
                for g in range(1, 4):
                    value = jnp.where(lane // 16 == g, turn(rows[g], 16 * g - at), value)
                value = jnp.where(lane < 64, value, turn(value, 64))
                if k < 4:
                    a3[k, z, pl.ds(s, 16, stride=2), :] = value
                else:
                    r3[z, pl.ds(s, 16, stride=2), :] = value
    s3[...] = a3[SINK]
    pre(a3, d3, r3, e3, 4)

    def keep3(k, z, value):
        value = fold_lanes(value)
        if k < 4:
            a4[k, z] = value
        if k == SINK:
            s4[z] = value
        if k == 4:
            r4[z] = value

    halve(a3, s3, e3, t3, keep3, 4, 32)
    pre(a4, d4, r4, e4, 2)

    def keep4(k, z, value):
        q5[k] = fold_lanes(value)

    halve(a4, s4, e4, t3.at[:, :, 0:16], keep4, 2, 16)
    ux, uy, uz, sink, r = q5[0], q5[1], q5[2], q5[3], q5[4]
    lx, ly = down(ux, 0), down(uy, 1)
    diag = sink + uz + uz + ux + lx + uy + ly
    rd = W / diag
    c = rd * r
    ux, lx, uy, ly = rd * ux, rd * lx, rd * uy, rd * ly
    v = c
    for _ in range(COARSE_SWEEPS - 1):
        beside = (ux * up(v, 0) + lx * down(v, 0)) + (uy * up(v, 1) + ly * down(v, 1))
        v = (v * (1.0 / 3.0) + c) + beside

    e = spread_rows(g4, spread_lanes(v))
    for z in range(2):
        a4[V, z] = a4[V, z] + e
    sweep(a4, a4.at[V], e4, 2)
    sweep(a4, e4, r4, 2)
    for z in range(2):
        e = spread_rows(g3.at[z], spread_lanes(r4[z]))
        a3[V, 2 * z] = a3[V, 2 * z] + e
        a3[V, 2 * z + 1] = a3[V, 2 * z + 1] + e
    sweep(a3, a3.at[V], e3, 4)
    sweep(a3, e3, r3, 4)
    b3[:, 8:40] = r3[...]
    b3[:, 0:8] = r3[:, 24:32]
    b3[:, 40:48] = r3[:, 0:8]
    lane = iota((8, 128), 1) % 64
    index = jnp.where(lane < 40, lane // 2, lane // 2 - 32) + 16 * gy
    index = lax.rem(index + 64, 64)
    for z in range(4):
        e = b3[lax.rem(z + gz, 4), pl.ds(2 * gx + 5, 8), :]
        e = pick(pltpu.roll(e, 5, 0), index)
        e = spread_rows(g2.at[z], e)
        e2[2 * z] = a2[V, 2 * z] + e
        e2[2 * z + 1] = a2[V, 2 * z + 1] + e
    sweep(a2, e2, f2, 8)
    sweep(a2, f2, e2, 8, range(-2, 4))
    for z in range(-2, 4):
        e = spread_rows(g1.at[z % 8], spread_lanes(e2[z % 8]))
        for zf in (2 * z % 16, 2 * z % 16 + 1):
            e1[0, zf] = a1[V, zf] + e
    sweep(a1, e1.at[0], e1.at[1], 16, range(-3, 7))
    sweep(a1, e1.at[1], e1.at[0], 16, range(-2, 6))
    upper = iota((8, 128), 0) < 4
    for zc in range(-2, 6):
        v = e1[0, zc % 16]
        v = jnp.concatenate([v[0:8], jnp.where(upper, v[8:16], v[24:32])], axis=0)
        for half in range(2):
            e = spread_rows(g0.at[half, zc + 2], spread_lanes(v, 64 * half))
            lanes = slice(128 * half, 128 * half + 128)
            for z in (2 * zc, 2 * zc + 1):
                if -3 <= z <= 10:
                    w0[0, z + H, :, lanes] = a0[V, z + H, :, lanes] + e

    def sweep0(src, dst):
        def body(z):
            w0[dst, z] = smoothed(a0, lambda k: w0[src, k], z, z - 1, z + 1)

        return body

    each(3, Z0 - 3, sweep0(0, 1))
    each(4, Z0 - 4, sweep0(1, 0))

    def last(z):
        v, beside = around(a0, lambda k: w0[0, k], z, z - 1, z + 1)
        r = W / a0[RD, z] * (1.5 * a0[C, z] - v) + beside
        pressure[z - H] = v[0:16, 0:128]
        left[z - H] = r[0:16, 0:128]

    each(H, H + 8, last)


def shift(value, axis, by):
    count = lax.axis_size(axis)
    return lax.ppermute(value, axis, [((i + by) % count, i) for i in range(count)])


def local(facies, boundary, hc, vc, source, density):
    pos = jnp.stack([lax.axis_index(n) for n in ("gx", "gy", "gz")]).astype(jnp.int32)
    tables = jnp.concatenate([hc, vc])
    raw = (facies, boundary, source, density)
    landing = [
        pltpu.VMEM((8, 16, 128), jnp.int32), pltpu.VMEM((8, 16, 128), jnp.int32),
        (8, 16, 128), (8, 16, 128), pltpu.SemaphoreType.DMA((4,)),
    ]
    plan = dict(spaces=[HBM] * 4, scratch=landing, limit=60)
    lo, hi = call(pack_z, [(4 * H - 2, 16, 128)] * 2, *raw, **plan)
    above, below = shift(lo, "gz", 1), shift(hi, "gz", -1)
    (own,) = call(fetch_own, [(4, 8, 16, 128)], *raw, **{**plan, "limit": 24})
    xl, xh, lo, hi = call(
        pack_x, [(4, Z0, 8, 128)] * 2 + [(XTILES, 8, 128)] * 2, own, above, below
    )
    ml, mh = shift(lo, "gx", 1), shift(hi, "gx", -1)
    rl, rh, lo, hi = call(
        pack_y, [(4, Z0, 8, 128)] * 2 + [(YTILES, 8, 128)] * 2, xl, xh, ml, mh
    )
    yl, yh = shift(lo, "gy", 1), shift(hi, "gy", -1)
    (main,) = call(
        main0, [(5, Z0, 32, 128)], pos, tables, xl, xh, rl, rh,
        spaces=[SMEM] * 2 + [VMEM] * 4, scratch=[(Z0, 32, 128)],
    )
    a0, packed = call(
        level0,
        [(6, Z0, 32, 256), (5, 2, 8, 128)],
        pos, tables, main, yl, yh,
        spaces=[SMEM] * 2 + [VMEM] * 3,
        scratch=[
            (4, Z0, 32, 128), (5, Z0, 32, 128), (Z0, 32, 128), (Z0, 16, 128), (Z0, 32, 256),
            (8, 16, 128), (6, 4, 16, 128), (6, 4, 8, 128),
        ],
    )
    blocks = [shift(packed, "gz", n) for n in (1, 2, 3)]
    stack, lo, hi = call(pack_y1, [(40, 8, 128)] + [(8, 8, 128)] * 2, packed, *blocks)
    right, left = shift(lo, "gy", 1), shift(hi, "gy", -1)
    full, lo, hi = call(pack_x1, [(56, 8, 128)] + [(28, 8, 128)] * 2, stack, right, left)
    near = (shift(full, "gx", 1), shift(full, "gx", -1), shift(lo, "gx", 2), shift(hi, "gx", -2))
    a1, a2, sent = call(
        level12,
        [(6, 16, 32, 128), (6, 8, 16, 128), (64, 1, 640)],
        pos, full, *near,
        spaces=[SMEM] + [VMEM] * 5,
        scratch=[
            (16, 32, 128), (16, 32, 128), (5, 8, 32, 128), (4, 2, 8, 128),
            (8, 16, 128), (8, 16, 128), (16, 32, 128), (8, 16, 128), (8, 16, 128),
        ],
    )
    got = lax.all_to_all(sent, ("gy", "gx"), 0, 0)
    return tuple(
        call(
            solve,
            [(8, 16, 128), (8, 16, 128)],
            pos, got, a0, a1, a2,
            spaces=[SMEM] + [VMEM] * 4,
            scratch=[
                (6, 4, 32, 128), (6, 2, 16, 128),
                (4, 32, 128), (2, 16, 128),
                (4, 32, 128), (2, 16, 128), (4, 32, 128), (2, 16, 128),
                (5, 2, 32, 128), (5, 8, 128),
                (2, 16, 32, 128), (8, 16, 128), (4, 32, 128), (2, 16, 128), (8, 16, 128),
                (16, 128), (2, 32, 128), (4, 16, 128), (8, 32, 128), (2, 8, 32, 128),
                (4, 48, 128), (2, Z0, 32, 256),
            ],
        )
    )


def solution(mesh):
    split = P("gz", "gx", "gy")
    return jax.shard_map(
        local,
        mesh=mesh,
        in_specs=(split, split, P(), P(), split, split),
        out_specs=(split, split),
        check_vma=False,
    )
```

```python
import jax
import jax.numpy as jnp
from jax import lax
from jax.experimental import pallas as pl
from jax.experimental.pallas import tpu as pltpu
from jax.sharding import PartitionSpec as P

COARSE_SWEEPS = 8
W = 2.0 / 3.0
F32 = jnp.float32
UX, UY, UZ, RD, C, V = range(6)
SINK = RD
H = 5
Z0 = 8 + 2 * H

VMEM = pl.BlockSpec(memory_space=pltpu.VMEM)
SMEM = pl.BlockSpec(memory_space=pltpu.SMEM)
HBM = pl.BlockSpec(memory_space=pltpu.HBM)


def call(kernel, outs, *args, scratch=(), spaces=None, limit=24):
    return pl.pallas_call(
        kernel,
        out_shape=[jax.ShapeDtypeStruct(s, F32) for s in outs],
        in_specs=spaces or [VMEM] * len(args),
        out_specs=[VMEM] * len(outs),
        scratch_shapes=[pltpu.VMEM(s, F32) if isinstance(s, tuple) else s for s in scratch],
        compiler_params=pltpu.CompilerParams(vmem_limit_bytes=limit * 2**20),
    )(*args)


def iota(shape, dim):
    return lax.broadcasted_iota(jnp.int32, shape, dim)


def up(a, dim):
    return pltpu.roll(a, a.shape[dim] - 1, dim)


def down(a, dim):
    return pltpu.roll(a, 1, dim)


def turn(a, by):
    by %= 128
    return pltpu.roll(a, by, a.ndim - 1) if by else a


def pick(a, index):
    return jnp.take_along_axis(a, index, axis=1, mode="promise_in_bounds")


def fold_lanes(a):
    return pick(a + up(a, 1), (2 * iota(a.shape, 1)) % 128)


def spread_lanes(a, first=0):
    return pick(a, first + iota(a.shape, 1) // 2)


def each(start, stop, body):
    for z in range(start, stop):
        body(z)


def wrap(z, n):
    return z % n


def around(a, field, z, zm, zp):
    v = field(z)
    ux, uy = a[UX, z], a[UY, z]
    out = ux * up(v, 0) + down(ux * v, 0)
    out = out + (uy * up(v, 1) + down(uy * v, 1))
    return v, out + (a[UZ, z] * field(zp) + a[UZ, zm] * field(zm))


def smoothed(a, field, z, zm, zp):
    v, beside = around(a, field, z, zm, zp)
    return v * (1.0 / 3.0) + a[C, z] + a[RD, z] * beside


def finish(a, d, r, z, zm):
    ux, uy = a[UX, z], a[UY, z]
    diag = a[SINK, z] + a[UZ, z] + a[UZ, zm] + ux + down(ux, 0) + uy + down(uy, 1)
    d[z] = diag
    rd = jnp.where(diag > 0.0, W / jnp.where(diag > 0.0, diag, 1.0), 0.0)
    a[RD, z] = rd
    if r is not None:
        a[C, z] = rd * r[z]


def circ(n):
    return lambda z: (z, wrap(z - 1, n), wrap(z + 1, n))


def pre(a, d, r, res, n):
    c3 = circ(n)
    each(0, n, lambda z: finish(a, d, r, z, wrap(z - 1, n)))

    def one(z):
        a[V, z] = smoothed(a, lambda k: a[C, k], *c3(z))

    each(0, n, one)

    def two(z):
        v, beside = around(a, lambda k: a[V, k], *c3(z))
        res[z] = d[z] * (1.5 * a[C, z] - v) + beside

    each(0, n, two)


def halve(a, sink, r, t, store, n, rows):
    odd_row = iota((rows, 128), 0) % 2 == 1
    odd_lane = iota((rows, 128), 1) % 2 == 1

    def body(z):
        lo, hi = 2 * z, 2 * z + 1
        parts = (
            jnp.where(odd_row, a[UX, lo] + a[UX, hi], 0.0),
            jnp.where(odd_lane, a[UY, lo] + a[UY, hi], 0.0),
            a[UZ, hi],
            sink[lo] + sink[hi],
            r[lo] + r[hi],
        )
        for k, part in enumerate(parts):
            t[k, z] = part
        for k in range(5):
            store(k, z, fold_rows(t.at[k, z], rows // 2))

    each(0, n // 2, body)


def fold_rows(t, n):
    return t[pl.ds(0, n, stride=2), :] + t[pl.ds(1, n, stride=2), :]


def spread_rows(t, value):
    n = value.shape[0]
    t[pl.ds(0, n, stride=2), :] = value
    t[pl.ds(1, n, stride=2), :] = value
    return t[...]


def fetch(f, b, s, d, fi, bi, sf, df, sems):
    copies = [
        pltpu.make_async_copy(src, dst, sems.at[k])
        for k, (src, dst) in enumerate(((f, fi), (b, bi), (s, sf), (d, df)))
    ]
    for copy in copies:
        copy.start()
    for copy in copies:
        copy.wait()
    return [fi[...].astype(F32), bi[...].astype(F32), sf[...], df[...]]


def pack_z(f, b, s, d, lo, hi, *scratch):
    f, b, s, d = fetch(f, b, s, d, *scratch)
    for value, at, n in ((f, 0, H), (d, H, H), (b, 2 * H, H - 1), (s, 3 * H - 1, H - 1)):
        lo[at : at + n] = value[0:n]
        hi[at : at + n] = value[8 - n : 8]


def fetch_own(f, b, s, d, own, *scratch):
    for k, value in enumerate(fetch(f, b, s, d, *scratch)):
        own[k] = value


FACIES, BOUNDARY, SOURCE, DENSITY = range(4)
XTILES = 2 * Z0 + 3


def pack_x(own, above, below, xl, xh, lo, hi):
    for out, row in ((xl, 0), (xh, 8)):
        rows = slice(row, row + 8)
        out[:, H : H + 8] = own[:, :, rows]
        for k, at in ((FACIES, 0), (DENSITY, H)):
            out[k, 0:H] = below[at : at + H, rows]
            out[k, H + 8 : Z0] = above[at : at + H, rows]
        for k, at in ((BOUNDARY, 2 * H), (SOURCE, 3 * H - 1)):
            out[k, 1:H] = below[at : at + H - 1, rows]
            out[k, H + 8 : Z0 - 1] = above[at : at + H - 1, rows]
            out[k, 0] = out[k, Z0 - 1] = jnp.zeros((8, 128), F32)
    first = iota((8, 128), 0) < 4
    lo[XTILES - 1] = hi[XTILES - 1] = jnp.zeros((8, 128), F32)
    for z in range(Z0):
        fifth = 2 * Z0 + z // 8, slice(z % 8, z % 8 + 1)
        f, b, s, d = (xl[k, z] for k in range(4))
        lo[2 * z] = jnp.where(first, b, pltpu.roll(s, 4, 0))
        lo[2 * z + 1] = jnp.where(first, d, pltpu.roll(f, 4, 0))
        lo[fifth] = f[4:5]
        f, b, s, d = (xh[k, z] for k in range(4))
        hi[2 * z] = jnp.where(first, pltpu.roll(b, 4, 0), s)
        hi[2 * z + 1] = jnp.where(first, pltpu.roll(d, 4, 0), f)
        hi[fifth] = f[3:4]


SMALL = 7
YTILES = SMALL + 5


def block_of(k, z, tile):
    if k == FACIES:
        return SMALL + z // 4, 8 * (4 * (z % 4) + tile), 8
    layer = (k - 1) * Z0 + z
    return layer // 8, 4 * (4 * (layer % 8) + tile), 4


def pack_y(xl, xh, ml, mh, rl, rh, lo, hi):
    row, lane = iota((8, 128), 0), iota((8, 128), 1)
    for z in range(Z0):
        fifth = 2 * Z0 + z // 8, slice(z % 8, z % 8 + 1)
        bs, df = ml[2 * z], ml[2 * z + 1]
        rl[BOUNDARY, z] = bs
        rl[SOURCE, z] = pltpu.roll(bs, 4, 0)
        rl[DENSITY, z] = df
        rl[FACIES, z] = jnp.where(row == 4, ml[fifth], pltpu.roll(df, 4, 0))
        bs, df = mh[2 * z], mh[2 * z + 1]
        rh[BOUNDARY, z] = pltpu.roll(bs, 4, 0)
        rh[SOURCE, z] = bs
        rh[DENSITY, z] = pltpu.roll(df, 4, 0)
        rh[FACIES, z] = jnp.where(row == 3, mh[fifth], df)
    left, right = [None] * YTILES, [None] * YTILES
    for k in range(4):
        for z in range(Z0):
            for tile, ref in enumerate((xl, xh, rl, rh)):
                g, at, width = block_of(k, z, tile)
                v = ref[k, z]
                v = turn(v, at)
                left[g] = v if at == 0 else jnp.where(lane // width == at // width, v, left[g])
                before = (at // width - 1) % (128 // width)
                right[g] = v if at == 0 else jnp.where(lane // width == before, v, right[g])
    for g in range(YTILES):
        lo[g] = left[g]
        hi[g] = right[g]


PART = PUX, PUZ, PSINK, PB, PH = range(5)


def tile0(pos, tables, raw, first_lane, part, vs, start=0, stop=Z0):
    row, lane = iota((32, 128), 0), iota((32, 128), 1)
    x = pos[0] * 16 + jnp.where(row < 24, row, row - 32)
    y = pos[1] * 128 + first_lane + (lane if first_lane == 0 else jnp.where(lane < 64, lane, lane - 256))
    inside = (x >= 0) & (x < 256) & (y >= 0) & (y < 512)
    for z in range(start, stop):
        zg = pos[2] * 8 + z - H
        here = inside & ((zg >= 0) & (zg < 32))
        kind = raw(FACIES, z)
        h = jnp.full((32, 128), tables[0], F32)
        v = jnp.full((32, 128), tables[8], F32)
        for n in range(1, 8):
            is_n = kind == float(n)
            h = jnp.where(is_n, tables[n], h)
            v = jnp.where(is_n, tables[8 + n], v)
        part[PH, z] = jnp.where(here, h, 0.0)
        vs[z] = jnp.where(here, v, 0.0)
    for z in range(start, stop - 1):
        h, v = part[PH, z], vs[z]
        hn, vn = up(h, 0), vs[z + 1]
        hsum, vsum = h + hn, v + vn
        hsum = jnp.where(hsum > 0.0, hsum, 1.0)
        vsum = jnp.where(vsum > 0.0, vsum, 1.0)
        twice = 2.0 / (hsum * vsum)
        part[PUX, z] = (h * hn) * (twice * vsum)
        part[PUZ, z] = (v * vn) * (twice * hsum)
    for z in range(start + 1, stop - 1):
        kind = raw(BOUNDARY, z)
        part[PSINK, z] = jnp.where(
            kind == 1.0, 2.0 * vs[z], jnp.where(kind == 2.0, 0.5 * part[PH, z], 0.0)
        )
        dens = raw(DENSITY, z)
        part[PB, z] = (
            raw(SOURCE, z)
            + 0.5 * part[PUZ, z] * (dens + raw(DENSITY, z + 1))
            - 0.5 * part[PUZ, z - 1] * (raw(DENSITY, z - 1) + dens)
        )


def main0(pos, tables, xl, xh, rl, rh, part, vs):
    def raw(k, z):
        return jnp.concatenate([ref[k, z] for ref in (xl, xh, rl, rh)], axis=0)

    tile0(pos, tables, raw, 0, part, vs)


def y_sides(yl, yh, raw, layers):
    lane = iota((8, 128), 1)
    for k in range(4):
        for z in layers:
            for tile in range(4):
                g, at, width = block_of(k, z, tile)
                both = jnp.where(lane // width == at // width, yl[g], yh[g])
                raw[k, z, 8 * tile : 8 * tile + 8] = turn(both, -at)


def setup0(a, main, side, z):
    def both(k):
        return jnp.concatenate([main[k, z], side[k, z]], axis=1)

    h, sink, ux, uz, lz = both(PH), both(PSINK), both(PUX), both(PUZ), a[UZ, z - 1]
    hn = up(h, 1)
    hsum = h + hn
    uy = 2.0 * h * hn / jnp.where(hsum > 0.0, hsum, 1.0)
    a[UX, z], a[UY, z], a[UZ, z] = ux, uy, uz
    lx, ly = down(ux, 0), down(uy, 1)
    diag = sink + lz + uz + lx + ux + ly + uy
    rd = jnp.where(diag > 0.0, W / jnp.where(diag > 0.0, diag, 1.0), 0.0)
    a[RD, z] = rd
    a[C, z] = rd * both(PB)
    return diag, sink, ux, uy, uz, lx, ly, lz


def level0(pos, tables, main, yl, yh, a, packed, raw, side, vs, hs, dd, res, t, m):
    lane8 = iota((8, 128), 1)
    y_sides(yl, yh, raw, range(2, Z0 - 2))
    tile0(pos, tables, lambda k, z: raw[k, z], 128, side, vs, 2, Z0 - 2)
    row, lane = iota((32, 256), 0), iota((32, 256), 1)
    odd_row, odd_lane = row % 2 == 1, lane % 2 == 1
    a[UZ, 2] = jnp.concatenate([main[PUZ, 2], side[PUZ, 2]], axis=1)
    for z in range(3, Z0 - 3):
        diag, sink, ux, uy, uz, lx, ly, lz = setup0(a, main, side, z)
        if H <= z < H + 8:
            dd[z - H] = diag[0:16, 0:128]
            outer = sink + jnp.where(odd_row, ux, lx) + jnp.where(odd_lane, uy, ly)
            hs[z - H] = (outer + (uz if (z - H) % 2 == 1 else lz))[0:16, 0:128]

    def first(z):
        a[V, z] = smoothed(a, lambda k: a[C, k], z, z - 1, z + 1)

    each(4, Z0 - 4, first)

    def residual(z):
        v, beside = around(a, lambda k: a[V, k], z, z - 1, z + 1)
        res[z - H] = dd[z - H] * (1.5 * a[C, z] - v)[0:16, 0:128] + beside[0:16, 0:128]

    each(H, H + 8, residual)

    o_row = iota((16, 128), 0) % 2 == 1
    o_lane = iota((16, 128), 1) % 2 == 1

    def coarsen(z):
        lo, hi = H + 2 * z, H + 2 * z + 1

        def pair(ref):
            return ref[lo, 0:16, 0:128] + ref[hi, 0:16, 0:128]

        parts = (
            jnp.where(o_row, pair(a.at[UX]), 0.0),
            jnp.where(o_lane, pair(a.at[UY]), 0.0),
            a[UZ, hi, 0:16, 0:128],
            pair(main.at[PSINK]),
            res[2 * z] + res[2 * z + 1],
            hs[2 * z] + hs[2 * z + 1],
        )
        for k, part in enumerate(parts):
            t[k, z] = part
        for k in range(6):
            m[k, z] = fold_rows(t.at[k, z], 8)

    each(0, 4, coarsen)
    lower = lane8 < 64
    for s in range(2):
        parts = [jnp.where(lower, fold_lanes(m[k, s]), fold_lanes(m[k, 2 + s])) for k in range(6)]
        for k in range(4):
            packed[k, s] = parts[k]
        packed[4, s] = W * parts[4] / parts[5]


OUTER = (2, 3, Z0 - 4, Z0 - 3)


def outer0(pos, tables, main, yl, yh, a0, field, raw, side, vs, a):
    for start, stop in ((0, 4), (Z0 - 4, Z0)):
        y_sides(yl, yh, raw, range(start, stop))
        tile0(pos, tables, lambda k, z: raw[k, z], 128, side, vs, start, stop)
        a[UZ, start] = jnp.concatenate([main[PUZ, start], side[PUZ, start]], axis=1)
        for z in range(start + 1, stop - 1):
            setup0(a, main, side, z)
    for z in (3, 4, Z0 - 5, Z0 - 4):
        for k in (UX, UY, UZ, RD, C):
            a[k, z] = a0[k, z]
    for n, z in enumerate(OUTER):
        field[n] = smoothed(a, lambda k: a[C, k], z, z - 1, z + 1)


def pack_y1(own, b1, b2, b3, stack, lo, hi):
    lane = iota((8, 128), 1)
    block, last = (lane % 64) // 12, ((lane + 12) % 64) // 12
    blocks = (own, b1, b2, b3)
    for g in range(8):
        left = right = None
        for at in range(5):
            k, n = divmod(5 * g + at, 8)
            v = blocks[n // 2][k, n % 2]
            stack[5 * g + at] = v
            v = turn(v, 12 * at)
            left = v if at == 0 else jnp.where(block == at, v, left)
            right = v if at == 0 else jnp.where(last == at, v, right)
        lo[g] = left
        hi[g] = right


def pack_x1(stack, right, left, full, lo, hi):
    first = iota((8, 128), 0) < 4
    full[0:40] = stack[...]
    full[40:48] = right[...]
    full[48:56] = left[...]
    for n in range(28):
        a, b = full[2 * n], pltpu.roll(full[2 * n + 1], 4, 0)
        lo[n] = jnp.where(first, a, b)
        hi[n] = jnp.where(first, b, a)


def level12(pos, full, xr, xl, xr2, xl2, a, b, sent, d1, r1, t1, m1, d2, r2, s1, s2, q2):
    gx, gy, gz = pos[0], pos[1], pos[2]
    row, lane = iota((8, 128), 0), iota((8, 128), 1)
    y = gy * 64 + jnp.where(lane < 96, lane, lane - 128)
    in_y = (y >= 0) & (y < 256)
    first = row < 4

    def middle(i):
        near, far = xr2[i // 2], xl2[i // 2]
        if i % 2 == 0:
            return jnp.where(first, near, far)
        return pltpu.roll(jnp.where(first, far, near), 4, 0)

    for tile, tiles in enumerate((full, xr, None, xl)):
        of = middle if tiles is None else lambda i, tiles=tiles: tiles[i]
        edges = [(of(40 + g), of(48 + g)) for g in range(8)]
        x = gx * 8 + jnp.where(8 * tile + row < 20, 8 * tile + row, 8 * tile + row - 32)
        inside = in_y & (x >= 0) & (x < 128)
        rows = slice(8 * tile, 8 * tile + 8)
        for k in range(5):
            for n in range(8):
                g, at = divmod(8 * k + n, 5)
                v = of(8 * k + n)
                near = jnp.where((lane % 64) // 12 == at, *edges[g])
                for part in range(2):
                    own = turn(v, 64 * part)
                    beyond = turn(near, 64 - 64 * part - 12 * at)
                    value = jnp.where(inside, jnp.where(lane < 64, own, beyond), 0.0)
                    z = 4 * (n // 2) + 2 * part + n % 2
                    a[k, z, rows] = value
                    if k == SINK:
                        s1[z, rows] = value
    pre(a, d1, None, r1, 16)

    def keep1(k, z, value):
        value = fold_lanes(value)
        if k < 4:
            b[k, z] = value
        if k == SINK:
            s2[z] = value
        if k == 4:
            q2[z] = value

    halve(a, s1, r1, t1, keep1, 16, 32)
    pre(b, d2, q2, r2, 8)

    def keep2(k, z, value):
        m1[z, 0, k : k + 1] = value[0:1]
        m1[z, 1, k : k + 1] = value[1:2]

    m1[...] = jnp.zeros((4, 2, 8, 128), F32)
    halve(b, s2, r2, t1.at[:, :, 0:16], keep2, 8, 16)
    total = jnp.zeros((8, 128), F32)
    for z in range(4):
        zg = lax.rem(z + gz, 4)
        for s in range(2):
            v = m1[z, s]
            v = pick(v + up(v, 1), 2 * (lane % 16))
            total = jnp.where(lane // 16 == lax.rem(2 * zg + s + gy, 8), v, total)
    for tile in range(5):
        value = total
        for i in range(8):
            value = jnp.where(row == i, total[(8 * tile + i) % 5 : (8 * tile + i) % 5 + 1], value)
        for i in range(8):
            sent[40 * i + 8 * tile : 40 * i + 8 * tile + 8] = value


def sweep(a, src, dst, n, layers=None):
    for z in layers or range(n):
        dst[z % n] = smoothed(a, lambda k: src[k], z % n, (z - 1) % n, (z + 1) % n)


def solve(
    pos, got, a0, v0, a1, a2, pressure, left,
    a3, a4, d3, d4, r3, r4, s3, s4, t3, q5, e1, e2, e3, e4, f2, g4, g3, g2, g1, g0, b3, w0,
):
    gx, gy, gz = pos[0], pos[1], pos[2]
    lane = iota((16, 128), 1)
    for k in range(5):
        rows = [got[pl.ds(80 * g + k, 16, stride=5), :] for g in range(4)]
        rows = rows + [turn(value, 64) for value in rows]
        for z in range(4):
            for s in range(2):
                at = 2 * z + s
                value = rows[0]
                for g in range(1, 8):
                    value = jnp.where(lane // 16 == (at + g) % 8, rows[g], value)
                value = turn(value, -16 * at)
                if k < 4:
                    a3[k, z, pl.ds(s, 16, stride=2), :] = value
                else:
                    r3[z, pl.ds(s, 16, stride=2), :] = value
    s3[...] = a3[SINK]
    pre(a3, d3, r3, e3, 4)

    def keep3(k, z, value):
        value = fold_lanes(value)
        if k < 4:
            a4[k, z] = value
        if k == SINK:
            s4[z] = value
        if k == 4:
            r4[z] = value

    halve(a3, s3, e3, t3, keep3, 4, 32)
    pre(a4, d4, r4, e4, 2)

    def keep4(k, z, value):
        q5[k] = fold_lanes(value)

    halve(a4, s4, e4, t3.at[:, :, 0:16], keep4, 2, 16)
    ux, uy, uz, sink, r = q5[0], q5[1], q5[2], q5[3], q5[4]
    lx, ly = down(ux, 0), down(uy, 1)
    diag = sink + uz + uz + ux + lx + uy + ly
    rd = W / diag
    c = rd * r
    ux, lx, uy, ly = rd * ux, rd * lx, rd * uy, rd * ly
    v = c
    for _ in range(COARSE_SWEEPS - 1):
        beside = (ux * up(v, 0) + lx * down(v, 0)) + (uy * up(v, 1) + ly * down(v, 1))
        v = (v * (1.0 / 3.0) + c) + beside

    e = spread_rows(g4, spread_lanes(v))
    for z in range(2):
        a4[V, z] = a4[V, z] + e
    sweep(a4, a4.at[V], e4, 2)
    sweep(a4, e4, r4, 2)
    for z in range(2):
        e = spread_rows(g3.at[z], spread_lanes(r4[z]))
        a3[V, 2 * z] = a3[V, 2 * z] + e
        a3[V, 2 * z + 1] = a3[V, 2 * z + 1] + e
    sweep(a3, a3.at[V], e3, 4)
    sweep(a3, e3, r3, 4)
    b3[:, 8:40] = r3[...]
    b3[:, 0:8] = r3[:, 24:32]
    b3[:, 40:48] = r3[:, 0:8]
    lane = iota((8, 128), 1) % 64
    index = jnp.where(lane < 40, lane // 2, lane // 2 - 32) + 16 * gy
    index = lax.rem(index + 64, 64)
    for z in range(4):
        e = b3[lax.rem(z + gz, 4), pl.ds(2 * gx + 5, 8), :]
        e = pick(pltpu.roll(e, 5, 0), index)
        e = spread_rows(g2.at[z], e)
        e2[2 * z] = a2[V, 2 * z] + e
        e2[2 * z + 1] = a2[V, 2 * z + 1] + e
    sweep(a2, e2, f2, 8)
    sweep(a2, f2, e2, 8, range(-2, 4))
    for z in range(-2, 4):
        e = spread_rows(g1.at[z % 8], spread_lanes(e2[z % 8]))
        for zf in (2 * z % 16, 2 * z % 16 + 1):
            e1[0, zf] = a1[V, zf] + e
    sweep(a1, e1.at[0], e1.at[1], 16, range(-3, 7))
    sweep(a1, e1.at[1], e1.at[0], 16, range(-2, 6))
    upper = iota((8, 128), 0) < 4
    for zc in range(-2, 6):
        v = e1[0, zc % 16]
        v = jnp.concatenate([v[0:8], jnp.where(upper, v[8:16], v[24:32])], axis=0)
        for half in range(2):
            e = spread_rows(g0.at[half, zc + 2], spread_lanes(v, 64 * half))
            lanes = slice(128 * half, 128 * half + 128)
            for z in (2 * zc, 2 * zc + 1):
                if -3 <= z <= 10:
                    old = v0.at[OUTER.index(z + H)] if z + H in OUTER else a0.at[V, z + H]
                    w0[0, z + H, :, lanes] = old[:, lanes] + e

    def sweep0(src, dst):
        def body(z):
            w0[dst, z] = smoothed(a0, lambda k: w0[src, k], z, z - 1, z + 1)

        return body

    each(3, Z0 - 3, sweep0(0, 1))
    each(4, Z0 - 4, sweep0(1, 0))

    def last(z):
        v, beside = around(a0, lambda k: w0[0, k], z, z - 1, z + 1)
        r = W / a0[RD, z] * (1.5 * a0[C, z] - v) + beside
        pressure[z - H] = v[0:16, 0:128]
        left[z - H] = r[0:16, 0:128]

    each(H, H + 8, last)


def shift(value, axis, by):
    count = lax.axis_size(axis)
    return lax.ppermute(value, axis, [((i + by) % count, i) for i in range(count)])


def local(facies, boundary, hc, vc, source, density):
    pos = jnp.stack([lax.axis_index(n) for n in ("gx", "gy", "gz")]).astype(jnp.int32)
    tables = jnp.concatenate([hc, vc])
    raw = (facies, boundary, source, density)
    landing = [
        pltpu.VMEM((8, 16, 128), jnp.int32), pltpu.VMEM((8, 16, 128), jnp.int32),
        (8, 16, 128), (8, 16, 128), pltpu.SemaphoreType.DMA((4,)),
    ]
    plan = dict(spaces=[HBM] * 4, scratch=landing, limit=60)
    lo, hi = call(pack_z, [(4 * H - 2, 16, 128)] * 2, *raw, **plan)
    above, below = shift(lo, "gz", 1), shift(hi, "gz", -1)
    (own,) = call(fetch_own, [(4, 8, 16, 128)], *raw, **{**plan, "limit": 24})
    xl, xh, lo, hi = call(
        pack_x, [(4, Z0, 8, 128)] * 2 + [(XTILES, 8, 128)] * 2, own, above, below
    )
    ml, mh = shift(lo, "gx", 1), shift(hi, "gx", -1)
    rl, rh, lo, hi = call(
        pack_y, [(4, Z0, 8, 128)] * 2 + [(YTILES, 8, 128)] * 2, xl, xh, ml, mh
    )
    yl, yh = shift(lo, "gy", 1), shift(hi, "gy", -1)
    (main,) = call(
        main0, [(5, Z0, 32, 128)], pos, tables, xl, xh, rl, rh,
        spaces=[SMEM] * 2 + [VMEM] * 4, scratch=[(Z0, 32, 128)],
    )
    a0, packed = call(
        level0,
        [(6, Z0, 32, 256), (5, 2, 8, 128)],
        pos, tables, main, yl, yh,
        spaces=[SMEM] * 2 + [VMEM] * 3,
        scratch=[
            (4, Z0, 32, 128), (5, Z0, 32, 128), (Z0, 32, 128), (8, 16, 128), (8, 16, 128),
            (8, 16, 128), (6, 4, 16, 128), (6, 4, 8, 128),
        ],
    )
    (v0,) = call(
        outer0, [(4, 32, 256)], pos, tables, main, yl, yh, a0,
        spaces=[SMEM] * 2 + [VMEM] * 4,
        scratch=[(4, Z0, 32, 128), (5, Z0, 32, 128), (Z0, 32, 128), (6, Z0, 32, 256)],
    )
    blocks = [shift(packed, "gz", n) for n in (1, 2, 3)]
    stack, lo, hi = call(pack_y1, [(40, 8, 128)] + [(8, 8, 128)] * 2, packed, *blocks)
    right, left = shift(lo, "gy", 1), shift(hi, "gy", -1)
    full, lo, hi = call(pack_x1, [(56, 8, 128)] + [(28, 8, 128)] * 2, stack, right, left)
    near = (shift(full, "gx", 1), shift(full, "gx", -1), shift(lo, "gx", 2), shift(hi, "gx", -2))
    a1, a2, sent = call(
        level12,
        [(6, 16, 32, 128), (6, 8, 16, 128), (320, 128)],
        pos, full, *near,
        spaces=[SMEM] + [VMEM] * 5,
        scratch=[
            (16, 32, 128), (16, 32, 128), (5, 8, 32, 128), (4, 2, 8, 128),
            (8, 16, 128), (8, 16, 128), (16, 32, 128), (8, 16, 128), (8, 16, 128),
        ],
    )
    got = lax.all_to_all(sent.reshape(64, 1, 640), ("gy", "gx"), 0, 0).reshape(320, 128)
    return tuple(
        call(
            solve,
            [(8, 16, 128), (8, 16, 128)],
            pos, got, a0, v0, a1, a2,
            spaces=[SMEM] + [VMEM] * 5,
            scratch=[
                (6, 4, 32, 128), (6, 2, 16, 128),
                (4, 32, 128), (2, 16, 128),
                (4, 32, 128), (2, 16, 128), (4, 32, 128), (2, 16, 128),
                (5, 2, 32, 128), (5, 8, 128),
                (2, 16, 32, 128), (8, 16, 128), (4, 32, 128), (2, 16, 128), (8, 16, 128),
                (16, 128), (2, 32, 128), (4, 16, 128), (8, 32, 128), (2, 8, 32, 128),
                (4, 48, 128), (2, Z0, 32, 256),
            ],
        )
    )


def solution(mesh):
    split = P("gz", "gx", "gy")
    return jax.shard_map(
        local,
        mesh=mesh,
        in_specs=(split, split, P(), P(), split, split),
        out_specs=(split, split),
        check_vma=False,
    )
```

```python
import jax
import jax.numpy as jnp
from jax import lax
from jax.experimental import pallas as pl
from jax.experimental.pallas import tpu as pltpu
from jax.sharding import PartitionSpec as P

COARSE_SWEEPS = 8
W = 2.0 / 3.0
F32 = jnp.float32
UX, UY, UZ, RD, C, V = range(6)
SINK = RD
H = 5
Z0 = 8 + 2 * H

VMEM = pl.BlockSpec(memory_space=pltpu.VMEM)
SMEM = pl.BlockSpec(memory_space=pltpu.SMEM)
HBM = pl.BlockSpec(memory_space=pltpu.HBM)


def call(kernel, outs, *args, scratch=(), spaces=None, limit=24):
    return pl.pallas_call(
        kernel,
        out_shape=[jax.ShapeDtypeStruct(s, F32) for s in outs],
        in_specs=spaces or [VMEM] * len(args),
        out_specs=[VMEM] * len(outs),
        scratch_shapes=[pltpu.VMEM(s, F32) if isinstance(s, tuple) else s for s in scratch],
        compiler_params=pltpu.CompilerParams(vmem_limit_bytes=limit * 2**20),
    )(*args)


def iota(shape, dim):
    return lax.broadcasted_iota(jnp.int32, shape, dim)


def up(a, dim):
    return pltpu.roll(a, a.shape[dim] - 1, dim)


def down(a, dim):
    return pltpu.roll(a, 1, dim)


def turn(a, by):
    by %= 128
    return pltpu.roll(a, by, a.ndim - 1) if by else a


def pick(a, index):
    return jnp.take_along_axis(a, index, axis=1, mode="promise_in_bounds")


def fold_lanes(a):
    return pick(a + up(a, 1), (2 * iota(a.shape, 1)) % 128)


def spread_lanes(a, first=0):
    return pick(a, first + iota(a.shape, 1) // 2)


def each(start, stop, body):
    for z in range(start, stop):
        body(z)


def wrap(z, n):
    return z % n


def around(a, field, z, zm, zp):
    v = field(z)
    ux, uy = a[UX, z], a[UY, z]
    out = ux * up(v, 0) + down(ux * v, 0)
    out = out + (uy * up(v, 1) + down(uy * v, 1))
    return v, out + (a[UZ, z] * field(zp) + a[UZ, zm] * field(zm))


def smoothed(a, field, z, zm, zp):
    v, beside = around(a, field, z, zm, zp)
    return v * (1.0 / 3.0) + a[C, z] + a[RD, z] * beside


def finish(a, d, r, z, zm):
    ux, uy = a[UX, z], a[UY, z]
    diag = a[SINK, z] + a[UZ, z] + a[UZ, zm] + ux + down(ux, 0) + uy + down(uy, 1)
    d[z] = diag
    rd = jnp.where(diag > 0.0, W / jnp.where(diag > 0.0, diag, 1.0), 0.0)
    a[RD, z] = rd
    if r is not None:
        a[C, z] = rd * r[z]


def circ(n):
    return lambda z: (z, wrap(z - 1, n), wrap(z + 1, n))


def pre(a, d, r, res, n):
    c3 = circ(n)
    each(0, n, lambda z: finish(a, d, r, z, wrap(z - 1, n)))

    def one(z):
        a[V, z] = smoothed(a, lambda k: a[C, k], *c3(z))

    each(0, n, one)

    def two(z):
        v, beside = around(a, lambda k: a[V, k], *c3(z))
        res[z] = d[z] * (1.5 * a[C, z] - v) + beside

    each(0, n, two)


def halve(a, sink, r, t, store, n, rows):
    odd_row = iota((rows, 128), 0) % 2 == 1
    odd_lane = iota((rows, 128), 1) % 2 == 1

    def body(z):
        lo, hi = 2 * z, 2 * z + 1
        parts = (
            jnp.where(odd_row, a[UX, lo] + a[UX, hi], 0.0),
            jnp.where(odd_lane, a[UY, lo] + a[UY, hi], 0.0),
            a[UZ, hi],
            sink[lo] + sink[hi],
            r[lo] + r[hi],
        )
        for k, part in enumerate(parts):
            t[k, z] = part
        for k in range(5):
            store(k, z, fold_rows(t.at[k, z], rows // 2))

    each(0, n // 2, body)


def fold_rows(t, n):
    return t[pl.ds(0, n, stride=2), :] + t[pl.ds(1, n, stride=2), :]


def spread_rows(t, value):
    n = value.shape[0]
    t[pl.ds(0, n, stride=2), :] = value
    t[pl.ds(1, n, stride=2), :] = value
    return t[...]


def fetch(f, b, s, d, fi, bi, sf, df, sems):
    copies = [
        pltpu.make_async_copy(src, dst, sems.at[k])
        for k, (src, dst) in enumerate(((f, fi), (b, bi), (s, sf), (d, df)))
    ]
    for copy in copies:
        copy.start()
    for copy in copies:
        copy.wait()
    return [fi[...].astype(F32), bi[...].astype(F32), sf[...], df[...]]


def pack_z(f, b, s, d, lo, hi, *scratch):
    f, b, s, d = fetch(f, b, s, d, *scratch)
    for value, at, n in ((f, 0, H), (d, H, H), (b, 2 * H, H - 1), (s, 3 * H - 1, H - 1)):
        lo[at : at + n] = value[0:n]
        hi[at : at + n] = value[8 - n : 8]


def fetch_own(f, b, s, d, own, *scratch):
    for k, value in enumerate(fetch(f, b, s, d, *scratch)):
        own[k] = value


FACIES, BOUNDARY, SOURCE, DENSITY = range(4)
XTILES = 2 * Z0 + 3


def pack_x(own, above, below, xl, xh, lo, hi):
    for out, row in ((xl, 0), (xh, 8)):
        rows = slice(row, row + 8)
        out[:, H : H + 8] = own[:, :, rows]
        for k, at in ((FACIES, 0), (DENSITY, H)):
            out[k, 0:H] = below[at : at + H, rows]
            out[k, H + 8 : Z0] = above[at : at + H, rows]
        for k, at in ((BOUNDARY, 2 * H), (SOURCE, 3 * H - 1)):
            out[k, 1:H] = below[at : at + H - 1, rows]
            out[k, H + 8 : Z0 - 1] = above[at : at + H - 1, rows]
            out[k, 0] = out[k, Z0 - 1] = jnp.zeros((8, 128), F32)
    first = iota((8, 128), 0) < 4
    lo[XTILES - 1] = hi[XTILES - 1] = jnp.zeros((8, 128), F32)
    for z in range(Z0):
        fifth = 2 * Z0 + z // 8, slice(z % 8, z % 8 + 1)
        f, b, s, d = (xl[k, z] for k in range(4))
        lo[2 * z] = jnp.where(first, b, pltpu.roll(s, 4, 0))
        lo[2 * z + 1] = jnp.where(first, d, pltpu.roll(f, 4, 0))
        lo[fifth] = f[4:5]
        f, b, s, d = (xh[k, z] for k in range(4))
        hi[2 * z] = jnp.where(first, pltpu.roll(b, 4, 0), s)
        hi[2 * z + 1] = jnp.where(first, pltpu.roll(d, 4, 0), f)
        hi[fifth] = f[3:4]


SMALL = 7
YTILES = SMALL + 5


def block_of(k, z, tile):
    if k == FACIES:
        return SMALL + z // 4, 8 * (4 * (z % 4) + tile), 8
    layer = (k - 1) * Z0 + z
    return layer // 8, 4 * (4 * (layer % 8) + tile), 4


def pack_y(xl, xh, ml, mh, rl, rh, lo, hi):
    row, lane = iota((8, 128), 0), iota((8, 128), 1)
    for z in range(Z0):
        fifth = 2 * Z0 + z // 8, slice(z % 8, z % 8 + 1)
        bs, df = ml[2 * z], ml[2 * z + 1]
        rl[BOUNDARY, z] = bs
        rl[SOURCE, z] = pltpu.roll(bs, 4, 0)
        rl[DENSITY, z] = df
        rl[FACIES, z] = jnp.where(row == 4, ml[fifth], pltpu.roll(df, 4, 0))
        bs, df = mh[2 * z], mh[2 * z + 1]
        rh[BOUNDARY, z] = pltpu.roll(bs, 4, 0)
        rh[SOURCE, z] = bs
        rh[DENSITY, z] = pltpu.roll(df, 4, 0)
        rh[FACIES, z] = jnp.where(row == 3, mh[fifth], df)
    left, right = [None] * YTILES, [None] * YTILES
    for k in range(4):
        for z in range(Z0):
            for tile, ref in enumerate((xl, xh, rl, rh)):
                g, at, width = block_of(k, z, tile)
                v = ref[k, z]
                v = turn(v, at)
                left[g] = v if at == 0 else jnp.where(lane // width == at // width, v, left[g])
                before = (at // width - 1) % (128 // width)
                right[g] = v if at == 0 else jnp.where(lane // width == before, v, right[g])
    for g in range(YTILES):
        lo[g] = left[g]
        hi[g] = right[g]


PART = PUX, PUZ, PSINK, PB, PH = range(5)


def tile0(pos, tables, raw, first_lane, part, vs, start=0, stop=Z0):
    row, lane = iota((32, 128), 0), iota((32, 128), 1)
    x = pos[0] * 16 + jnp.where(row < 24, row, row - 32)
    y = pos[1] * 128 + first_lane + (lane if first_lane == 0 else jnp.where(lane < 64, lane, lane - 256))
    inside = (x >= 0) & (x < 256) & (y >= 0) & (y < 512)
    for z in range(start, stop):
        zg = pos[2] * 8 + z - H
        here = inside & ((zg >= 0) & (zg < 32))
        kind = raw(FACIES, z)
        h = jnp.full((32, 128), tables[0], F32)
        v = jnp.full((32, 128), tables[8], F32)
        for n in range(1, 8):
            is_n = kind == float(n)
            h = jnp.where(is_n, tables[n], h)
            v = jnp.where(is_n, tables[8 + n], v)
        part[PH, z] = jnp.where(here, h, 0.0)
        vs[z] = jnp.where(here, v, 0.0)
    for z in range(start, stop - 1):
        h, v = part[PH, z], vs[z]
        hn, vn = up(h, 0), vs[z + 1]
        hsum, vsum = h + hn, v + vn
        hsum = jnp.where(hsum > 0.0, hsum, 1.0)
        vsum = jnp.where(vsum > 0.0, vsum, 1.0)
        twice = 2.0 / (hsum * vsum)
        part[PUX, z] = (h * hn) * (twice * vsum)
        part[PUZ, z] = (v * vn) * (twice * hsum)
    for z in range(start + 1, stop - 1):
        kind = raw(BOUNDARY, z)
        part[PSINK, z] = jnp.where(
            kind == 1.0, 2.0 * vs[z], jnp.where(kind == 2.0, 0.5 * part[PH, z], 0.0)
        )
        dens = raw(DENSITY, z)
        part[PB, z] = (
            raw(SOURCE, z)
            + 0.5 * part[PUZ, z] * (dens + raw(DENSITY, z + 1))
            - 0.5 * part[PUZ, z - 1] * (raw(DENSITY, z - 1) + dens)
        )


def main0(pos, tables, xl, xh, rl, rh, part, vs):
    def raw(k, z):
        return jnp.concatenate([ref[k, z] for ref in (xl, xh, rl, rh)], axis=0)

    tile0(pos, tables, raw, 0, part, vs)


def y_sides(yl, yh, raw, layers):
    lane = iota((8, 128), 1)
    for k in range(4):
        for z in layers:
            for tile in range(4):
                g, at, width = block_of(k, z, tile)
                both = jnp.where(lane // width == at // width, yl[g], yh[g])
                raw[k, z, 8 * tile : 8 * tile + 8] = turn(both, -at)


def setup0(a, main, side, z):
    def both(k):
        return jnp.concatenate([main[k, z], side[k, z]], axis=1)

    h, sink, ux, uz, lz = both(PH), both(PSINK), both(PUX), both(PUZ), a[UZ, z - 1]
    hn = up(h, 1)
    hsum = h + hn
    uy = 2.0 * h * hn / jnp.where(hsum > 0.0, hsum, 1.0)
    a[UX, z], a[UY, z], a[UZ, z] = ux, uy, uz
    lx, ly = down(ux, 0), down(uy, 1)
    diag = sink + lz + uz + lx + ux + ly + uy
    rd = jnp.where(diag > 0.0, W / jnp.where(diag > 0.0, diag, 1.0), 0.0)
    a[RD, z] = rd
    a[C, z] = rd * both(PB)
    return diag, sink, ux, uy, uz, lx, ly, lz


def level0(pos, tables, main, yl, yh, a, packed, raw, side, vs, hs, dd, res, t, m):
    lane8 = iota((8, 128), 1)
    y_sides(yl, yh, raw, range(2, Z0 - 2))
    tile0(pos, tables, lambda k, z: raw[k, z], 128, side, vs, 2, Z0 - 2)
    row, lane = iota((32, 256), 0), iota((32, 256), 1)
    odd_row, odd_lane = row % 2 == 1, lane % 2 == 1
    a[UZ, 2] = jnp.concatenate([main[PUZ, 2], side[PUZ, 2]], axis=1)
    for z in range(3, Z0 - 3):
        diag, sink, ux, uy, uz, lx, ly, lz = setup0(a, main, side, z)
        if H <= z < H + 8:
            dd[z - H] = diag[0:16, 0:128]
            outer = sink + jnp.where(odd_row, ux, lx) + jnp.where(odd_lane, uy, ly)
            hs[z - H] = (outer + (uz if (z - H) % 2 == 1 else lz))[0:16, 0:128]

    def first(z):
        a[V, z] = smoothed(a, lambda k: a[C, k], z, z - 1, z + 1)

    each(4, Z0 - 4, first)

    def residual(z):
        v, beside = around(a, lambda k: a[V, k], z, z - 1, z + 1)
        res[z - H] = dd[z - H] * (1.5 * a[C, z] - v)[0:16, 0:128] + beside[0:16, 0:128]

    each(H, H + 8, residual)

    o_row = iota((16, 128), 0) % 2 == 1
    o_lane = iota((16, 128), 1) % 2 == 1

    def coarsen(z):
        lo, hi = H + 2 * z, H + 2 * z + 1

        def pair(ref):
            return ref[lo, 0:16, 0:128] + ref[hi, 0:16, 0:128]

        parts = (
            jnp.where(o_row, pair(a.at[UX]), 0.0),
            jnp.where(o_lane, pair(a.at[UY]), 0.0),
            a[UZ, hi, 0:16, 0:128],
            pair(main.at[PSINK]),
            res[2 * z] + res[2 * z + 1],
            hs[2 * z] + hs[2 * z + 1],
        )
        for k, part in enumerate(parts):
            t[k, z] = part
        for k in range(6):
            m[k, z] = fold_rows(t.at[k, z], 8)

    each(0, 4, coarsen)
    lower = lane8 < 64
    for s in range(2):
        parts = [jnp.where(lower, fold_lanes(m[k, s]), fold_lanes(m[k, 2 + s])) for k in range(6)]
        for k in range(4):
            packed[k, s] = parts[k]
        packed[4, s] = W * parts[4] / parts[5]


OUTER = (2, 3, Z0 - 4, Z0 - 3)


def outer0(pos, tables, main, yl, yh, a0, field, raw, side, vs, a):
    for start, stop in ((0, 4), (Z0 - 4, Z0)):
        y_sides(yl, yh, raw, range(start, stop))
        tile0(pos, tables, lambda k, z: raw[k, z], 128, side, vs, start, stop)
        a[UZ, start] = jnp.concatenate([main[PUZ, start], side[PUZ, start]], axis=1)
        for z in range(start + 1, stop - 1):
            setup0(a, main, side, z)
    for z in (3, 4, Z0 - 5, Z0 - 4):
        for k in (UX, UY, UZ, RD, C):
            a[k, z] = a0[k, z]
    for n, z in enumerate(OUTER):
        field[n] = smoothed(a, lambda k: a[C, k], z, z - 1, z + 1)


def pack_y1(own, b1, b2, b3, stack, lo, hi):
    lane = iota((8, 128), 1)
    block, last = (lane % 64) // 12, ((lane + 12) % 64) // 12
    blocks = (own, b1, b2, b3)
    for g in range(8):
        left = right = None
        for at in range(5):
            k, n = divmod(5 * g + at, 8)
            v = blocks[n // 2][k, n % 2]
            stack[5 * g + at] = v
            v = turn(v, 12 * at)
            left = v if at == 0 else jnp.where(block == at, v, left)
            right = v if at == 0 else jnp.where(last == at, v, right)
        lo[g] = left
        hi[g] = right


def pack_x1(stack, right, left, full, lo, hi):
    first = iota((8, 128), 0) < 4
    full[0:40] = stack[...]
    full[40:48] = right[...]
    full[48:56] = left[...]
    for n in range(28):
        a, b = full[2 * n], pltpu.roll(full[2 * n + 1], 4, 0)
        lo[n] = jnp.where(first, a, b)
        hi[n] = jnp.where(first, b, a)


def level12(pos, full, xr, xl, xr2, xl2, before, a, b, sent, d1, r1, t1, m1, d2, r2, s1, s2, q2):
    gx, gy, gz = pos[0], pos[1], pos[2]
    row, lane = iota((8, 128), 0), iota((8, 128), 1)
    y = gy * 64 + jnp.where(lane < 96, lane, lane - 128)
    in_y = (y >= 0) & (y < 256)
    first = row < 4

    def middle(i):
        near, far = xr2[i // 2], xl2[i // 2]
        if i % 2 == 0:
            return jnp.where(first, near, far)
        return pltpu.roll(jnp.where(first, far, near), 4, 0)

    for tile, tiles in enumerate((full, xr, None, xl)):
        of = middle if tiles is None else lambda i, tiles=tiles: tiles[i]
        edges = [(of(40 + g), of(48 + g)) for g in range(8)]
        x = gx * 8 + jnp.where(8 * tile + row < 20, 8 * tile + row, 8 * tile + row - 32)
        inside = in_y & (x >= 0) & (x < 128)
        rows = slice(8 * tile, 8 * tile + 8)
        for k in range(5):
            for n in range(8):
                g, at = divmod(8 * k + n, 5)
                v = of(8 * k + n)
                near = jnp.where((lane % 64) // 12 == at, *edges[g])
                for part in range(2):
                    own = turn(v, 64 * part)
                    beyond = turn(near, 64 - 64 * part - 12 * at)
                    value = jnp.where(inside, jnp.where(lane < 64, own, beyond), 0.0)
                    z = 4 * (n // 2) + 2 * part + n % 2
                    a[k, z, rows] = value
                    if k == SINK:
                        s1[z, rows] = value
    pre(a, d1, None, r1, 16)

    def keep1(k, z, value):
        value = fold_lanes(value)
        if k < 4:
            b[k, z] = value
        if k == SINK:
            s2[z] = value
        if k == 4:
            q2[z] = value

    halve(a, s1, r1, t1, keep1, 16, 32)
    pre(b, d2, q2, r2, 8)

    def keep2(k, z, value):
        m1[z, 0, k : k + 1] = value[0:1]
        m1[z, 1, k : k + 1] = value[1:2]

    m1[...] = jnp.zeros((4, 2, 8, 128), F32)
    halve(b, s2, r2, t1.at[:, :, 0:16], keep2, 8, 16)
    total = jnp.zeros((8, 128), F32)
    for z in range(4):
        zg = lax.rem(z + gz, 4)
        for s in range(2):
            v = m1[z, s]
            v = pick(v + up(v, 1), 2 * (lane % 16))
            total = jnp.where(lane // 16 == lax.rem(2 * zg + s + gy, 8), v, total)
    for tile in range(5):
        value = total
        for i in range(8):
            value = jnp.where(row == i, total[(8 * tile + i) % 5 : (8 * tile + i) % 5 + 1], value)
        for i in range(8):
            sent[40 * i + 8 * tile : 40 * i + 8 * tile + 8] = value


def sweep(a, src, dst, n, layers=None):
    for z in layers or range(n):
        dst[z % n] = smoothed(a, lambda k: src[k], z % n, (z - 1) % n, (z + 1) % n)


def solve(
    pos, got, a0, v0, a1, a2, pressure, left,
    a3, a4, d3, d4, r3, r4, s3, s4, t3, q5, e1, e2, e3, e4, f2, g4, g3, g2, g1, g0, b3, w0,
):
    gx, gy, gz = pos[0], pos[1], pos[2]
    lane = iota((16, 128), 1)
    for k in range(5):
        rows = [got[pl.ds(80 * g + k, 16, stride=5), :] for g in range(4)]
        rows = rows + [turn(value, 64) for value in rows]
        for z in range(4):
            for s in range(2):
                at = 2 * z + s
                value = rows[0]
                for g in range(1, 8):
                    value = jnp.where(lane // 16 == (at + g) % 8, rows[g], value)
                value = turn(value, -16 * at)
                if k < 4:
                    a3[k, z, pl.ds(s, 16, stride=2), :] = value
                else:
                    r3[z, pl.ds(s, 16, stride=2), :] = value
    s3[...] = a3[SINK]
    pre(a3, d3, r3, e3, 4)

    def keep3(k, z, value):
        value = fold_lanes(value)
        if k < 4:
            a4[k, z] = value
        if k == SINK:
            s4[z] = value
        if k == 4:
            r4[z] = value

    halve(a3, s3, e3, t3, keep3, 4, 32)
    pre(a4, d4, r4, e4, 2)

    def keep4(k, z, value):
        q5[k] = fold_lanes(value)

    halve(a4, s4, e4, t3.at[:, :, 0:16], keep4, 2, 16)
    ux, uy, uz, sink, r = q5[0], q5[1], q5[2], q5[3], q5[4]
    lx, ly = down(ux, 0), down(uy, 1)
    diag = sink + uz + uz + ux + lx + uy + ly
    rd = W / diag
    c = rd * r
    ux, lx, uy, ly = rd * ux, rd * lx, rd * uy, rd * ly
    v = c
    for _ in range(COARSE_SWEEPS - 1):
        beside = (ux * up(v, 0) + lx * down(v, 0)) + (uy * up(v, 1) + ly * down(v, 1))
        v = (v * (1.0 / 3.0) + c) + beside

    e = spread_rows(g4, spread_lanes(v))
    for z in range(2):
        a4[V, z] = a4[V, z] + e
    sweep(a4, a4.at[V], e4, 2)
    sweep(a4, e4, r4, 2)
    for z in range(2):
        e = spread_rows(g3.at[z], spread_lanes(r4[z]))
        a3[V, 2 * z] = a3[V, 2 * z] + e
        a3[V, 2 * z + 1] = a3[V, 2 * z + 1] + e
    sweep(a3, a3.at[V], e3, 4)
    sweep(a3, e3, r3, 4)
    b3[:, 8:40] = r3[...]
    b3[:, 0:8] = r3[:, 24:32]
    b3[:, 40:48] = r3[:, 0:8]
    lane = iota((8, 128), 1) % 64
    index = jnp.where(lane < 40, lane // 2, lane // 2 - 32) + 16 * gy
    index = lax.rem(index + 64, 64)
    for z in range(4):
        e = b3[lax.rem(z + gz, 4), pl.ds(2 * gx + 5, 8), :]
        e = pick(pltpu.roll(e, 5, 0), index)
        e = spread_rows(g2.at[z], e)
        e2[2 * z] = a2[V, 2 * z] + e
        e2[2 * z + 1] = a2[V, 2 * z + 1] + e
    sweep(a2, e2, f2, 8)
    sweep(a2, f2, e2, 8, range(-2, 4))
    for z in range(-2, 4):
        e = spread_rows(g1.at[z % 8], spread_lanes(e2[z % 8]))
        for zf in (2 * z % 16, 2 * z % 16 + 1):
            e1[0, zf] = a1[V, zf] + e
    sweep(a1, e1.at[0], e1.at[1], 16, range(-3, 7))
    sweep(a1, e1.at[1], e1.at[0], 16, range(-2, 6))
    upper = iota((8, 128), 0) < 4
    for zc in range(-2, 6):
        v = e1[0, zc % 16]
        v = jnp.concatenate([v[0:8], jnp.where(upper, v[8:16], v[24:32])], axis=0)
        for half in range(2):
            e = spread_rows(g0.at[half, zc + 2], spread_lanes(v, 64 * half))
            lanes = slice(128 * half, 128 * half + 128)
            for z in (2 * zc, 2 * zc + 1):
                if -3 <= z <= 10:
                    old = v0.at[OUTER.index(z + H)] if z + H in OUTER else a0.at[V, z + H]
                    w0[0, z + H, :, lanes] = old[:, lanes] + e

    def sweep0(src, dst):
        def body(z):
            w0[dst, z] = smoothed(a0, lambda k: w0[src, k], z, z - 1, z + 1)

        return body

    each(3, Z0 - 3, sweep0(0, 1))
    each(4, Z0 - 4, sweep0(1, 0))

    def last(z):
        v, beside = around(a0, lambda k: w0[0, k], z, z - 1, z + 1)
        r = W / a0[RD, z] * (1.5 * a0[C, z] - v) + beside
        pressure[z - H] = v[0:16, 0:128]
        left[z - H] = r[0:16, 0:128]

    each(H, H + 8, last)


def shift(value, axis, by):
    count = lax.axis_size(axis)
    return lax.ppermute(value, axis, [((i + by) % count, i) for i in range(count)])


def local(facies, boundary, hc, vc, source, density):
    pos = jnp.stack([lax.axis_index(n) for n in ("gx", "gy", "gz")]).astype(jnp.int32)
    tables = jnp.concatenate([hc, vc])
    raw = (facies, boundary, source, density)
    landing = [
        pltpu.VMEM((8, 16, 128), jnp.int32), pltpu.VMEM((8, 16, 128), jnp.int32),
        (8, 16, 128), (8, 16, 128), pltpu.SemaphoreType.DMA((4,)),
    ]
    plan = dict(spaces=[HBM] * 4, scratch=landing, limit=60)
    lo, hi = call(pack_z, [(4 * H - 2, 16, 128)] * 2, *raw, **plan)
    above, below = shift(lo, "gz", 1), shift(hi, "gz", -1)
    (own,) = call(fetch_own, [(4, 8, 16, 128)], *raw, **{**plan, "limit": 24})
    xl, xh, lo, hi = call(
        pack_x, [(4, Z0, 8, 128)] * 2 + [(XTILES, 8, 128)] * 2, own, above, below
    )
    ml, mh = shift(lo, "gx", 1), shift(hi, "gx", -1)
    rl, rh, lo, hi = call(
        pack_y, [(4, Z0, 8, 128)] * 2 + [(YTILES, 8, 128)] * 2, xl, xh, ml, mh
    )
    yl, yh = shift(lo, "gy", 1), shift(hi, "gy", -1)
    (main,) = call(
        main0, [(5, Z0, 32, 128)], pos, tables, xl, xh, rl, rh,
        spaces=[SMEM] * 2 + [VMEM] * 4, scratch=[(Z0, 32, 128)],
    )
    a0, packed = call(
        level0,
        [(6, Z0, 32, 256), (5, 2, 8, 128)],
        pos, tables, main, yl, yh,
        spaces=[SMEM] * 2 + [VMEM] * 3,
        scratch=[
            (4, Z0, 32, 128), (5, Z0, 32, 128), (Z0, 32, 128), (8, 16, 128), (8, 16, 128),
            (8, 16, 128), (6, 4, 16, 128), (6, 4, 8, 128),
        ],
    )
    (v0,) = call(
        outer0, [(4, 32, 256)], pos, tables, main, yl, yh, a0,
        spaces=[SMEM] * 2 + [VMEM] * 4,
        scratch=[(4, Z0, 32, 128), (5, Z0, 32, 128), (Z0, 32, 128), (6, Z0, 32, 256)],
    )
    blocks = [shift(packed, "gz", n) for n in (1, 2, 3)]
    stack, lo, hi = call(pack_y1, [(40, 8, 128)] + [(8, 8, 128)] * 2, packed, *blocks)
    right, left = shift(lo, "gy", 1), shift(hi, "gy", -1)
    full, lo, hi = call(pack_x1, [(56, 8, 128)] + [(28, 8, 128)] * 2, stack, right, left)
    near = (shift(full, "gx", 1), shift(full, "gx", -1), shift(lo, "gx", 2), shift(hi, "gx", -2))
    a1, a2, sent = call(
        level12,
        [(6, 16, 32, 128), (6, 8, 16, 128), (320, 128)],
        pos, full, *near, v0,
        spaces=[SMEM] + [VMEM] * 6,
        scratch=[
            (16, 32, 128), (16, 32, 128), (5, 8, 32, 128), (4, 2, 8, 128),
            (8, 16, 128), (8, 16, 128), (16, 32, 128), (8, 16, 128), (8, 16, 128),
        ],
    )
    got = lax.all_to_all(sent.reshape(64, 1, 640), ("gy", "gx"), 0, 0).reshape(320, 128)
    return tuple(
        call(
            solve,
            [(8, 16, 128), (8, 16, 128)],
            pos, got, a0, v0, a1, a2,
            spaces=[SMEM] + [VMEM] * 5,
            scratch=[
                (6, 4, 32, 128), (6, 2, 16, 128),
                (4, 32, 128), (2, 16, 128),
                (4, 32, 128), (2, 16, 128), (4, 32, 128), (2, 16, 128),
                (5, 2, 32, 128), (5, 8, 128),
                (2, 16, 32, 128), (8, 16, 128), (4, 32, 128), (2, 16, 128), (8, 16, 128),
                (16, 128), (2, 32, 128), (4, 16, 128), (8, 32, 128), (2, 8, 32, 128),
                (4, 48, 128), (2, Z0, 32, 256),
            ],
        )
    )


def solution(mesh):
    split = P("gz", "gx", "gy")
    return jax.shard_map(
        local,
        mesh=mesh,
        in_specs=(split, split, P(), P(), split, split),
        out_specs=(split, split),
        check_vma=False,
    )
```

```python
import jax
import jax.numpy as jnp
from jax import lax
from jax.experimental import pallas as pl
from jax.experimental.pallas import tpu as pltpu
from jax.sharding import PartitionSpec as P

COARSE_SWEEPS = 8
W = 2.0 / 3.0
F32 = jnp.float32
UX, UY, UZ, RD, C, V = range(6)
SINK = RD
H = 5
Z0 = 8 + 2 * H

VMEM = pl.BlockSpec(memory_space=pltpu.VMEM)
SMEM = pl.BlockSpec(memory_space=pltpu.SMEM)
HBM = pl.BlockSpec(memory_space=pltpu.HBM)


def call(kernel, outs, *args, scratch=(), spaces=None, limit=24, pin=False):
    return pl.pallas_call(
        kernel,
        out_shape=[(pltpu.VMEM if pin else jax.ShapeDtypeStruct)(s, F32) for s in outs],
        in_specs=spaces or [VMEM] * len(args),
        out_specs=[VMEM] * len(outs),
        scratch_shapes=[pltpu.VMEM(s, F32) if isinstance(s, tuple) else s for s in scratch],
        compiler_params=pltpu.CompilerParams(vmem_limit_bytes=limit * 2**20),
    )(*args)


def iota(shape, dim):
    return lax.broadcasted_iota(jnp.int32, shape, dim)


def up(a, dim):
    return pltpu.roll(a, a.shape[dim] - 1, dim)


def down(a, dim):
    return pltpu.roll(a, 1, dim)


def turn(a, by):
    by %= 128
    return pltpu.roll(a, by, a.ndim - 1) if by else a


def pick(a, index):
    return jnp.take_along_axis(a, index, axis=1, mode="promise_in_bounds")


def fold_lanes(a):
    return pick(a + up(a, 1), (2 * iota(a.shape, 1)) % 128)


def spread_lanes(a, first=0):
    return pick(a, first + iota(a.shape, 1) // 2)


def each(start, stop, body):
    for z in range(start, stop):
        body(z)


def wrap(z, n):
    return z % n


def around(a, field, z, zm, zp):
    v = field(z)
    ux, uy = a[UX, z], a[UY, z]
    out = ux * up(v, 0) + down(ux * v, 0)
    out = out + (uy * up(v, 1) + down(uy * v, 1))
    return v, out + (a[UZ, z] * field(zp) + a[UZ, zm] * field(zm))


def smoothed(a, field, z, zm, zp):
    v, beside = around(a, field, z, zm, zp)
    return v * (1.0 / 3.0) + a[C, z] + a[RD, z] * beside


def finish(a, d, r, z, zm):
    ux, uy = a[UX, z], a[UY, z]
    diag = a[SINK, z] + a[UZ, z] + a[UZ, zm] + ux + down(ux, 0) + uy + down(uy, 1)
    d[z] = diag
    rd = jnp.where(diag > 0.0, W / jnp.where(diag > 0.0, diag, 1.0), 0.0)
    a[RD, z] = rd
    if r is not None:
        a[C, z] = rd * r[z]


def circ(n):
    return lambda z: (z, wrap(z - 1, n), wrap(z + 1, n))


def pre(a, d, r, res, n):
    c3 = circ(n)
    each(0, n, lambda z: finish(a, d, r, z, wrap(z - 1, n)))

    def one(z):
        a[V, z] = smoothed(a, lambda k: a[C, k], *c3(z))

    each(0, n, one)

    def two(z):
        v, beside = around(a, lambda k: a[V, k], *c3(z))
        res[z] = d[z] * (1.5 * a[C, z] - v) + beside

    each(0, n, two)


def halve(a, sink, r, t, store, n, rows):
    odd_row = iota((rows, 128), 0) % 2 == 1
    odd_lane = iota((rows, 128), 1) % 2 == 1

    def body(z):
        lo, hi = 2 * z, 2 * z + 1
        parts = (
            jnp.where(odd_row, a[UX, lo] + a[UX, hi], 0.0),
            jnp.where(odd_lane, a[UY, lo] + a[UY, hi], 0.0),
            a[UZ, hi],
            sink[lo] + sink[hi],
            r[lo] + r[hi],
        )
        for k, part in enumerate(parts):
            t[k, z] = part
        for k in range(5):
            store(k, z, fold_rows(t.at[k, z], rows // 2))

    each(0, n // 2, body)


def fold_rows(t, n):
    return t[pl.ds(0, n, stride=2), :] + t[pl.ds(1, n, stride=2), :]


def spread_rows(t, value):
    n = value.shape[0]
    t[pl.ds(0, n, stride=2), :] = value
    t[pl.ds(1, n, stride=2), :] = value
    return t[...]


def pack_z(f, b, s, d, lo, hi, own, fi, bi, sems):
    copies = [
        pltpu.make_async_copy(src, dst, sems.at[k])
        for k, (src, dst) in enumerate(((f, fi), (b, bi), (s, own.at[2]), (d, own.at[3])))
    ]
    for copy in copies:
        copy.start()
    for k, (at, n) in enumerate(((0, H), (2 * H, H - 1), (3 * H - 1, H - 1), (H, H))):
        copies[k].wait()
        if k < 2:
            own[k] = (fi, bi)[k][...].astype(F32)
        lo[at : at + n] = own[k, 0:n]
        hi[at : at + n] = own[k, 8 - n : 8]


FACIES, BOUNDARY, SOURCE, DENSITY = range(4)
XTILES = 2 * Z0 + 3


def pack_x(own, above, below, xl, xh, lo, hi):
    for out, row in ((xl, 0), (xh, 8)):
        rows = slice(row, row + 8)
        out[:, H : H + 8] = own[:, :, rows]
        for k, at in ((FACIES, 0), (DENSITY, H)):
            out[k, 0:H] = below[at : at + H, rows]
            out[k, H + 8 : Z0] = above[at : at + H, rows]
        for k, at in ((BOUNDARY, 2 * H), (SOURCE, 3 * H - 1)):
            out[k, 1:H] = below[at : at + H - 1, rows]
            out[k, H + 8 : Z0 - 1] = above[at : at + H - 1, rows]
            out[k, 0] = out[k, Z0 - 1] = jnp.zeros((8, 128), F32)
    first = iota((8, 128), 0) < 4
    lo[XTILES - 1] = hi[XTILES - 1] = jnp.zeros((8, 128), F32)
    for z in range(Z0):
        fifth = 2 * Z0 + z // 8, slice(z % 8, z % 8 + 1)
        f, b, s, d = (xl[k, z] for k in range(4))
        lo[2 * z] = jnp.where(first, b, pltpu.roll(s, 4, 0))
        lo[2 * z + 1] = jnp.where(first, d, pltpu.roll(f, 4, 0))
        lo[fifth] = f[4:5]
        f, b, s, d = (xh[k, z] for k in range(4))
        hi[2 * z] = jnp.where(first, pltpu.roll(b, 4, 0), s)
        hi[2 * z + 1] = jnp.where(first, pltpu.roll(d, 4, 0), f)
        hi[fifth] = f[3:4]


SMALL = 7
YTILES = SMALL + 5


def block_of(k, z, tile):
    if k == FACIES:
        return SMALL + z // 4, 8 * (4 * (z % 4) + tile), 8
    layer = (k - 1) * Z0 + z
    return layer // 8, 4 * (4 * (layer % 8) + tile), 4


def pack_y(xl, xh, ml, mh, rl, rh, lo, hi):
    row, lane = iota((8, 128), 0), iota((8, 128), 1)
    for z in range(Z0):
        fifth = 2 * Z0 + z // 8, slice(z % 8, z % 8 + 1)
        bs, df = ml[2 * z], ml[2 * z + 1]
        rl[BOUNDARY, z] = bs
        rl[SOURCE, z] = pltpu.roll(bs, 4, 0)
        rl[DENSITY, z] = df
        rl[FACIES, z] = jnp.where(row == 4, ml[fifth], pltpu.roll(df, 4, 0))
        bs, df = mh[2 * z], mh[2 * z + 1]
        rh[BOUNDARY, z] = pltpu.roll(bs, 4, 0)
        rh[SOURCE, z] = bs
        rh[DENSITY, z] = pltpu.roll(df, 4, 0)
        rh[FACIES, z] = jnp.where(row == 3, mh[fifth], df)
    left, right = [None] * YTILES, [None] * YTILES
    for k in range(4):
        for z in range(Z0):
            for tile, ref in enumerate((xl, xh, rl, rh)):
                g, at, width = block_of(k, z, tile)
                v = ref[k, z]
                v = turn(v, at)
                left[g] = v if at == 0 else jnp.where(lane // width == at // width, v, left[g])
                before = (at // width - 1) % (128 // width)
                right[g] = v if at == 0 else jnp.where(lane // width == before, v, right[g])
    for g in range(YTILES):
        lo[g] = left[g]
        hi[g] = right[g]


PART = PUX, PUZ, PSINK, PB, PH = range(5)


def tile0(pos, tables, raw, first_lane, part, vs, start=0, stop=Z0):
    row, lane = iota((32, 128), 0), iota((32, 128), 1)
    x = pos[0] * 16 + jnp.where(row < 24, row, row - 32)
    y = pos[1] * 128 + first_lane + (lane if first_lane == 0 else jnp.where(lane < 64, lane, lane - 256))
    inside = (x >= 0) & (x < 256) & (y >= 0) & (y < 512)
    for z in range(start, stop):
        zg = pos[2] * 8 + z - H
        here = inside & ((zg >= 0) & (zg < 32))
        kind = raw(FACIES, z)
        h = jnp.full((32, 128), tables[0], F32)
        v = jnp.full((32, 128), tables[8], F32)
        for n in range(1, 8):
            is_n = kind == float(n)
            h = jnp.where(is_n, tables[n], h)
            v = jnp.where(is_n, tables[8 + n], v)
        part[PH, z] = jnp.where(here, h, 0.0)
        vs[z] = jnp.where(here, v, 0.0)
    for z in range(start, stop - 1):
        h, v = part[PH, z], vs[z]
        hn, vn = up(h, 0), vs[z + 1]
        hsum, vsum = h + hn, v + vn
        hsum = jnp.where(hsum > 0.0, hsum, 1.0)
        vsum = jnp.where(vsum > 0.0, vsum, 1.0)
        twice = 2.0 / (hsum * vsum)
        part[PUX, z] = (h * hn) * (twice * vsum)
        part[PUZ, z] = (v * vn) * (twice * hsum)
    for z in range(start + 1, stop - 1):
        kind = raw(BOUNDARY, z)
        part[PSINK, z] = jnp.where(
            kind == 1.0, 2.0 * vs[z], jnp.where(kind == 2.0, 0.5 * part[PH, z], 0.0)
        )
        dens = raw(DENSITY, z)
        part[PB, z] = (
            raw(SOURCE, z)
            + 0.5 * part[PUZ, z] * (dens + raw(DENSITY, z + 1))
            - 0.5 * part[PUZ, z - 1] * (raw(DENSITY, z - 1) + dens)
        )


def main0(pos, tables, xl, xh, rl, rh, part, vs):
    def raw(k, z):
        return jnp.concatenate([ref[k, z] for ref in (xl, xh, rl, rh)], axis=0)

    tile0(pos, tables, raw, 0, part, vs)


def y_sides(yl, yh, raw, layers):
    lane = iota((8, 128), 1)
    for k in range(4):
        for z in layers:
            for tile in range(4):
                g, at, width = block_of(k, z, tile)
                both = jnp.where(lane // width == at // width, yl[g], yh[g])
                raw[k, z, 8 * tile : 8 * tile + 8] = turn(both, -at)


def setup0(a, main, side, z):
    def both(k):
        return jnp.concatenate([main[k, z], side[k, z]], axis=1)

    h, sink, ux, uz, lz = both(PH), both(PSINK), both(PUX), both(PUZ), a[UZ, z - 1]
    hn = up(h, 1)
    hsum = h + hn
    uy = 2.0 * h * hn / jnp.where(hsum > 0.0, hsum, 1.0)
    a[UX, z], a[UY, z], a[UZ, z] = ux, uy, uz
    lx, ly = down(ux, 0), down(uy, 1)
    diag = sink + lz + uz + lx + ux + ly + uy
    rd = jnp.where(diag > 0.0, W / jnp.where(diag > 0.0, diag, 1.0), 0.0)
    a[RD, z] = rd
    a[C, z] = rd * both(PB)
    return diag, sink, ux, uy, uz, lx, ly, lz


def level0(pos, tables, main, yl, yh, a, packed, raw, side, vs, hs, dd, res, t, m):
    lane8 = iota((8, 128), 1)
    y_sides(yl, yh, raw, range(2, Z0 - 2))
    tile0(pos, tables, lambda k, z: raw[k, z], 128, side, vs, 2, Z0 - 2)
    row, lane = iota((32, 256), 0), iota((32, 256), 1)
    odd_row, odd_lane = row % 2 == 1, lane % 2 == 1
    a[UZ, 2] = jnp.concatenate([main[PUZ, 2], side[PUZ, 2]], axis=1)
    for z in range(3, Z0 - 3):
        diag, sink, ux, uy, uz, lx, ly, lz = setup0(a, main, side, z)
        if H <= z < H + 8:
            dd[z - H] = diag[0:16, 0:128]
            outer = sink + jnp.where(odd_row, ux, lx) + jnp.where(odd_lane, uy, ly)
            hs[z - H] = (outer + (uz if (z - H) % 2 == 1 else lz))[0:16, 0:128]

    def first(z):
        a[V, z] = smoothed(a, lambda k: a[C, k], z, z - 1, z + 1)

    each(4, Z0 - 4, first)

    def residual(z):
        v, beside = around(a, lambda k: a[V, k], z, z - 1, z + 1)
        res[z - H] = dd[z - H] * (1.5 * a[C, z] - v)[0:16, 0:128] + beside[0:16, 0:128]

    each(H, H + 8, residual)

    o_row = iota((16, 128), 0) % 2 == 1
    o_lane = iota((16, 128), 1) % 2 == 1

    def coarsen(z):
        lo, hi = H + 2 * z, H + 2 * z + 1

        def pair(ref):
            return ref[lo, 0:16, 0:128] + ref[hi, 0:16, 0:128]

        parts = (
            jnp.where(o_row, pair(a.at[UX]), 0.0),
            jnp.where(o_lane, pair(a.at[UY]), 0.0),
            a[UZ, hi, 0:16, 0:128],
            pair(main.at[PSINK]),
            res[2 * z] + res[2 * z + 1],
            hs[2 * z] + hs[2 * z + 1],
        )
        for k, part in enumerate(parts):
            t[k, z] = part
        for k in range(6):
            m[k, z] = fold_rows(t.at[k, z], 8)

    each(0, 4, coarsen)
    lower = lane8 < 64
    for s in range(2):
        parts = [jnp.where(lower, fold_lanes(m[k, s]), fold_lanes(m[k, 2 + s])) for k in range(6)]
        for k in range(4):
            packed[k, s] = parts[k]
        packed[4, s] = W * parts[4] / parts[5]


OUTER = (2, 3, Z0 - 4, Z0 - 3)


def outer0(pos, tables, main, yl, yh, a0, field, raw, side, vs, a):
    for start, stop in ((0, 4), (Z0 - 4, Z0)):
        y_sides(yl, yh, raw, range(start, stop))
        tile0(pos, tables, lambda k, z: raw[k, z], 128, side, vs, start, stop)
        a[UZ, start] = jnp.concatenate([main[PUZ, start], side[PUZ, start]], axis=1)
        for z in range(start + 1, stop - 1):
            setup0(a, main, side, z)
    for z in (3, 4, Z0 - 5, Z0 - 4):
        for k in (UX, UY, UZ, RD, C):
            a[k, z] = a0[k, z]
    for n, z in enumerate(OUTER):
        field[n] = smoothed(a, lambda k: a[C, k], z, z - 1, z + 1)


def pack_y1(own, b1, b2, b3, stack, lo, hi):
    lane = iota((8, 128), 1)
    block, last = (lane % 64) // 12, ((lane + 12) % 64) // 12
    blocks = (own, b1, b2, b3)
    for g in range(8):
        left = right = None
        for at in range(5):
            k, n = divmod(5 * g + at, 8)
            v = blocks[n // 2][k, n % 2]
            stack[5 * g + at] = v
            v = turn(v, 12 * at)
            left = v if at == 0 else jnp.where(block == at, v, left)
            right = v if at == 0 else jnp.where(last == at, v, right)
        lo[g] = left
        hi[g] = right


def pack_x1(stack, right, left, full, lo, hi):
    first = iota((8, 128), 0) < 4
    full[0:40] = stack[...]
    full[40:48] = right[...]
    full[48:56] = left[...]
    for n in range(28):
        a, b = full[2 * n], pltpu.roll(full[2 * n + 1], 4, 0)
        lo[n] = jnp.where(first, a, b)
        hi[n] = jnp.where(first, b, a)


def level12(pos, full, xr, xl, xr2, xl2, before, a, b, sent, d1, r1, t1, m1, d2, r2, s1, s2, q2):
    gx, gy, gz = pos[0], pos[1], pos[2]
    row, lane = iota((8, 128), 0), iota((8, 128), 1)
    y = gy * 64 + jnp.where(lane < 96, lane, lane - 128)
    in_y = (y >= 0) & (y < 256)
    first = row < 4

    def middle(i):
        near, far = xr2[i // 2], xl2[i // 2]
        if i % 2 == 0:
            return jnp.where(first, near, far)
        return pltpu.roll(jnp.where(first, far, near), 4, 0)

    for tile, tiles in enumerate((full, xr, None, xl)):
        of = middle if tiles is None else lambda i, tiles=tiles: tiles[i]
        edges = [(of(40 + g), of(48 + g)) for g in range(8)]
        x = gx * 8 + jnp.where(8 * tile + row < 20, 8 * tile + row, 8 * tile + row - 32)
        inside = in_y & (x >= 0) & (x < 128)
        rows = slice(8 * tile, 8 * tile + 8)
        for k in range(5):
            for n in range(8):
                g, at = divmod(8 * k + n, 5)
                v = of(8 * k + n)
                near = jnp.where((lane % 64) // 12 == at, *edges[g])
                for part in range(2):
                    own = turn(v, 64 * part)
                    beyond = turn(near, 64 - 64 * part - 12 * at)
                    value = jnp.where(inside, jnp.where(lane < 64, own, beyond), 0.0)
                    z = 4 * (n // 2) + 2 * part + n % 2
                    a[k, z, rows] = value
                    if k == SINK:
                        s1[z, rows] = value
    pre(a, d1, None, r1, 16)

    def keep1(k, z, value):
        value = fold_lanes(value)
        if k < 4:
            b[k, z] = value
        if k == SINK:
            s2[z] = value
        if k == 4:
            q2[z] = value

    halve(a, s1, r1, t1, keep1, 16, 32)
    pre(b, d2, q2, r2, 8)

    def keep2(k, z, value):
        m1[z, 0, k : k + 1] = value[0:1]
        m1[z, 1, k : k + 1] = value[1:2]

    m1[...] = jnp.zeros((4, 2, 8, 128), F32)
    halve(b, s2, r2, t1.at[:, :, 0:16], keep2, 8, 16)
    total = jnp.zeros((8, 128), F32)
    for z in range(4):
        zg = lax.rem(z + gz, 4)
        for s in range(2):
            v = m1[z, s]
            v = pick(v + up(v, 1), 2 * (lane % 16))
            total = jnp.where(lane // 16 == lax.rem(2 * zg + s + gy, 8), v, total)
    for tile in range(5):
        value = total
        for i in range(8):
            value = jnp.where(row == i, total[(8 * tile + i) % 5 : (8 * tile + i) % 5 + 1], value)
        for i in range(8):
            sent[40 * i + 8 * tile : 40 * i + 8 * tile + 8] = value


def cut(v):
    return jnp.concatenate([v[0:16], v[24:32]], axis=0)


class Cut:
    def __init__(self, ref):
        self.ref = ref

    def __getitem__(self, at):
        return cut(self.ref[at])


def sweep(a, src, dst, n, layers=None):
    for z in layers or range(n):
        dst[z % n] = smoothed(a, lambda k: src[k], z % n, (z - 1) % n, (z + 1) % n)


def solve(
    pos, got, a0, v0, a1, a2, pressure, left,
    a3, a4, d3, d4, r3, r4, s3, s4, t3, q5, e1, e2, e3, e4, f2, g4, g3, g2, g1, g0, b3, w0,
):
    gx, gy, gz = pos[0], pos[1], pos[2]
    lane = iota((16, 128), 1)
    for k in range(5):
        rows = [got[pl.ds(80 * g + k, 16, stride=5), :] for g in range(4)]
        rows = rows + [turn(value, 64) for value in rows]
        for z in range(4):
            for s in range(2):
                at = 2 * z + s
                value = rows[0]
                for g in range(1, 8):
                    value = jnp.where(lane // 16 == (at + g) % 8, rows[g], value)
                value = turn(value, -16 * at)
                if k < 4:
                    a3[k, z, pl.ds(s, 16, stride=2), :] = value
                else:
                    r3[z, pl.ds(s, 16, stride=2), :] = value
    s3[...] = a3[SINK]
    pre(a3, d3, r3, e3, 4)

    def keep3(k, z, value):
        value = fold_lanes(value)
        if k < 4:
            a4[k, z] = value
        if k == SINK:
            s4[z] = value
        if k == 4:
            r4[z] = value

    halve(a3, s3, e3, t3, keep3, 4, 32)
    pre(a4, d4, r4, e4, 2)

    def keep4(k, z, value):
        q5[k] = fold_lanes(value)

    halve(a4, s4, e4, t3.at[:, :, 0:16], keep4, 2, 16)
    ux, uy, uz, sink, r = q5[0], q5[1], q5[2], q5[3], q5[4]
    lx, ly = down(ux, 0), down(uy, 1)
    diag = sink + uz + uz + ux + lx + uy + ly
    rd = W / diag
    c = rd * r
    ux, lx, uy, ly = rd * ux, rd * lx, rd * uy, rd * ly
    v = c
    for _ in range(COARSE_SWEEPS - 1):
        beside = (ux * up(v, 0) + lx * down(v, 0)) + (uy * up(v, 1) + ly * down(v, 1))
        v = (v * (1.0 / 3.0) + c) + beside

    e = spread_rows(g4, spread_lanes(v))
    for z in range(2):
        a4[V, z] = a4[V, z] + e
    sweep(a4, a4.at[V], e4, 2)
    sweep(a4, e4, r4, 2)
    for z in range(2):
        e = spread_rows(g3.at[z], spread_lanes(r4[z]))
        a3[V, 2 * z] = a3[V, 2 * z] + e
        a3[V, 2 * z + 1] = a3[V, 2 * z + 1] + e
    sweep(a3, a3.at[V], e3, 4)
    sweep(a3, e3, r3, 4)
    b3[:, 8:40] = r3[...]
    b3[:, 0:8] = r3[:, 24:32]
    b3[:, 40:48] = r3[:, 0:8]
    lane = iota((8, 128), 1) % 64
    index = jnp.where(lane < 40, lane // 2, lane // 2 - 32) + 16 * gy
    index = lax.rem(index + 64, 64)
    for z in range(4):
        e = b3[lax.rem(z + gz, 4), pl.ds(2 * gx + 5, 8), :]
        e = pick(pltpu.roll(e, 5, 0), index)
        e = spread_rows(g2.at[z], e)
        e2[2 * z] = a2[V, 2 * z] + e
        e2[2 * z + 1] = a2[V, 2 * z + 1] + e
    sweep(a2, e2, f2, 8)
    sweep(a2, f2, e2, 8, range(-2, 4))
    for z in range(-2, 4):
        e = cut(spread_rows(g1.at[z % 8], spread_lanes(e2[z % 8])))
        for zf in (2 * z % 16, 2 * z % 16 + 1):
            e1[0, zf] = cut(a1[V, zf]) + e
    sweep(Cut(a1), e1.at[0], e1.at[1], 16, range(-3, 7))
    sweep(Cut(a1), e1.at[1], e1.at[0], 16, range(-2, 6))
    upper = iota((8, 128), 0) < 4
    for zc in range(-2, 6):
        v = e1[0, zc % 16]
        v = jnp.concatenate([v[0:8], jnp.where(upper, v[8:16], v[16:24])], axis=0)
        for half in range(2):
            e = spread_rows(g0.at[half, zc + 2], spread_lanes(v, 64 * half))
            lanes = slice(128 * half, 128 * half + 128)
            for z in (2 * zc, 2 * zc + 1):
                if -3 <= z <= 10:
                    old = v0.at[OUTER.index(z + H)] if z + H in OUTER else a0.at[V, z + H]
                    w0[0, z + H, :, lanes] = old[:, lanes] + e

    def sweep0(src, dst):
        def body(z):
            w0[dst, z] = smoothed(a0, lambda k: w0[src, k], z, z - 1, z + 1)

        return body

    each(3, Z0 - 3, sweep0(0, 1))
    each(4, Z0 - 4, sweep0(1, 0))

    def last(z):
        v, beside = around(a0, lambda k: w0[0, k], z, z - 1, z + 1)
        r = W / a0[RD, z] * (1.5 * a0[C, z] - v) + beside
        pressure[z - H] = v[0:16, 0:128]
        left[z - H] = r[0:16, 0:128]

    each(H, H + 8, last)


def shift(value, axis, by):
    count = lax.axis_size(axis)
    return lax.ppermute(value, axis, [((i + by) % count, i) for i in range(count)])


def local(facies, boundary, hc, vc, source, density):
    pos = jnp.stack([lax.axis_index(n) for n in ("gx", "gy", "gz")]).astype(jnp.int32)
    tables = jnp.concatenate([hc, vc])
    lo, hi, own = call(
        pack_z,
        [(4 * H - 2, 16, 128)] * 2 + [(4, 8, 16, 128)],
        facies, boundary, source, density,
        spaces=[HBM] * 4,
        scratch=[
            pltpu.VMEM((8, 16, 128), jnp.int32), pltpu.VMEM((8, 16, 128), jnp.int32),
            pltpu.SemaphoreType.DMA((4,)),
        ],
        limit=60,
        pin=True,
    )
    above, below = shift(lo, "gz", 1), shift(hi, "gz", -1)
    xl, xh, lo, hi = call(
        pack_x, [(4, Z0, 8, 128)] * 2 + [(XTILES, 8, 128)] * 2, own, above, below
    )
    ml, mh = shift(lo, "gx", 1), shift(hi, "gx", -1)
    rl, rh, lo, hi = call(
        pack_y, [(4, Z0, 8, 128)] * 2 + [(YTILES, 8, 128)] * 2, xl, xh, ml, mh
    )
    yl, yh = shift(lo, "gy", 1), shift(hi, "gy", -1)
    (main,) = call(
        main0, [(5, Z0, 32, 128)], pos, tables, xl, xh, rl, rh,
        spaces=[SMEM] * 2 + [VMEM] * 4, scratch=[(Z0, 32, 128)],
    )
    a0, packed = call(
        level0,
        [(6, Z0, 32, 256), (5, 2, 8, 128)],
        pos, tables, main, yl, yh,
        spaces=[SMEM] * 2 + [VMEM] * 3,
        scratch=[
            (4, Z0, 32, 128), (5, Z0, 32, 128), (Z0, 32, 128), (8, 16, 128), (8, 16, 128),
            (8, 16, 128), (6, 4, 16, 128), (6, 4, 8, 128),
        ],
    )
    (v0,) = call(
        outer0, [(4, 32, 256)], pos, tables, main, yl, yh, a0,
        spaces=[SMEM] * 2 + [VMEM] * 4,
        scratch=[(4, Z0, 32, 128), (5, Z0, 32, 128), (Z0, 32, 128), (6, Z0, 32, 256)],
    )
    blocks = [shift(packed, "gz", n) for n in (1, 2, 3)]
    stack, lo, hi = call(pack_y1, [(40, 8, 128)] + [(8, 8, 128)] * 2, packed, *blocks)
    right, left = shift(lo, "gy", 1), shift(hi, "gy", -1)
    full, lo, hi = call(pack_x1, [(56, 8, 128)] + [(28, 8, 128)] * 2, stack, right, left)
    near = (shift(full, "gx", 1), shift(full, "gx", -1), shift(lo, "gx", 2), shift(hi, "gx", -2))
    a1, a2, sent = call(
        level12,
        [(6, 16, 32, 128), (6, 8, 16, 128), (320, 128)],
        pos, full, *near, v0,
        spaces=[SMEM] + [VMEM] * 6,
        scratch=[
            (16, 32, 128), (16, 32, 128), (5, 8, 32, 128), (4, 2, 8, 128),
            (8, 16, 128), (8, 16, 128), (16, 32, 128), (8, 16, 128), (8, 16, 128),
        ],
    )
    got = lax.all_to_all(sent.reshape(64, 1, 640), ("gy", "gx"), 0, 0).reshape(320, 128)
    return tuple(
        call(
            solve,
            [(8, 16, 128), (8, 16, 128)],
            pos, got, a0, v0, a1, a2,
            spaces=[SMEM] + [VMEM] * 5,
            scratch=[
                (6, 4, 32, 128), (6, 2, 16, 128),
                (4, 32, 128), (2, 16, 128),
                (4, 32, 128), (2, 16, 128), (4, 32, 128), (2, 16, 128),
                (5, 2, 32, 128), (5, 8, 128),
                (2, 16, 24, 128), (8, 16, 128), (4, 32, 128), (2, 16, 128), (8, 16, 128),
                (16, 128), (2, 32, 128), (4, 16, 128), (8, 32, 128), (2, 8, 32, 128),
                (4, 48, 128), (2, Z0, 32, 256),
            ],
        )
    )


def solution(mesh):
    split = P("gz", "gx", "gy")
    return jax.shard_map(
        local,
        mesh=mesh,
        in_specs=(split, split, P(), P(), split, split),
        out_specs=(split, split),
        check_vma=False,
    )
```

```python
import jax
import jax.numpy as jnp
from jax import lax
from jax.experimental import pallas as pl
from jax.experimental.pallas import tpu as pltpu
from jax.sharding import PartitionSpec as P

COARSE_SWEEPS = 8
W = 2.0 / 3.0
F32 = jnp.float32
UX, UY, UZ, RD, C, V = range(6)
SINK = RD
H = 5
Z0 = 8 + 2 * H

VMEM = pl.BlockSpec(memory_space=pltpu.VMEM)
SMEM = pl.BlockSpec(memory_space=pltpu.SMEM)
HBM = pl.BlockSpec(memory_space=pltpu.HBM)


def call(kernel, outs, *args, scratch=(), spaces=None, limit=24, pin=False):
    return pl.pallas_call(
        kernel,
        out_shape=[(pltpu.VMEM if pin else jax.ShapeDtypeStruct)(s, F32) for s in outs],
        in_specs=spaces or [VMEM] * len(args),
        out_specs=[VMEM] * len(outs),
        scratch_shapes=[pltpu.VMEM(s, F32) if isinstance(s, tuple) else s for s in scratch],
        compiler_params=pltpu.CompilerParams(vmem_limit_bytes=limit * 2**20),
    )(*args)


def iota(shape, dim):
    return lax.broadcasted_iota(jnp.int32, shape, dim)


def up(a, dim):
    return pltpu.roll(a, a.shape[dim] - 1, dim)


def down(a, dim):
    return pltpu.roll(a, 1, dim)


def turn(a, by):
    by %= 128
    return pltpu.roll(a, by, a.ndim - 1) if by else a


def pick(a, index):
    return jnp.take_along_axis(a, index, axis=1, mode="promise_in_bounds")


def fold_lanes(a):
    return pick(a + up(a, 1), (2 * iota(a.shape, 1)) % 128)


def spread_lanes(a, first=0):
    return pick(a, first + iota(a.shape, 1) // 2)


def each(start, stop, body):
    for z in range(start, stop):
        body(z)


def wrap(z, n):
    return z % n


class Held:
    def __init__(self, ref=None):
        self.values, self.ref = {}, ref

    def __getitem__(self, at):
        return self.values[at]

    def __setitem__(self, at, value):
        self.values[at] = value
        if self.ref is not None:
            self.ref[at] = value


class Field:
    def __init__(self, held, k):
        self.held, self.k = held, k

    def __getitem__(self, z):
        return self.held[self.k, z]


def around(a, field, z, zm, zp):
    v = field(z)
    ux, uy = a[UX, z], a[UY, z]
    out = ux * up(v, 0) + down(ux * v, 0)
    out = out + (uy * up(v, 1) + down(uy * v, 1))
    return v, out + (a[UZ, z] * field(zp) + a[UZ, zm] * field(zm))


def smoothed(a, field, z, zm, zp):
    v, beside = around(a, field, z, zm, zp)
    return v * (1.0 / 3.0) + a[C, z] + a[RD, z] * beside


def finish(a, d, r, z, zm):
    ux, uy = a[UX, z], a[UY, z]
    diag = a[SINK, z] + a[UZ, z] + a[UZ, zm] + ux + down(ux, 0) + uy + down(uy, 1)
    d[z] = diag
    rd = jnp.where(diag > 0.0, W / jnp.where(diag > 0.0, diag, 1.0), 0.0)
    a[RD, z] = rd
    if r is not None:
        a[C, z] = rd * r[z]


def circ(n):
    return lambda z: (z, wrap(z - 1, n), wrap(z + 1, n))


def pre(a, d, r, res, n):
    c3 = circ(n)
    each(0, n, lambda z: finish(a, d, r, z, wrap(z - 1, n)))

    def one(z):
        a[V, z] = smoothed(a, lambda k: a[C, k], *c3(z))

    each(0, n, one)

    def two(z):
        v, beside = around(a, lambda k: a[V, k], *c3(z))
        res[z] = d[z] * (1.5 * a[C, z] - v) + beside

    each(0, n, two)


def halve(a, sink, r, t, store, n, rows):
    odd_row = iota((rows, 128), 0) % 2 == 1
    odd_lane = iota((rows, 128), 1) % 2 == 1

    def body(z):
        lo, hi = 2 * z, 2 * z + 1
        parts = (
            jnp.where(odd_row, a[UX, lo] + a[UX, hi], 0.0),
            jnp.where(odd_lane, a[UY, lo] + a[UY, hi], 0.0),
            a[UZ, hi],
            sink[lo] + sink[hi],
            r[lo] + r[hi],
        )
        for k, part in enumerate(parts):
            t[k, z] = part
        for k in range(5):
            store(k, z, fold_rows(t.at[k, z], rows // 2))

    each(0, n // 2, body)


def fold_rows(t, n):
    return t[pl.ds(0, n, stride=2), :] + t[pl.ds(1, n, stride=2), :]


def spread_rows(t, value):
    n = value.shape[0]
    t[pl.ds(0, n, stride=2), :] = value
    t[pl.ds(1, n, stride=2), :] = value
    return t[...]


def pack_z(f, b, s, d, lo, hi, own, fi, bi, sems):
    copies = [
        pltpu.make_async_copy(src, dst, sems.at[k])
        for k, (src, dst) in enumerate(((f, fi), (b, bi), (s, own.at[2]), (d, own.at[3])))
    ]
    for copy in copies:
        copy.start()
    for k, (at, n) in enumerate(((0, H), (2 * H, H - 1), (3 * H - 1, H - 1), (H, H))):
        copies[k].wait()
        if k < 2:
            own[k] = (fi, bi)[k][...].astype(F32)
        lo[at : at + n] = own[k, 0:n]
        hi[at : at + n] = own[k, 8 - n : 8]


FACIES, BOUNDARY, SOURCE, DENSITY = range(4)
XTILES = 2 * Z0 + 3


def pack_x(own, above, below, xl, xh, lo, hi):
    for out, row in ((xl, 0), (xh, 8)):
        rows = slice(row, row + 8)
        out[:, H : H + 8] = own[:, :, rows]
        for k, at in ((FACIES, 0), (DENSITY, H)):
            out[k, 0:H] = below[at : at + H, rows]
            out[k, H + 8 : Z0] = above[at : at + H, rows]
        for k, at in ((BOUNDARY, 2 * H), (SOURCE, 3 * H - 1)):
            out[k, 1:H] = below[at : at + H - 1, rows]
            out[k, H + 8 : Z0 - 1] = above[at : at + H - 1, rows]
            out[k, 0] = out[k, Z0 - 1] = jnp.zeros((8, 128), F32)
    first = iota((8, 128), 0) < 4
    lo[XTILES - 1] = hi[XTILES - 1] = jnp.zeros((8, 128), F32)
    for z in range(Z0):
        fifth = 2 * Z0 + z // 8, slice(z % 8, z % 8 + 1)
        f, b, s, d = (xl[k, z] for k in range(4))
        lo[2 * z] = jnp.where(first, b, pltpu.roll(s, 4, 0))
        lo[2 * z + 1] = jnp.where(first, d, pltpu.roll(f, 4, 0))
        lo[fifth] = f[4:5]
        f, b, s, d = (xh[k, z] for k in range(4))
        hi[2 * z] = jnp.where(first, pltpu.roll(b, 4, 0), s)
        hi[2 * z + 1] = jnp.where(first, pltpu.roll(d, 4, 0), f)
        hi[fifth] = f[3:4]


SMALL = 7
YTILES = SMALL + 5


def block_of(k, z, tile):
    if k == FACIES:
        return SMALL + z // 4, 8 * (4 * (z % 4) + tile), 8
    layer = (k - 1) * Z0 + z
    return layer // 8, 4 * (4 * (layer % 8) + tile), 4


def pack_y(xl, xh, ml, mh, rl, rh, lo, hi):
    row, lane = iota((8, 128), 0), iota((8, 128), 1)
    for z in range(Z0):
        fifth = 2 * Z0 + z // 8, slice(z % 8, z % 8 + 1)
        bs, df = ml[2 * z], ml[2 * z + 1]
        rl[BOUNDARY, z] = bs
        rl[SOURCE, z] = pltpu.roll(bs, 4, 0)
        rl[DENSITY, z] = df
        rl[FACIES, z] = jnp.where(row == 4, ml[fifth], pltpu.roll(df, 4, 0))
        bs, df = mh[2 * z], mh[2 * z + 1]
        rh[BOUNDARY, z] = pltpu.roll(bs, 4, 0)
        rh[SOURCE, z] = bs
        rh[DENSITY, z] = pltpu.roll(df, 4, 0)
        rh[FACIES, z] = jnp.where(row == 3, mh[fifth], df)
    left, right = [None] * YTILES, [None] * YTILES
    for k in range(4):
        for z in range(Z0):
            for tile, ref in enumerate((xl, xh, rl, rh)):
                g, at, width = block_of(k, z, tile)
                v = ref[k, z]
                v = turn(v, at)
                left[g] = v if at == 0 else jnp.where(lane // width == at // width, v, left[g])
                before = (at // width - 1) % (128 // width)
                right[g] = v if at == 0 else jnp.where(lane // width == before, v, right[g])
    for g in range(YTILES):
        lo[g] = left[g]
        hi[g] = right[g]


PART = PUX, PUZ, PSINK, PB, PH = range(5)


def tile0(pos, tables, raw, first_lane, part, vs, start=0, stop=Z0):
    row, lane = iota((32, 128), 0), iota((32, 128), 1)
    x = pos[0] * 16 + jnp.where(row < 24, row, row - 32)
    y = pos[1] * 128 + first_lane + (lane if first_lane == 0 else jnp.where(lane < 64, lane, lane - 256))
    inside = (x >= 0) & (x < 256) & (y >= 0) & (y < 512)
    for z in range(start, stop):
        zg = pos[2] * 8 + z - H
        here = inside & ((zg >= 0) & (zg < 32))
        kind = raw(FACIES, z)
        h = jnp.full((32, 128), tables[0], F32)
        v = jnp.full((32, 128), tables[8], F32)
        for n in range(1, 8):
            is_n = kind == float(n)
            h = jnp.where(is_n, tables[n], h)
            v = jnp.where(is_n, tables[8 + n], v)
        part[PH, z] = jnp.where(here, h, 0.0)
        vs[z] = jnp.where(here, v, 0.0)
    for z in range(start, stop - 1):
        h, v = part[PH, z], vs[z]
        hn, vn = up(h, 0), vs[z + 1]
        hsum, vsum = h + hn, v + vn
        hsum = jnp.where(hsum > 0.0, hsum, 1.0)
        vsum = jnp.where(vsum > 0.0, vsum, 1.0)
        twice = 2.0 / (hsum * vsum)
        part[PUX, z] = (h * hn) * (twice * vsum)
        part[PUZ, z] = (v * vn) * (twice * hsum)
    for z in range(start + 1, stop - 1):
        kind = raw(BOUNDARY, z)
        part[PSINK, z] = jnp.where(
            kind == 1.0, 2.0 * vs[z], jnp.where(kind == 2.0, 0.5 * part[PH, z], 0.0)
        )
        dens = raw(DENSITY, z)
        part[PB, z] = (
            raw(SOURCE, z)
            + 0.5 * part[PUZ, z] * (dens + raw(DENSITY, z + 1))
            - 0.5 * part[PUZ, z - 1] * (raw(DENSITY, z - 1) + dens)
        )


def main0(pos, tables, xl, xh, rl, rh, part, vs):
    def raw(k, z):
        return jnp.concatenate([ref[k, z] for ref in (xl, xh, rl, rh)], axis=0)

    tile0(pos, tables, raw, 0, part, vs)


def y_sides(yl, yh, raw, layers):
    lane = iota((8, 128), 1)
    for k in range(4):
        for z in layers:
            for tile in range(4):
                g, at, width = block_of(k, z, tile)
                both = jnp.where(lane // width == at // width, yl[g], yh[g])
                raw[k, z, 8 * tile : 8 * tile + 8] = turn(both, -at)


def setup0(a, main, side, z):
    def both(k):
        return jnp.concatenate([main[k, z], side[k, z]], axis=1)

    h, sink, ux, uz, lz = both(PH), both(PSINK), both(PUX), both(PUZ), a[UZ, z - 1]
    hn = up(h, 1)
    hsum = h + hn
    uy = 2.0 * h * hn / jnp.where(hsum > 0.0, hsum, 1.0)
    a[UX, z], a[UY, z], a[UZ, z] = ux, uy, uz
    lx, ly = down(ux, 0), down(uy, 1)
    diag = sink + lz + uz + lx + ux + ly + uy
    rd = jnp.where(diag > 0.0, W / jnp.where(diag > 0.0, diag, 1.0), 0.0)
    a[RD, z] = rd
    a[C, z] = rd * both(PB)
    return diag, sink, ux, uy, uz, lx, ly, lz


def level0(pos, tables, main, yl, yh, a, packed, raw, side, vs, hs, dd, res, t, m):
    lane8 = iota((8, 128), 1)
    y_sides(yl, yh, raw, range(2, Z0 - 2))
    tile0(pos, tables, lambda k, z: raw[k, z], 128, side, vs, 2, Z0 - 2)
    row, lane = iota((32, 256), 0), iota((32, 256), 1)
    odd_row, odd_lane = row % 2 == 1, lane % 2 == 1
    a[UZ, 2] = jnp.concatenate([main[PUZ, 2], side[PUZ, 2]], axis=1)
    for z in range(3, Z0 - 3):
        diag, sink, ux, uy, uz, lx, ly, lz = setup0(a, main, side, z)
        if H <= z < H + 8:
            dd[z - H] = diag[0:16, 0:128]
            outer = sink + jnp.where(odd_row, ux, lx) + jnp.where(odd_lane, uy, ly)
            hs[z - H] = (outer + (uz if (z - H) % 2 == 1 else lz))[0:16, 0:128]

    def first(z):
        a[V, z] = smoothed(a, lambda k: a[C, k], z, z - 1, z + 1)

    each(4, Z0 - 4, first)

    def residual(z):
        v, beside = around(a, lambda k: a[V, k], z, z - 1, z + 1)
        res[z - H] = dd[z - H] * (1.5 * a[C, z] - v)[0:16, 0:128] + beside[0:16, 0:128]

    each(H, H + 8, residual)

    o_row = iota((16, 128), 0) % 2 == 1
    o_lane = iota((16, 128), 1) % 2 == 1

    def coarsen(z):
        lo, hi = H + 2 * z, H + 2 * z + 1

        def pair(ref):
            return ref[lo, 0:16, 0:128] + ref[hi, 0:16, 0:128]

        parts = (
            jnp.where(o_row, pair(a.at[UX]), 0.0),
            jnp.where(o_lane, pair(a.at[UY]), 0.0),
            a[UZ, hi, 0:16, 0:128],
            pair(main.at[PSINK]),
            res[2 * z] + res[2 * z + 1],
            hs[2 * z] + hs[2 * z + 1],
        )
        for k, part in enumerate(parts):
            t[k, z] = part
        for k in range(6):
            m[k, z] = fold_rows(t.at[k, z], 8)

    each(0, 4, coarsen)
    lower = lane8 < 64
    for s in range(2):
        parts = [jnp.where(lower, fold_lanes(m[k, s]), fold_lanes(m[k, 2 + s])) for k in range(6)]
        for k in range(4):
            packed[k, s] = parts[k]
        packed[4, s] = W * parts[4] / parts[5]


OUTER = (2, 3, Z0 - 4, Z0 - 3)


def outer0(pos, tables, main, yl, yh, a0, field, raw, side, vs, a):
    for start, stop in ((0, 4), (Z0 - 4, Z0)):
        y_sides(yl, yh, raw, range(start, stop))
        tile0(pos, tables, lambda k, z: raw[k, z], 128, side, vs, start, stop)
        a[UZ, start] = jnp.concatenate([main[PUZ, start], side[PUZ, start]], axis=1)
        for z in range(start + 1, stop - 1):
            setup0(a, main, side, z)
    for z in (3, 4, Z0 - 5, Z0 - 4):
        for k in (UX, UY, UZ, RD, C):
            a[k, z] = a0[k, z]
    for n, z in enumerate(OUTER):
        field[n] = smoothed(a, lambda k: a[C, k], z, z - 1, z + 1)


def pack_y1(own, b1, b2, b3, stack, lo, hi):
    lane = iota((8, 128), 1)
    block, last = (lane % 64) // 12, ((lane + 12) % 64) // 12
    blocks = (own, b1, b2, b3)
    for g in range(8):
        left = right = None
        for at in range(5):
            k, n = divmod(5 * g + at, 8)
            v = blocks[n // 2][k, n % 2]
            stack[5 * g + at] = v
            v = turn(v, 12 * at)
            left = v if at == 0 else jnp.where(block == at, v, left)
            right = v if at == 0 else jnp.where(last == at, v, right)
        lo[g] = left
        hi[g] = right


def pack_x1(stack, right, left, full, lo, hi):
    first = iota((8, 128), 0) < 4
    full[0:40] = stack[...]
    full[40:48] = right[...]
    full[48:56] = left[...]
    for n in range(28):
        a, b = full[2 * n], pltpu.roll(full[2 * n + 1], 4, 0)
        lo[n] = jnp.where(first, a, b)
        hi[n] = jnp.where(first, b, a)


def level12(pos, full, xr, xl, xr2, xl2, before, a, b2, sent, d1, r1, t1, m1, s1):
    b, d2, r2, s2, q2 = Held(b2), Held(), Held(), Held(), Held()
    gx, gy, gz = pos[0], pos[1], pos[2]
    row, lane = iota((8, 128), 0), iota((8, 128), 1)
    y = gy * 64 + jnp.where(lane < 96, lane, lane - 128)
    in_y = (y >= 0) & (y < 256)
    first = row < 4

    def middle(i):
        near, far = xr2[i // 2], xl2[i // 2]
        if i % 2 == 0:
            return jnp.where(first, near, far)
        return pltpu.roll(jnp.where(first, far, near), 4, 0)

    for tile, tiles in enumerate((full, xr, None, xl)):
        of = middle if tiles is None else lambda i, tiles=tiles: tiles[i]
        edges = [(of(40 + g), of(48 + g)) for g in range(8)]
        x = gx * 8 + jnp.where(8 * tile + row < 20, 8 * tile + row, 8 * tile + row - 32)
        inside = in_y & (x >= 0) & (x < 128)
        rows = slice(8 * tile, 8 * tile + 8)
        for k in range(5):
            for n in range(8):
                g, at = divmod(8 * k + n, 5)
                v = of(8 * k + n)
                near = jnp.where((lane % 64) // 12 == at, *edges[g])
                for part in range(2):
                    own = turn(v, 64 * part)
                    beyond = turn(near, 64 - 64 * part - 12 * at)
                    value = jnp.where(inside, jnp.where(lane < 64, own, beyond), 0.0)
                    z = 4 * (n // 2) + 2 * part + n % 2
                    a[k, z, rows] = value
                    if k == SINK:
                        s1[z, rows] = value
    pre(a, d1, None, r1, 16)

    def keep1(k, z, value):
        value = fold_lanes(value)
        if k < 4:
            b[k, z] = value
        if k == SINK:
            s2[z] = value
        if k == 4:
            q2[z] = value

    halve(a, s1, r1, t1, keep1, 16, 32)
    pre(b, d2, q2, r2, 8)

    def keep2(k, z, value):
        m1[z, 0, k : k + 1] = value[0:1]
        m1[z, 1, k : k + 1] = value[1:2]

    m1[...] = jnp.zeros((4, 2, 8, 128), F32)
    halve(b, s2, r2, t1.at[:, :, 0:16], keep2, 8, 16)
    total = jnp.zeros((8, 128), F32)
    for z in range(4):
        zg = lax.rem(z + gz, 4)
        for s in range(2):
            v = m1[z, s]
            v = pick(v + up(v, 1), 2 * (lane % 16))
            total = jnp.where(lane // 16 == lax.rem(2 * zg + s + gy, 8), v, total)
    for tile in range(5):
        value = total
        for i in range(8):
            value = jnp.where(row == i, total[(8 * tile + i) % 5 : (8 * tile + i) % 5 + 1], value)
        for i in range(8):
            sent[40 * i + 8 * tile : 40 * i + 8 * tile + 8] = value


def cut(v):
    return jnp.concatenate([v[0:16], v[24:32]], axis=0)


class Cut:
    def __init__(self, ref):
        self.ref = ref

    def __getitem__(self, at):
        return cut(self.ref[at])


def sweep(a, src, dst, n, layers=None):
    for z in layers or range(n):
        dst[z % n] = smoothed(a, lambda k: src[k], z % n, (z - 1) % n, (z + 1) % n)


def solve(
    pos, got, a0, v0, a1, a2, pressure, left,
    got3, t3, e1, g4, g3, g2, g1, g0, b3, w0,
):
    a3, a4, d3, d4, r3, r4, s3, s4, e2, e3, e4, f2, q5 = (Held() for _ in range(13))
    gx, gy, gz = pos[0], pos[1], pos[2]
    lane = iota((16, 128), 1)
    for k in range(5):
        rows = [got[pl.ds(80 * g + k, 16, stride=5), :] for g in range(4)]
        rows = rows + [turn(value, 64) for value in rows]
        for z in range(4):
            for s in range(2):
                at = 2 * z + s
                value = rows[0]
                for g in range(1, 8):
                    value = jnp.where(lane // 16 == (at + g) % 8, rows[g], value)
                value = turn(value, -16 * at)
                got3[k, z, pl.ds(s, 16, stride=2), :] = value
    for z in range(4):
        for k in range(4):
            a3[k, z] = got3[k, z]
        s3[z], r3[z] = got3[SINK, z], got3[4, z]
    pre(a3, d3, r3, e3, 4)

    def keep3(k, z, value):
        value = fold_lanes(value)
        if k < 4:
            a4[k, z] = value
        if k == SINK:
            s4[z] = value
        if k == 4:
            r4[z] = value

    halve(a3, s3, e3, t3, keep3, 4, 32)
    pre(a4, d4, r4, e4, 2)

    def keep4(k, z, value):
        q5[k] = fold_lanes(value)

    halve(a4, s4, e4, t3.at[:, :, 0:16], keep4, 2, 16)
    ux, uy, uz, sink, r = q5[0], q5[1], q5[2], q5[3], q5[4]
    lx, ly = down(ux, 0), down(uy, 1)
    diag = sink + uz + uz + ux + lx + uy + ly
    rd = W / diag
    c = rd * r
    ux, lx, uy, ly = rd * ux, rd * lx, rd * uy, rd * ly
    v = c
    for _ in range(COARSE_SWEEPS - 1):
        beside = (ux * up(v, 0) + lx * down(v, 0)) + (uy * up(v, 1) + ly * down(v, 1))
        v = (v * (1.0 / 3.0) + c) + beside

    e = spread_rows(g4, spread_lanes(v))
    for z in range(2):
        a4[V, z] = a4[V, z] + e
    sweep(a4, Field(a4, V), e4, 2)
    sweep(a4, e4, r4, 2)
    for z in range(2):
        e = spread_rows(g3.at[z], spread_lanes(r4[z]))
        a3[V, 2 * z] = a3[V, 2 * z] + e
        a3[V, 2 * z + 1] = a3[V, 2 * z + 1] + e
    sweep(a3, Field(a3, V), e3, 4)
    sweep(a3, e3, r3, 4)
    for z in range(4):
        b3[z, 8:40] = r3[z]
        b3[z, 0:8] = r3[z][24:32]
        b3[z, 40:48] = r3[z][0:8]
    lane = iota((8, 128), 1) % 64
    index = jnp.where(lane < 40, lane // 2, lane // 2 - 32) + 16 * gy
    index = lax.rem(index + 64, 64)
    for z in range(4):
        e = b3[lax.rem(z + gz, 4), pl.ds(2 * gx + 5, 8), :]
        e = pick(pltpu.roll(e, 5, 0), index)
        e = spread_rows(g2.at[z], e)
        e2[2 * z] = a2[V, 2 * z] + e
        e2[2 * z + 1] = a2[V, 2 * z + 1] + e
    sweep(a2, e2, f2, 8)
    sweep(a2, f2, e2, 8, range(-2, 4))
    for z in range(-2, 4):
        e = cut(spread_rows(g1.at[z % 8], spread_lanes(e2[z % 8])))
        for zf in (2 * z % 16, 2 * z % 16 + 1):
            e1[0, zf] = cut(a1[V, zf]) + e
    sweep(Cut(a1), e1.at[0], e1.at[1], 16, range(-3, 7))
    sweep(Cut(a1), e1.at[1], e1.at[0], 16, range(-2, 6))
    upper = iota((8, 128), 0) < 4
    for zc in range(-2, 6):
        v = e1[0, zc % 16]
        v = jnp.concatenate([v[0:8], jnp.where(upper, v[8:16], v[16:24])], axis=0)
        for half in range(2):
            e = spread_rows(g0.at[half, zc + 2], spread_lanes(v, 64 * half))
            lanes = slice(128 * half, 128 * half + 128)
            for z in (2 * zc, 2 * zc + 1):
                if -3 <= z <= 10:
                    old = v0.at[OUTER.index(z + H)] if z + H in OUTER else a0.at[V, z + H]
                    w0[0, z + H, :, lanes] = old[:, lanes] + e

    def sweep0(src, dst):
        def body(z):
            w0[dst, z] = smoothed(a0, lambda k: w0[src, k], z, z - 1, z + 1)

        return body

    each(3, Z0 - 3, sweep0(0, 1))
    each(4, Z0 - 4, sweep0(1, 0))

    def last(z):
        v, beside = around(a0, lambda k: w0[0, k], z, z - 1, z + 1)
        r = W / a0[RD, z] * (1.5 * a0[C, z] - v) + beside
        pressure[z - H] = v[0:16, 0:128]
        left[z - H] = r[0:16, 0:128]

    each(H, H + 8, last)


def shift(value, axis, by):
    count = lax.axis_size(axis)
    return lax.ppermute(value, axis, [((i + by) % count, i) for i in range(count)])


def local(facies, boundary, hc, vc, source, density):
    pos = jnp.stack([lax.axis_index(n) for n in ("gx", "gy", "gz")]).astype(jnp.int32)
    tables = jnp.concatenate([hc, vc])
    lo, hi, own = call(
        pack_z,
        [(4 * H - 2, 16, 128)] * 2 + [(4, 8, 16, 128)],
        facies, boundary, source, density,
        spaces=[HBM] * 4,
        scratch=[
            pltpu.VMEM((8, 16, 128), jnp.int32), pltpu.VMEM((8, 16, 128), jnp.int32),
            pltpu.SemaphoreType.DMA((4,)),
        ],
        limit=60,
        pin=True,
    )
    above, below = shift(lo, "gz", 1), shift(hi, "gz", -1)
    xl, xh, lo, hi = call(
        pack_x, [(4, Z0, 8, 128)] * 2 + [(XTILES, 8, 128)] * 2, own, above, below
    )
    ml, mh = shift(lo, "gx", 1), shift(hi, "gx", -1)
    rl, rh, lo, hi = call(
        pack_y, [(4, Z0, 8, 128)] * 2 + [(YTILES, 8, 128)] * 2, xl, xh, ml, mh
    )
    yl, yh = shift(lo, "gy", 1), shift(hi, "gy", -1)
    (main,) = call(
        main0, [(5, Z0, 32, 128)], pos, tables, xl, xh, rl, rh,
        spaces=[SMEM] * 2 + [VMEM] * 4, scratch=[(Z0, 32, 128)],
    )
    a0, packed = call(
        level0,
        [(6, Z0, 32, 256), (5, 2, 8, 128)],
        pos, tables, main, yl, yh,
        spaces=[SMEM] * 2 + [VMEM] * 3,
        scratch=[
            (4, Z0, 32, 128), (5, Z0, 32, 128), (Z0, 32, 128), (8, 16, 128), (8, 16, 128),
            (8, 16, 128), (6, 4, 16, 128), (6, 4, 8, 128),
        ],
    )
    (v0,) = call(
        outer0, [(4, 32, 256)], pos, tables, main, yl, yh, a0,
        spaces=[SMEM] * 2 + [VMEM] * 4,
        scratch=[(4, Z0, 32, 128), (5, Z0, 32, 128), (Z0, 32, 128), (6, Z0, 32, 256)],
    )
    blocks = [shift(packed, "gz", n) for n in (1, 2, 3)]
    stack, lo, hi = call(pack_y1, [(40, 8, 128)] + [(8, 8, 128)] * 2, packed, *blocks)
    right, left = shift(lo, "gy", 1), shift(hi, "gy", -1)
    full, lo, hi = call(pack_x1, [(56, 8, 128)] + [(28, 8, 128)] * 2, stack, right, left)
    near = (shift(full, "gx", 1), shift(full, "gx", -1), shift(lo, "gx", 2), shift(hi, "gx", -2))
    a1, a2, sent = call(
        level12,
        [(6, 16, 32, 128), (6, 8, 16, 128), (320, 128)],
        pos, full, *near, v0,
        spaces=[SMEM] + [VMEM] * 6,
        scratch=[
            (16, 32, 128), (16, 32, 128), (5, 8, 32, 128), (4, 2, 8, 128), (16, 32, 128),
        ],
    )
    got = lax.all_to_all(sent.reshape(64, 1, 640), ("gy", "gx"), 0, 0).reshape(320, 128)
    return tuple(
        call(
            solve,
            [(8, 16, 128), (8, 16, 128)],
            pos, got, a0, v0, a1, a2,
            spaces=[SMEM] + [VMEM] * 5,
            scratch=[
                (5, 4, 32, 128), (5, 2, 32, 128), (2, 16, 24, 128),
                (16, 128), (2, 32, 128), (4, 16, 128), (8, 32, 128), (2, 8, 32, 128),
                (4, 48, 128), (2, Z0, 32, 256),
            ],
        )
    )


def solution(mesh):
    split = P("gz", "gx", "gy")
    return jax.shard_map(
        local,
        mesh=mesh,
        in_specs=(split, split, P(), P(), split, split),
        out_specs=(split, split),
        check_vma=False,
    )
```

```python
import jax
import jax.numpy as jnp
from jax import lax
from jax.experimental import pallas as pl
from jax.experimental.pallas import tpu as pltpu
from jax.sharding import PartitionSpec as P

COARSE_SWEEPS = 8
W = 2.0 / 3.0
F32 = jnp.float32
UX, UY, UZ, RD, C, V = range(6)
SINK = RD
H = 5
Z0 = 8 + 2 * H

VMEM = pl.BlockSpec(memory_space=pltpu.VMEM)
HBM = pl.BlockSpec(memory_space=pltpu.HBM)


def call(kernel, outs, *args, scratch=(), spaces=None, limit=24, pin=False):
    return pl.pallas_call(
        kernel,
        out_shape=[(pltpu.VMEM if pin else jax.ShapeDtypeStruct)(s, F32) for s in outs],
        in_specs=spaces or [VMEM] * len(args),
        out_specs=[VMEM] * len(outs),
        scratch_shapes=[pltpu.VMEM(s, F32) if isinstance(s, tuple) else s for s in scratch],
        compiler_params=pltpu.CompilerParams(vmem_limit_bytes=limit * 2**20),
    )(*args)


def position():
    return [lax.axis_index(name) for name in ("gx", "gy", "gz")]


def iota(shape, dim):
    return lax.broadcasted_iota(jnp.int32, shape, dim)


def up(a, dim):
    return pltpu.roll(a, a.shape[dim] - 1, dim)


def down(a, dim):
    return pltpu.roll(a, 1, dim)


def turn(a, by):
    by %= 128
    return pltpu.roll(a, by, a.ndim - 1) if by else a


def pick(a, index):
    return jnp.take_along_axis(a, index, axis=1, mode="promise_in_bounds")


def fold_lanes(a):
    return pick(a + up(a, 1), (2 * iota(a.shape, 1)) % 128)


def spread_lanes(a, first=0):
    return pick(a, first + iota(a.shape, 1) // 2)


def each(start, stop, body):
    for z in range(start, stop):
        body(z)


def wrap(z, n):
    return z % n


class Held:
    def __init__(self):
        self.values = {}

    def __getitem__(self, at):
        return self.values[at]

    def __setitem__(self, at, value):
        self.values[at] = value


class Field:
    def __init__(self, held, k):
        self.held, self.k = held, k

    def __getitem__(self, z):
        return self.held[self.k, z]


def around(a, field, z, zm, zp):
    v = field(z)
    ux, uy = a[UX, z], a[UY, z]
    out = ux * up(v, 0) + down(ux * v, 0)
    out = out + (uy * up(v, 1) + down(uy * v, 1))
    return v, out + (a[UZ, z] * field(zp) + a[UZ, zm] * field(zm))


def smoothed(a, field, z, zm, zp):
    v, beside = around(a, field, z, zm, zp)
    return v * (1.0 / 3.0) + a[C, z] + a[RD, z] * beside


def finish(a, d, r, z, zm):
    ux, uy = a[UX, z], a[UY, z]
    diag = a[SINK, z] + a[UZ, z] + a[UZ, zm] + ux + down(ux, 0) + uy + down(uy, 1)
    d[z] = diag
    rd = jnp.where(diag > 0.0, W / jnp.where(diag > 0.0, diag, 1.0), 0.0)
    a[RD, z] = rd
    if r is not None:
        a[C, z] = rd * r[z]


def circ(n):
    return lambda z: (z, wrap(z - 1, n), wrap(z + 1, n))


def pre(a, d, r, res, n):
    c3 = circ(n)
    each(0, n, lambda z: finish(a, d, r, z, wrap(z - 1, n)))

    def one(z):
        a[V, z] = smoothed(a, lambda k: a[C, k], *c3(z))

    each(0, n, one)

    def two(z):
        v, beside = around(a, lambda k: a[V, k], *c3(z))
        res[z] = d[z] * (1.5 * a[C, z] - v) + beside

    each(0, n, two)


def halve(a, sink, r, t, store, n, rows):
    odd_row = iota((rows, 128), 0) % 2 == 1
    odd_lane = iota((rows, 128), 1) % 2 == 1

    def body(z):
        lo, hi = 2 * z, 2 * z + 1
        parts = (
            jnp.where(odd_row, a[UX, lo] + a[UX, hi], 0.0),
            jnp.where(odd_lane, a[UY, lo] + a[UY, hi], 0.0),
            a[UZ, hi],
            sink[lo] + sink[hi],
            r[lo] + r[hi],
        )
        for k, part in enumerate(parts):
            t[k, z] = part
        for k in range(5):
            store(k, z, fold_rows(t.at[k, z], rows // 2))

    each(0, n // 2, body)


def fold_rows(t, n):
    return t[pl.ds(0, n, stride=2), :] + t[pl.ds(1, n, stride=2), :]


def spread_rows(t, value):
    n = value.shape[0]
    t[pl.ds(0, n, stride=2), :] = value
    t[pl.ds(1, n, stride=2), :] = value
    return t[...]


def pack_z(f, b, s, d, lo, hi, own, fi, bi, sems):
    copies = [
        pltpu.make_async_copy(src, dst, sems.at[k])
        for k, (src, dst) in enumerate(((f, fi), (b, bi), (s, own.at[2]), (d, own.at[3])))
    ]
    for copy in copies:
        copy.start()
    for k, (at, n) in enumerate(((0, H), (2 * H, H - 1), (3 * H - 1, H - 1), (H, H))):
        copies[k].wait()
        if k < 2:
            own[k] = (fi, bi)[k][...].astype(F32)
        lo[at : at + n] = own[k, 0:n]
        hi[at : at + n] = own[k, 8 - n : 8]


FACIES, BOUNDARY, SOURCE, DENSITY = range(4)
XTILES = 2 * Z0 + 3


def pack_x(own, above, below, xl, xh, lo, hi):
    for out, row in ((xl, 0), (xh, 8)):
        rows = slice(row, row + 8)
        out[:, H : H + 8] = own[:, :, rows]
        for k, at in ((FACIES, 0), (DENSITY, H)):
            out[k, 0:H] = below[at : at + H, rows]
            out[k, H + 8 : Z0] = above[at : at + H, rows]
        for k, at in ((BOUNDARY, 2 * H), (SOURCE, 3 * H - 1)):
            out[k, 1:H] = below[at : at + H - 1, rows]
            out[k, H + 8 : Z0 - 1] = above[at : at + H - 1, rows]
            out[k, 0] = out[k, Z0 - 1] = jnp.zeros((8, 128), F32)
    first = iota((8, 128), 0) < 4
    lo[XTILES - 1] = hi[XTILES - 1] = jnp.zeros((8, 128), F32)
    for z in range(Z0):
        fifth = 2 * Z0 + z // 8, slice(z % 8, z % 8 + 1)
        f, b, s, d = (xl[k, z] for k in range(4))
        lo[2 * z] = jnp.where(first, b, pltpu.roll(s, 4, 0))
        lo[2 * z + 1] = jnp.where(first, d, pltpu.roll(f, 4, 0))
        lo[fifth] = f[4:5]
        f, b, s, d = (xh[k, z] for k in range(4))
        hi[2 * z] = jnp.where(first, pltpu.roll(b, 4, 0), s)
        hi[2 * z + 1] = jnp.where(first, pltpu.roll(d, 4, 0), f)
        hi[fifth] = f[3:4]


SMALL = 7
YTILES = SMALL + 5


def block_of(k, z, tile):
    if k == FACIES:
        return SMALL + z // 4, 8 * (4 * (z % 4) + tile), 8
    layer = (k - 1) * Z0 + z
    return layer // 8, 4 * (4 * (layer % 8) + tile), 4


def pack_y(xl, xh, ml, mh, rl, rh, lo, hi):
    row, lane = iota((8, 128), 0), iota((8, 128), 1)
    for z in range(Z0):
        fifth = 2 * Z0 + z // 8, slice(z % 8, z % 8 + 1)
        bs, df = ml[2 * z], ml[2 * z + 1]
        rl[BOUNDARY, z] = bs
        rl[SOURCE, z] = pltpu.roll(bs, 4, 0)
        rl[DENSITY, z] = df
        rl[FACIES, z] = jnp.where(row == 4, ml[fifth], pltpu.roll(df, 4, 0))
        bs, df = mh[2 * z], mh[2 * z + 1]
        rh[BOUNDARY, z] = pltpu.roll(bs, 4, 0)
        rh[SOURCE, z] = bs
        rh[DENSITY, z] = pltpu.roll(df, 4, 0)
        rh[FACIES, z] = jnp.where(row == 3, mh[fifth], df)
    left, right = [None] * YTILES, [None] * YTILES
    for k in range(4):
        for z in range(Z0):
            for tile, ref in enumerate((xl, xh, rl, rh)):
                g, at, width = block_of(k, z, tile)
                v = ref[k, z]
                v = turn(v, at)
                left[g] = v if at == 0 else jnp.where(lane // width == at // width, v, left[g])
                before = (at // width - 1) % (128 // width)
                right[g] = v if at == 0 else jnp.where(lane // width == before, v, right[g])
    for g in range(YTILES):
        lo[g] = left[g]
        hi[g] = right[g]


PART = PUX, PUZ, PSINK, PB, PH = range(5)


def tile0(tables, raw, first_lane, part, vs, start=0, stop=Z0):
    pos = position()
    table = [jnp.broadcast_to(tables[n : n + 1], (32, 128)) for n in range(16)]
    row, lane = iota((32, 128), 0), iota((32, 128), 1)
    x = pos[0] * 16 + jnp.where(row < 24, row, row - 32)
    y = pos[1] * 128 + first_lane + (lane if first_lane == 0 else jnp.where(lane < 64, lane, lane - 256))
    inside = (x >= 0) & (x < 256) & (y >= 0) & (y < 512)
    for z in range(start, stop):
        zg = pos[2] * 8 + z - H
        here = inside & ((zg >= 0) & (zg < 32))
        kind = raw(FACIES, z)
        h = table[0]
        v = table[8]
        for n in range(1, 8):
            is_n = kind == float(n)
            h = jnp.where(is_n, table[n], h)
            v = jnp.where(is_n, table[8 + n], v)
        part[PH, z] = jnp.where(here, h, 0.0)
        vs[z] = jnp.where(here, v, 0.0)
    for z in range(start, stop - 1):
        h, v = part[PH, z], vs[z]
        hn, vn = up(h, 0), vs[z + 1]
        hsum, vsum = h + hn, v + vn
        hsum = jnp.where(hsum > 0.0, hsum, 1.0)
        vsum = jnp.where(vsum > 0.0, vsum, 1.0)
        twice = 2.0 / (hsum * vsum)
        part[PUX, z] = (h * hn) * (twice * vsum)
        part[PUZ, z] = (v * vn) * (twice * hsum)
    for z in range(start + 1, stop - 1):
        kind = raw(BOUNDARY, z)
        part[PSINK, z] = jnp.where(
            kind == 1.0, 2.0 * vs[z], jnp.where(kind == 2.0, 0.5 * part[PH, z], 0.0)
        )
        dens = raw(DENSITY, z)
        part[PB, z] = (
            raw(SOURCE, z)
            + 0.5 * part[PUZ, z] * (dens + raw(DENSITY, z + 1))
            - 0.5 * part[PUZ, z - 1] * (raw(DENSITY, z - 1) + dens)
        )


def main0(tables, xl, xh, rl, rh, part, vs):
    def raw(k, z):
        return jnp.concatenate([ref[k, z] for ref in (xl, xh, rl, rh)], axis=0)

    tile0(tables, raw, 0, part, vs)


def y_sides(yl, yh, raw, layers):
    lane = iota((8, 128), 1)
    for k in range(4):
        for z in layers:
            for tile in range(4):
                g, at, width = block_of(k, z, tile)
                both = jnp.where(lane // width == at // width, yl[g], yh[g])
                raw[k, z, 8 * tile : 8 * tile + 8] = turn(both, -at)


def setup0(a, main, side, z):
    def both(k):
        return jnp.concatenate([main[k, z], side[k, z]], axis=1)

    h, sink, ux, uz, lz = both(PH), both(PSINK), both(PUX), both(PUZ), a[UZ, z - 1]
    hn = up(h, 1)
    hsum = h + hn
    uy = 2.0 * h * hn / jnp.where(hsum > 0.0, hsum, 1.0)
    a[UX, z], a[UY, z], a[UZ, z] = ux, uy, uz
    lx, ly = down(ux, 0), down(uy, 1)
    diag = sink + lz + uz + lx + ux + ly + uy
    rd = jnp.where(diag > 0.0, W / jnp.where(diag > 0.0, diag, 1.0), 0.0)
    a[RD, z] = rd
    a[C, z] = rd * both(PB)
    return diag, sink, ux, uy, uz, lx, ly, lz


def level0(tables, main, yl, yh, a, packed, raw, side, vs, hs, dd, res, t, m):
    lane8 = iota((8, 128), 1)
    y_sides(yl, yh, raw, range(2, Z0 - 2))
    tile0(tables, lambda k, z: raw[k, z], 128, side, vs, 2, Z0 - 2)
    row, lane = iota((32, 256), 0), iota((32, 256), 1)
    odd_row, odd_lane = row % 2 == 1, lane % 2 == 1
    a[UZ, 2] = jnp.concatenate([main[PUZ, 2], side[PUZ, 2]], axis=1)
    for z in range(3, Z0 - 3):
        diag, sink, ux, uy, uz, lx, ly, lz = setup0(a, main, side, z)
        if H <= z < H + 8:
            dd[z - H] = diag[0:16, 0:128]
            outer = sink + jnp.where(odd_row, ux, lx) + jnp.where(odd_lane, uy, ly)
            hs[z - H] = (outer + (uz if (z - H) % 2 == 1 else lz))[0:16, 0:128]

    def first(z):
        a[V, z] = smoothed(a, lambda k: a[C, k], z, z - 1, z + 1)

    each(4, Z0 - 4, first)

    def residual(z):
        v, beside = around(a, lambda k: a[V, k], z, z - 1, z + 1)
        res[z - H] = dd[z - H] * (1.5 * a[C, z] - v)[0:16, 0:128] + beside[0:16, 0:128]

    each(H, H + 8, residual)

    o_row = iota((16, 128), 0) % 2 == 1
    o_lane = iota((16, 128), 1) % 2 == 1

    def coarsen(z):
        lo, hi = H + 2 * z, H + 2 * z + 1

        def pair(ref):
            return ref[lo, 0:16, 0:128] + ref[hi, 0:16, 0:128]

        parts = (
            jnp.where(o_row, pair(a.at[UX]), 0.0),
            jnp.where(o_lane, pair(a.at[UY]), 0.0),
            a[UZ, hi, 0:16, 0:128],
            pair(main.at[PSINK]),
            res[2 * z] + res[2 * z + 1],
            hs[2 * z] + hs[2 * z + 1],
        )
        for k, part in enumerate(parts):
            t[k, z] = part
        for k in range(6):
            m[k, z] = fold_rows(t.at[k, z], 8)

    each(0, 4, coarsen)
    lower = lane8 < 64
    for s in range(2):
        parts = [jnp.where(lower, fold_lanes(m[k, s]), fold_lanes(m[k, 2 + s])) for k in range(6)]
        for k in range(4):
            packed[k, s] = parts[k]
        packed[4, s] = W * parts[4] / parts[5]


OUTER = (2, 3, Z0 - 4, Z0 - 3)


def outer0(tables, main, yl, yh, a0, field, raw, side, vs, a):
    for start, stop in ((0, 4), (Z0 - 4, Z0)):
        y_sides(yl, yh, raw, range(start, stop))
        tile0(tables, lambda k, z: raw[k, z], 128, side, vs, start, stop)
        a[UZ, start] = jnp.concatenate([main[PUZ, start], side[PUZ, start]], axis=1)
        for z in range(start + 1, stop - 1):
            setup0(a, main, side, z)
    for z in (3, 4, Z0 - 5, Z0 - 4):
        for k in (UX, UY, UZ, RD, C):
            a[k, z] = a0[k, z]
    for n, z in enumerate(OUTER):
        field[n] = smoothed(a, lambda k: a[C, k], z, z - 1, z + 1)


def pack_y1(own, b1, b2, b3, stack, lo, hi):
    lane = iota((8, 128), 1)
    block, last = (lane % 64) // 12, ((lane + 12) % 64) // 12
    blocks = (own, b1, b2, b3)
    for g in range(8):
        left = right = None
        for at in range(5):
            k, n = divmod(5 * g + at, 8)
            v = blocks[n // 2][k, n % 2]
            stack[5 * g + at] = v
            v = turn(v, 12 * at)
            left = v if at == 0 else jnp.where(block == at, v, left)
            right = v if at == 0 else jnp.where(last == at, v, right)
        lo[g] = left
        hi[g] = right


def pack_x1(stack, right, left, full, lo, hi):
    first = iota((8, 128), 0) < 4
    full[0:40] = stack[...]
    full[40:48] = right[...]
    full[48:56] = left[...]
    for n in range(28):
        a, b = full[2 * n], pltpu.roll(full[2 * n + 1], 4, 0)
        lo[n] = jnp.where(first, a, b)
        hi[n] = jnp.where(first, b, a)


def level12(full, xr, xl, xr2, xl2, before, a, b, sent, d1, r1, t1, m1, d2, r2, s1, s2, q2):
    gx, gy, gz = position()
    row, lane = iota((8, 128), 0), iota((8, 128), 1)
    y = gy * 64 + jnp.where(lane < 96, lane, lane - 128)
    in_y = (y >= 0) & (y < 256)
    first = row < 4

    def middle(i):
        near, far = xr2[i // 2], xl2[i // 2]
        if i % 2 == 0:
            return jnp.where(first, near, far)
        return pltpu.roll(jnp.where(first, far, near), 4, 0)

    for tile, tiles in enumerate((full, xr, None, xl)):
        of = middle if tiles is None else lambda i, tiles=tiles: tiles[i]
        edges = [(of(40 + g), of(48 + g)) for g in range(8)]
        x = gx * 8 + jnp.where(8 * tile + row < 20, 8 * tile + row, 8 * tile + row - 32)
        inside = in_y & (x >= 0) & (x < 128)
        rows = slice(8 * tile, 8 * tile + 8)
        for k in range(5):
            for n in range(8):
                g, at = divmod(8 * k + n, 5)
                v = of(8 * k + n)
                near = jnp.where((lane % 64) // 12 == at, *edges[g])
                for part in range(2):
                    own = turn(v, 64 * part)
                    beyond = turn(near, 64 - 64 * part - 12 * at)
                    value = jnp.where(inside, jnp.where(lane < 64, own, beyond), 0.0)
                    z = 4 * (n // 2) + 2 * part + n % 2
                    a[k, z, rows] = value
                    if k == SINK:
                        s1[z, rows] = value
    pre(a, d1, None, r1, 16)

    def keep1(k, z, value):
        value = fold_lanes(value)
        if k < 4:
            b[k, z] = value
        if k == SINK:
            s2[z] = value
        if k == 4:
            q2[z] = value

    halve(a, s1, r1, t1, keep1, 16, 32)
    pre(b, d2, q2, r2, 8)

    def keep2(k, z, value):
        m1[z, 0, k : k + 1] = value[0:1]
        m1[z, 1, k : k + 1] = value[1:2]

    m1[...] = jnp.zeros((4, 2, 8, 128), F32)
    halve(b, s2, r2, t1.at[:, :, 0:16], keep2, 8, 16)
    total = jnp.zeros((8, 128), F32)
    for z in range(4):
        zg = lax.rem(z + gz, 4)
        for s in range(2):
            v = m1[z, s]
            v = pick(v + up(v, 1), 2 * (lane % 16))
            total = jnp.where(lane // 16 == lax.rem(2 * zg + s + gy, 8), v, total)
    for tile in range(5):
        value = total
        for i in range(8):
            value = jnp.where(row == i, total[(8 * tile + i) % 5 : (8 * tile + i) % 5 + 1], value)
        for i in range(8):
            sent[40 * i + 8 * tile : 40 * i + 8 * tile + 8] = value


def cut(v):
    return jnp.concatenate([v[0:16], v[24:32]], axis=0)


class Cut:
    def __init__(self, ref):
        self.ref = ref

    def __getitem__(self, at):
        return cut(self.ref[at])


def sweep(a, src, dst, n, layers=None):
    for z in layers or range(n):
        dst[z % n] = smoothed(a, lambda k: src[k], z % n, (z - 1) % n, (z + 1) % n)


def solve(
    got, a0, v0, a1, a2, pressure, left,
    got3, t3, e1, g4, g3, g2, g1, g0, b3, w0,
):
    a3, a4, d3, d4, r3, r4, s3, s4, e2, e3, e4, f2, q5 = (Held() for _ in range(13))
    gx, gy, gz = position()
    lane = iota((16, 128), 1)
    for k in range(5):
        rows = [got[pl.ds(80 * g + k, 16, stride=5), :] for g in range(4)]
        rows = rows + [turn(value, 64) for value in rows]
        for z in range(4):
            for s in range(2):
                at = 2 * z + s
                value = rows[0]
                for g in range(1, 8):
                    value = jnp.where(lane // 16 == (at + g) % 8, rows[g], value)
                value = turn(value, -16 * at)
                got3[k, z, pl.ds(s, 16, stride=2), :] = value
    for z in range(4):
        for k in range(4):
            a3[k, z] = got3[k, z]
        s3[z], r3[z] = got3[SINK, z], got3[4, z]
    pre(a3, d3, r3, e3, 4)

    def keep3(k, z, value):
        value = fold_lanes(value)
        if k < 4:
            a4[k, z] = value
        if k == SINK:
            s4[z] = value
        if k == 4:
            r4[z] = value

    halve(a3, s3, e3, t3, keep3, 4, 32)
    pre(a4, d4, r4, e4, 2)

    def keep4(k, z, value):
        q5[k] = fold_lanes(value)

    halve(a4, s4, e4, t3.at[:, :, 0:16], keep4, 2, 16)
    ux, uy, uz, sink, r = q5[0], q5[1], q5[2], q5[3], q5[4]
    lx, ly = down(ux, 0), down(uy, 1)
    diag = sink + uz + uz + ux + lx + uy + ly
    rd = W / diag
    c = rd * r
    ux, lx, uy, ly = rd * ux, rd * lx, rd * uy, rd * ly
    v = c
    for _ in range(COARSE_SWEEPS - 1):
        beside = (ux * up(v, 0) + lx * down(v, 0)) + (uy * up(v, 1) + ly * down(v, 1))
        v = (v * (1.0 / 3.0) + c) + beside

    e = spread_rows(g4, spread_lanes(v))
    for z in range(2):
        a4[V, z] = a4[V, z] + e
    sweep(a4, Field(a4, V), e4, 2)
    sweep(a4, e4, r4, 2)
    for z in range(2):
        e = spread_rows(g3.at[z], spread_lanes(r4[z]))
        a3[V, 2 * z] = a3[V, 2 * z] + e
        a3[V, 2 * z + 1] = a3[V, 2 * z + 1] + e
    sweep(a3, Field(a3, V), e3, 4)
    sweep(a3, e3, r3, 4)
    for z in range(4):
        b3[z, 8:40] = r3[z]
        b3[z, 0:8] = r3[z][24:32]
        b3[z, 40:48] = r3[z][0:8]
    lane = iota((8, 128), 1) % 64
    index = jnp.where(lane < 40, lane // 2, lane // 2 - 32) + 16 * gy
    index = lax.rem(index + 64, 64)
    for z in range(4):
        e = b3[lax.rem(z + gz, 4), pl.ds(2 * gx + 5, 8), :]
        e = pick(pltpu.roll(e, 5, 0), index)
        e = spread_rows(g2.at[z], e)
        e2[2 * z] = a2[V, 2 * z] + e
        e2[2 * z + 1] = a2[V, 2 * z + 1] + e
    sweep(a2, e2, f2, 8)
    sweep(a2, f2, e2, 8, range(-2, 4))
    for z in range(-2, 4):
        e = cut(spread_rows(g1.at[z % 8], spread_lanes(e2[z % 8])))
        for zf in (2 * z % 16, 2 * z % 16 + 1):
            e1[0, zf] = cut(a1[V, zf]) + e
    sweep(Cut(a1), e1.at[0], e1.at[1], 16, range(-3, 7))
    sweep(Cut(a1), e1.at[1], e1.at[0], 16, range(-2, 6))
    upper = iota((8, 128), 0) < 4
    for zc in range(-2, 6):
        v = e1[0, zc % 16]
        v = jnp.concatenate([v[0:8], jnp.where(upper, v[8:16], v[16:24])], axis=0)
        for half in range(2):
            e = spread_rows(g0.at[half, zc + 2], spread_lanes(v, 64 * half))
            lanes = slice(128 * half, 128 * half + 128)
            for z in (2 * zc, 2 * zc + 1):
                if -3 <= z <= 10:
                    old = v0.at[OUTER.index(z + H)] if z + H in OUTER else a0.at[V, z + H]
                    w0[0, z + H, :, lanes] = old[:, lanes] + e

    def sweep0(src, dst):
        def body(z):
            w0[dst, z] = smoothed(a0, lambda k: w0[src, k], z, z - 1, z + 1)

        return body

    each(3, Z0 - 3, sweep0(0, 1))
    each(4, Z0 - 4, sweep0(1, 0))

    def last(z):
        v, beside = around(a0, lambda k: w0[0, k], z, z - 1, z + 1)
        r = W / a0[RD, z] * (1.5 * a0[C, z] - v) + beside
        pressure[z - H] = v[0:16, 0:128]
        left[z - H] = r[0:16, 0:128]

    each(H, H + 8, last)


def shift(value, axis, by):
    count = lax.axis_size(axis)
    return lax.ppermute(value, axis, [((i + by) % count, i) for i in range(count)])


def local(facies, boundary, hc, vc, source, density):
    tables = jnp.broadcast_to(jnp.concatenate([hc, vc])[:, None], (16, 128))
    lo, hi, own = call(
        pack_z,
        [(4 * H - 2, 16, 128)] * 2 + [(4, 8, 16, 128)],
        facies, boundary, source, density,
        spaces=[HBM] * 4,
        scratch=[
            pltpu.VMEM((8, 16, 128), jnp.int32), pltpu.VMEM((8, 16, 128), jnp.int32),
            pltpu.SemaphoreType.DMA((4,)),
        ],
        limit=60,
        pin=True,
    )
    above, below = shift(lo, "gz", 1), shift(hi, "gz", -1)
    xl, xh, lo, hi = call(
        pack_x, [(4, Z0, 8, 128)] * 2 + [(XTILES, 8, 128)] * 2, own, above, below
    )
    ml, mh = shift(lo, "gx", 1), shift(hi, "gx", -1)
    rl, rh, lo, hi = call(
        pack_y, [(4, Z0, 8, 128)] * 2 + [(YTILES, 8, 128)] * 2, xl, xh, ml, mh
    )
    yl, yh = shift(lo, "gy", 1), shift(hi, "gy", -1)
    (main,) = call(
        main0, [(5, Z0, 32, 128)], tables, xl, xh, rl, rh, scratch=[(Z0, 32, 128)],
    )
    a0, packed = call(
        level0,
        [(6, Z0, 32, 256), (5, 2, 8, 128)],
        tables, main, yl, yh,
        scratch=[
            (4, Z0, 32, 128), (5, Z0, 32, 128), (Z0, 32, 128), (8, 16, 128), (8, 16, 128),
            (8, 16, 128), (6, 4, 16, 128), (6, 4, 8, 128),
        ],
    )
    (v0,) = call(
        outer0, [(4, 32, 256)], tables, main, yl, yh, a0,
        scratch=[(4, Z0, 32, 128), (5, Z0, 32, 128), (Z0, 32, 128), (6, Z0, 32, 256)],
    )
    blocks = [shift(packed, "gz", n) for n in (1, 2, 3)]
    stack, lo, hi = call(pack_y1, [(40, 8, 128)] + [(8, 8, 128)] * 2, packed, *blocks)
    right, left = shift(lo, "gy", 1), shift(hi, "gy", -1)
    full, lo, hi = call(pack_x1, [(56, 8, 128)] + [(28, 8, 128)] * 2, stack, right, left)
    near = (shift(full, "gx", 1), shift(full, "gx", -1), shift(lo, "gx", 2), shift(hi, "gx", -2))
    a1, a2, sent = call(
        level12,
        [(6, 16, 32, 128), (6, 8, 16, 128), (320, 128)],
        full, *near, v0,
        scratch=[
            (16, 32, 128), (16, 32, 128), (5, 8, 32, 128), (4, 2, 8, 128),
            (8, 16, 128), (8, 16, 128), (16, 32, 128), (8, 16, 128), (8, 16, 128),
        ],
    )
    got = lax.all_to_all(sent.reshape(64, 1, 640), ("gy", "gx"), 0, 0).reshape(320, 128)
    return tuple(
        call(
            solve,
            [(8, 16, 128), (8, 16, 128)],
            got, a0, v0, a1, a2,
            scratch=[
                (5, 4, 32, 128), (5, 2, 32, 128), (2, 16, 24, 128),
                (16, 128), (2, 32, 128), (4, 16, 128), (8, 32, 128), (2, 8, 32, 128),
                (4, 48, 128), (2, Z0, 32, 256),
            ],
        )
    )


def solution(mesh):
    split = P("gz", "gx", "gy")
    return jax.shard_map(
        local,
        mesh=mesh,
        in_specs=(split, split, P(), P(), split, split),
        out_specs=(split, split),
        check_vma=False,
    )
```

```python
import jax
import jax.numpy as jnp
from jax import lax
from jax.experimental import pallas as pl
from jax.experimental.pallas import tpu as pltpu
from jax.sharding import PartitionSpec as P

COARSE_SWEEPS = 8
W = 2.0 / 3.0
F32 = jnp.float32
UX, UY, UZ, RD, C, V = range(6)
SINK = RD
H = 5
Z0 = 8 + 2 * H

VMEM = pl.BlockSpec(memory_space=pltpu.VMEM)
HBM = pl.BlockSpec(memory_space=pltpu.HBM)


def call(kernel, outs, *args, scratch=(), spaces=None, limit=24, pin=False, out_space=VMEM):
    return pl.pallas_call(
        kernel,
        out_shape=[(pltpu.VMEM if pin else jax.ShapeDtypeStruct)(s, F32) for s in outs],
        in_specs=spaces or [VMEM] * len(args),
        out_specs=[out_space] * len(outs),
        scratch_shapes=[pltpu.VMEM(s, F32) if isinstance(s, tuple) else s for s in scratch],
        compiler_params=pltpu.CompilerParams(vmem_limit_bytes=limit * 2**20),
    )(*args)


def position():
    return [lax.axis_index(name) for name in ("gx", "gy", "gz")]


def iota(shape, dim):
    return lax.broadcasted_iota(jnp.int32, shape, dim)


def up(a, dim):
    return pltpu.roll(a, a.shape[dim] - 1, dim)


def down(a, dim):
    return pltpu.roll(a, 1, dim)


def turn(a, by):
    by %= 128
    return pltpu.roll(a, by, a.ndim - 1) if by else a


def pick(a, index):
    return jnp.take_along_axis(a, index, axis=1, mode="promise_in_bounds")


def fold_lanes(a):
    return pick(a + up(a, 1), (2 * iota(a.shape, 1)) % 128)


def spread_lanes(a, first=0):
    return pick(a, first + iota(a.shape, 1) // 2)


def each(start, stop, body):
    for z in range(start, stop):
        body(z)


def wrap(z, n):
    return z % n


class Held:
    def __init__(self):
        self.values = {}

    def __getitem__(self, at):
        return self.values[at]

    def __setitem__(self, at, value):
        self.values[at] = value


class Field:
    def __init__(self, held, k):
        self.held, self.k = held, k

    def __getitem__(self, z):
        return self.held[self.k, z]


def around(a, field, z, zm, zp):
    v = field(z)
    ux, uy = a[UX, z], a[UY, z]
    out = ux * up(v, 0) + down(ux * v, 0)
    out = out + (uy * up(v, 1) + down(uy * v, 1))
    return v, out + (a[UZ, z] * field(zp) + a[UZ, zm] * field(zm))


def smoothed(a, field, z, zm, zp):
    v, beside = around(a, field, z, zm, zp)
    return v * (1.0 / 3.0) + a[C, z] + a[RD, z] * beside


def finish(a, d, r, z, zm):
    ux, uy = a[UX, z], a[UY, z]
    diag = a[SINK, z] + a[UZ, z] + a[UZ, zm] + ux + down(ux, 0) + uy + down(uy, 1)
    d[z] = diag
    rd = jnp.where(diag > 0.0, W / jnp.where(diag > 0.0, diag, 1.0), 0.0)
    a[RD, z] = rd
    if r is not None:
        a[C, z] = rd * r[z]


def circ(n):
    return lambda z: (z, wrap(z - 1, n), wrap(z + 1, n))


def pre(a, d, r, res, n):
    c3 = circ(n)
    each(0, n, lambda z: finish(a, d, r, z, wrap(z - 1, n)))

    def one(z):
        a[V, z] = smoothed(a, lambda k: a[C, k], *c3(z))

    each(0, n, one)

    def two(z):
        v, beside = around(a, lambda k: a[V, k], *c3(z))
        res[z] = d[z] * (1.5 * a[C, z] - v) + beside

    each(0, n, two)


def halve(a, sink, r, t, store, n, rows):
    odd_row = iota((rows, 128), 0) % 2 == 1
    odd_lane = iota((rows, 128), 1) % 2 == 1

    def body(z):
        lo, hi = 2 * z, 2 * z + 1
        parts = (
            jnp.where(odd_row, a[UX, lo] + a[UX, hi], 0.0),
            jnp.where(odd_lane, a[UY, lo] + a[UY, hi], 0.0),
            a[UZ, hi],
            sink[lo] + sink[hi],
            r[lo] + r[hi],
        )
        for k, part in enumerate(parts):
            t[k, z] = part
        for k in range(5):
            store(k, z, fold_rows(t.at[k, z], rows // 2))

    each(0, n // 2, body)


def fold_rows(t, n):
    return t[pl.ds(0, n, stride=2), :] + t[pl.ds(1, n, stride=2), :]


def spread_rows(t, value):
    n = value.shape[0]
    t[pl.ds(0, n, stride=2), :] = value
    t[pl.ds(1, n, stride=2), :] = value
    return t[...]


def pack_z(f, b, s, d, lo, hi, own, fi, bi, sems):
    copies = [
        pltpu.make_async_copy(src, dst, sems.at[k])
        for k, (src, dst) in enumerate(((f, fi), (b, bi), (s, own.at[2]), (d, own.at[3])))
    ]
    for copy in copies:
        copy.start()
    for k, (at, n) in enumerate(((0, H), (2 * H, H - 1), (3 * H - 1, H - 1), (H, H))):
        copies[k].wait()
        if k < 2:
            own[k] = (fi, bi)[k][...].astype(F32)
        lo[at : at + n] = own[k, 0:n]
        hi[at : at + n] = own[k, 8 - n : 8]


FACIES, BOUNDARY, SOURCE, DENSITY = range(4)
XTILES = 2 * Z0 + 3


def pack_x(own, above, below, xl, xh, lo, hi):
    for out, row in ((xl, 0), (xh, 8)):
        rows = slice(row, row + 8)
        out[:, H : H + 8] = own[:, :, rows]
        for k, at in ((FACIES, 0), (DENSITY, H)):
            out[k, 0:H] = below[at : at + H, rows]
            out[k, H + 8 : Z0] = above[at : at + H, rows]
        for k, at in ((BOUNDARY, 2 * H), (SOURCE, 3 * H - 1)):
            out[k, 1:H] = below[at : at + H - 1, rows]
            out[k, H + 8 : Z0 - 1] = above[at : at + H - 1, rows]
            out[k, 0] = out[k, Z0 - 1] = jnp.zeros((8, 128), F32)
    first = iota((8, 128), 0) < 4
    lo[XTILES - 1] = hi[XTILES - 1] = jnp.zeros((8, 128), F32)
    for z in range(Z0):
        fifth = 2 * Z0 + z // 8, slice(z % 8, z % 8 + 1)
        f, b, s, d = (xl[k, z] for k in range(4))
        lo[2 * z] = jnp.where(first, b, pltpu.roll(s, 4, 0))
        lo[2 * z + 1] = jnp.where(first, d, pltpu.roll(f, 4, 0))
        lo[fifth] = f[4:5]
        f, b, s, d = (xh[k, z] for k in range(4))
        hi[2 * z] = jnp.where(first, pltpu.roll(b, 4, 0), s)
        hi[2 * z + 1] = jnp.where(first, pltpu.roll(d, 4, 0), f)
        hi[fifth] = f[3:4]


SMALL = 7
YTILES = SMALL + 5


def block_of(k, z, tile):
    if k == FACIES:
        return SMALL + z // 4, 8 * (4 * (z % 4) + tile), 8
    layer = (k - 1) * Z0 + z
    return layer // 8, 4 * (4 * (layer % 8) + tile), 4


def pack_y(xl, xh, ml, mh, rl, rh, lo, hi):
    row, lane = iota((8, 128), 0), iota((8, 128), 1)
    for z in range(Z0):
        fifth = 2 * Z0 + z // 8, slice(z % 8, z % 8 + 1)
        bs, df = ml[2 * z], ml[2 * z + 1]
        rl[BOUNDARY, z] = bs
        rl[SOURCE, z] = pltpu.roll(bs, 4, 0)
        rl[DENSITY, z] = df
        rl[FACIES, z] = jnp.where(row == 4, ml[fifth], pltpu.roll(df, 4, 0))
        bs, df = mh[2 * z], mh[2 * z + 1]
        rh[BOUNDARY, z] = pltpu.roll(bs, 4, 0)
        rh[SOURCE, z] = bs
        rh[DENSITY, z] = pltpu.roll(df, 4, 0)
        rh[FACIES, z] = jnp.where(row == 3, mh[fifth], df)
    left, right = [None] * YTILES, [None] * YTILES
    for k in range(4):
        for z in range(Z0):
            for tile, ref in enumerate((xl, xh, rl, rh)):
                g, at, width = block_of(k, z, tile)
                v = ref[k, z]
                v = turn(v, at)
                left[g] = v if at == 0 else jnp.where(lane // width == at // width, v, left[g])
                before = (at // width - 1) % (128 // width)
                right[g] = v if at == 0 else jnp.where(lane // width == before, v, right[g])
    for g in range(YTILES):
        lo[g] = left[g]
        hi[g] = right[g]


PART = PUX, PUZ, PSINK, PB, PH = range(5)


def tile0(tables, raw, first_lane, part, vs, start=0, stop=Z0):
    pos = position()
    table = [jnp.broadcast_to(tables[n : n + 1], (32, 128)) for n in range(16)]
    row, lane = iota((32, 128), 0), iota((32, 128), 1)
    x = pos[0] * 16 + jnp.where(row < 24, row, row - 32)
    y = pos[1] * 128 + first_lane + (lane if first_lane == 0 else jnp.where(lane < 64, lane, lane - 256))
    inside = (x >= 0) & (x < 256) & (y >= 0) & (y < 512)
    for z in range(start, stop):
        zg = pos[2] * 8 + z - H
        here = inside & ((zg >= 0) & (zg < 32))
        kind = raw(FACIES, z)
        h = table[0]
        v = table[8]
        for n in range(1, 8):
            is_n = kind == float(n)
            h = jnp.where(is_n, table[n], h)
            v = jnp.where(is_n, table[8 + n], v)
        part[PH, z] = jnp.where(here, h, 0.0)
        vs[z] = jnp.where(here, v, 0.0)
    for z in range(start, stop - 1):
        h, v = part[PH, z], vs[z]
        hn, vn = up(h, 0), vs[z + 1]
        hsum, vsum = h + hn, v + vn
        hsum = jnp.where(hsum > 0.0, hsum, 1.0)
        vsum = jnp.where(vsum > 0.0, vsum, 1.0)
        twice = 2.0 / (hsum * vsum)
        part[PUX, z] = (h * hn) * (twice * vsum)
        part[PUZ, z] = (v * vn) * (twice * hsum)
    for z in range(start + 1, stop - 1):
        kind = raw(BOUNDARY, z)
        part[PSINK, z] = jnp.where(
            kind == 1.0, 2.0 * vs[z], jnp.where(kind == 2.0, 0.5 * part[PH, z], 0.0)
        )
        dens = raw(DENSITY, z)
        part[PB, z] = (
            raw(SOURCE, z)
            + 0.5 * part[PUZ, z] * (dens + raw(DENSITY, z + 1))
            - 0.5 * part[PUZ, z - 1] * (raw(DENSITY, z - 1) + dens)
        )


def main0(tables, xl, xh, rl, rh, part, vs):
    def raw(k, z):
        return jnp.concatenate([ref[k, z] for ref in (xl, xh, rl, rh)], axis=0)

    tile0(tables, raw, 0, part, vs)


def y_sides(yl, yh, raw, layers):
    lane = iota((8, 128), 1)
    for k in range(4):
        for z in layers:
            for tile in range(4):
                g, at, width = block_of(k, z, tile)
                both = jnp.where(lane // width == at // width, yl[g], yh[g])
                raw[k, z, 8 * tile : 8 * tile + 8] = turn(both, -at)


def setup0(a, main, side, z):
    def both(k):
        return jnp.concatenate([main[k, z], side[k, z]], axis=1)

    h, sink, ux, uz, lz = both(PH), both(PSINK), both(PUX), both(PUZ), a[UZ, z - 1]
    hn = up(h, 1)
    hsum = h + hn
    uy = 2.0 * h * hn / jnp.where(hsum > 0.0, hsum, 1.0)
    a[UX, z], a[UY, z], a[UZ, z] = ux, uy, uz
    lx, ly = down(ux, 0), down(uy, 1)
    diag = sink + lz + uz + lx + ux + ly + uy
    rd = jnp.where(diag > 0.0, W / jnp.where(diag > 0.0, diag, 1.0), 0.0)
    a[RD, z] = rd
    a[C, z] = rd * both(PB)
    return diag, sink, ux, uy, uz, lx, ly, lz


def level0(tables, main, yl, yh, a, packed, raw, side, vs, hs, dd, res, t, m):
    lane8 = iota((8, 128), 1)
    y_sides(yl, yh, raw, range(2, Z0 - 2))
    tile0(tables, lambda k, z: raw[k, z], 128, side, vs, 2, Z0 - 2)
    row, lane = iota((32, 256), 0), iota((32, 256), 1)
    odd_row, odd_lane = row % 2 == 1, lane % 2 == 1
    a[UZ, 2] = jnp.concatenate([main[PUZ, 2], side[PUZ, 2]], axis=1)
    for z in range(3, Z0 - 3):
        diag, sink, ux, uy, uz, lx, ly, lz = setup0(a, main, side, z)
        if H <= z < H + 8:
            dd[z - H] = diag[0:16, 0:128]
            outer = sink + jnp.where(odd_row, ux, lx) + jnp.where(odd_lane, uy, ly)
            hs[z - H] = (outer + (uz if (z - H) % 2 == 1 else lz))[0:16, 0:128]

    def first(z):
        a[V, z] = smoothed(a, lambda k: a[C, k], z, z - 1, z + 1)

    each(4, Z0 - 4, first)

    def residual(z):
        v, beside = around(a, lambda k: a[V, k], z, z - 1, z + 1)
        res[z - H] = dd[z - H] * (1.5 * a[C, z] - v)[0:16, 0:128] + beside[0:16, 0:128]

    each(H, H + 8, residual)

    o_row = iota((16, 128), 0) % 2 == 1
    o_lane = iota((16, 128), 1) % 2 == 1

    def coarsen(z):
        lo, hi = H + 2 * z, H + 2 * z + 1

        def pair(ref):
            return ref[lo, 0:16, 0:128] + ref[hi, 0:16, 0:128]

        parts = (
            jnp.where(o_row, pair(a.at[UX]), 0.0),
            jnp.where(o_lane, pair(a.at[UY]), 0.0),
            a[UZ, hi, 0:16, 0:128],
            pair(main.at[PSINK]),
            res[2 * z] + res[2 * z + 1],
            hs[2 * z] + hs[2 * z + 1],
        )
        for k, part in enumerate(parts):
            t[k, z] = part
        for k in range(6):
            m[k, z] = fold_rows(t.at[k, z], 8)

    each(0, 4, coarsen)
    lower = lane8 < 64
    for s in range(2):
        parts = [jnp.where(lower, fold_lanes(m[k, s]), fold_lanes(m[k, 2 + s])) for k in range(6)]
        for k in range(4):
            packed[k, s] = parts[k]
        packed[4, s] = W * parts[4] / parts[5]


OUTER = (2, 3, Z0 - 4, Z0 - 3)


def outer0(tables, main, yl, yh, a0, field, raw, side, vs, a):
    for start, stop in ((0, 4), (Z0 - 4, Z0)):
        y_sides(yl, yh, raw, range(start, stop))
        tile0(tables, lambda k, z: raw[k, z], 128, side, vs, start, stop)
        a[UZ, start] = jnp.concatenate([main[PUZ, start], side[PUZ, start]], axis=1)
        for z in range(start + 1, stop - 1):
            setup0(a, main, side, z)
    for z in (3, 4, Z0 - 5, Z0 - 4):
        for k in (UX, UY, UZ, RD, C):
            a[k, z] = a0[k, z]
    for n, z in enumerate(OUTER):
        field[n] = smoothed(a, lambda k: a[C, k], z, z - 1, z + 1)


def pack_y1(own, b1, b2, b3, stack, lo, hi):
    lane = iota((8, 128), 1)
    block, last = (lane % 64) // 12, ((lane + 12) % 64) // 12
    blocks = (own, b1, b2, b3)
    for g in range(8):
        left = right = None
        for at in range(5):
            k, n = divmod(5 * g + at, 8)
            v = blocks[n // 2][k, n % 2]
            stack[5 * g + at] = v
            v = turn(v, 12 * at)
            left = v if at == 0 else jnp.where(block == at, v, left)
            right = v if at == 0 else jnp.where(last == at, v, right)
        lo[g] = left
        hi[g] = right


def pack_x1(stack, right, left, full, lo, hi):
    first = iota((8, 128), 0) < 4
    full[0:40] = stack[...]
    full[40:48] = right[...]
    full[48:56] = left[...]
    for n in range(28):
        a, b = full[2 * n], pltpu.roll(full[2 * n + 1], 4, 0)
        lo[n] = jnp.where(first, a, b)
        hi[n] = jnp.where(first, b, a)


def level12(full, xr, xl, xr2, xl2, before, a, b, sent, d1, r1, t1, m1, d2, r2, s1, s2, q2):
    gx, gy, gz = position()
    row, lane = iota((8, 128), 0), iota((8, 128), 1)
    y = gy * 64 + jnp.where(lane < 96, lane, lane - 128)
    in_y = (y >= 0) & (y < 256)
    first = row < 4

    def middle(i):
        near, far = xr2[i // 2], xl2[i // 2]
        if i % 2 == 0:
            return jnp.where(first, near, far)
        return pltpu.roll(jnp.where(first, far, near), 4, 0)

    for tile, tiles in enumerate((full, xr, None, xl)):
        of = middle if tiles is None else lambda i, tiles=tiles: tiles[i]
        edges = [(of(40 + g), of(48 + g)) for g in range(8)]
        x = gx * 8 + jnp.where(8 * tile + row < 20, 8 * tile + row, 8 * tile + row - 32)
        inside = in_y & (x >= 0) & (x < 128)
        rows = slice(8 * tile, 8 * tile + 8)
        for k in range(5):
            for n in range(8):
                g, at = divmod(8 * k + n, 5)
                v = of(8 * k + n)
                near = jnp.where((lane % 64) // 12 == at, *edges[g])
                for part in range(2):
                    own = turn(v, 64 * part)
                    beyond = turn(near, 64 - 64 * part - 12 * at)
                    value = jnp.where(inside, jnp.where(lane < 64, own, beyond), 0.0)
                    z = 4 * (n // 2) + 2 * part + n % 2
                    a[k, z, rows] = value
                    if k == SINK:
                        s1[z, rows] = value
    pre(a, d1, None, r1, 16)

    def keep1(k, z, value):
        value = fold_lanes(value)
        if k < 4:
            b[k, z] = value
        if k == SINK:
            s2[z] = value
        if k == 4:
            q2[z] = value

    halve(a, s1, r1, t1, keep1, 16, 32)
    pre(b, d2, q2, r2, 8)

    def keep2(k, z, value):
        m1[z, 0, k : k + 1] = value[0:1]
        m1[z, 1, k : k + 1] = value[1:2]

    m1[...] = jnp.zeros((4, 2, 8, 128), F32)
    halve(b, s2, r2, t1.at[:, :, 0:16], keep2, 8, 16)
    total = jnp.zeros((8, 128), F32)
    for z in range(4):
        zg = lax.rem(z + gz, 4)
        for s in range(2):
            v = m1[z, s]
            v = pick(v + up(v, 1), 2 * (lane % 16))
            total = jnp.where(lane // 16 == lax.rem(2 * zg + s + gy, 8), v, total)
    for tile in range(5):
        value = total
        for i in range(8):
            value = jnp.where(row == i, total[(8 * tile + i) % 5 : (8 * tile + i) % 5 + 1], value)
        for i in range(8):
            sent[40 * i + 8 * tile : 40 * i + 8 * tile + 8] = value


def cut(v):
    return jnp.concatenate([v[0:16], v[24:32]], axis=0)


class Cut:
    def __init__(self, ref):
        self.ref = ref

    def __getitem__(self, at):
        return cut(self.ref[at])


def sweep(a, src, dst, n, layers=None):
    for z in layers or range(n):
        dst[z % n] = smoothed(a, lambda k: src[k], z % n, (z - 1) % n, (z + 1) % n)


def solve(
    got, a0, v0, a1, a2, pressure, left,
    got3, t3, e1, g4, g3, g2, g1, g0, b3, w0, final, rest, sems,
):
    a3, a4, d3, d4, r3, r4, s3, s4, e2, e3, e4, f2, q5 = (Held() for _ in range(13))
    gx, gy, gz = position()
    lane = iota((16, 128), 1)
    for k in range(5):
        rows = [got[pl.ds(80 * g + k, 16, stride=5), :] for g in range(4)]
        rows = rows + [turn(value, 64) for value in rows]
        for z in range(4):
            for s in range(2):
                at = 2 * z + s
                value = rows[0]
                for g in range(1, 8):
                    value = jnp.where(lane // 16 == (at + g) % 8, rows[g], value)
                value = turn(value, -16 * at)
                got3[k, z, pl.ds(s, 16, stride=2), :] = value
    for z in range(4):
        for k in range(4):
            a3[k, z] = got3[k, z]
        s3[z], r3[z] = got3[SINK, z], got3[4, z]
    pre(a3, d3, r3, e3, 4)

    def keep3(k, z, value):
        value = fold_lanes(value)
        if k < 4:
            a4[k, z] = value
        if k == SINK:
            s4[z] = value
        if k == 4:
            r4[z] = value

    halve(a3, s3, e3, t3, keep3, 4, 32)
    pre(a4, d4, r4, e4, 2)

    def keep4(k, z, value):
        q5[k] = fold_lanes(value)

    halve(a4, s4, e4, t3.at[:, :, 0:16], keep4, 2, 16)
    ux, uy, uz, sink, r = q5[0], q5[1], q5[2], q5[3], q5[4]
    lx, ly = down(ux, 0), down(uy, 1)
    diag = sink + uz + uz + ux + lx + uy + ly
    rd = W / diag
    c = rd * r
    ux, lx, uy, ly = rd * ux, rd * lx, rd * uy, rd * ly
    v = c
    for _ in range(COARSE_SWEEPS - 1):
        beside = (ux * up(v, 0) + lx * down(v, 0)) + (uy * up(v, 1) + ly * down(v, 1))
        v = (v * (1.0 / 3.0) + c) + beside

    e = spread_rows(g4, spread_lanes(v))
    for z in range(2):
        a4[V, z] = a4[V, z] + e
    sweep(a4, Field(a4, V), e4, 2)
    sweep(a4, e4, r4, 2)
    for z in range(2):
        e = spread_rows(g3.at[z], spread_lanes(r4[z]))
        a3[V, 2 * z] = a3[V, 2 * z] + e
        a3[V, 2 * z + 1] = a3[V, 2 * z + 1] + e
    sweep(a3, Field(a3, V), e3, 4)
    sweep(a3, e3, r3, 4)
    for z in range(4):
        b3[z, 8:40] = r3[z]
        b3[z, 0:8] = r3[z][24:32]
        b3[z, 40:48] = r3[z][0:8]
    lane = iota((8, 128), 1) % 64
    index = jnp.where(lane < 40, lane // 2, lane // 2 - 32) + 16 * gy
    index = lax.rem(index + 64, 64)
    for z in range(4):
        e = b3[lax.rem(z + gz, 4), pl.ds(2 * gx + 5, 8), :]
        e = pick(pltpu.roll(e, 5, 0), index)
        e = spread_rows(g2.at[z], e)
        e2[2 * z] = a2[V, 2 * z] + e
        e2[2 * z + 1] = a2[V, 2 * z + 1] + e
    sweep(a2, e2, f2, 8)
    sweep(a2, f2, e2, 8, range(-2, 4))
    for z in range(-2, 4):
        e = cut(spread_rows(g1.at[z % 8], spread_lanes(e2[z % 8])))
        for zf in (2 * z % 16, 2 * z % 16 + 1):
            e1[0, zf] = cut(a1[V, zf]) + e
    sweep(Cut(a1), e1.at[0], e1.at[1], 16, range(-3, 7))
    sweep(Cut(a1), e1.at[1], e1.at[0], 16, range(-2, 6))
    upper = iota((8, 128), 0) < 4
    for zc in range(-2, 6):
        v = e1[0, zc % 16]
        v = jnp.concatenate([v[0:8], jnp.where(upper, v[8:16], v[16:24])], axis=0)
        for half in range(2):
            e = spread_rows(g0.at[half, zc + 2], spread_lanes(v, 64 * half))
            lanes = slice(128 * half, 128 * half + 128)
            for z in (2 * zc, 2 * zc + 1):
                if -3 <= z <= 10:
                    old = v0.at[OUTER.index(z + H)] if z + H in OUTER else a0.at[V, z + H]
                    w0[0, z + H, :, lanes] = old[:, lanes] + e

    def sweep0(src, dst):
        def body(z):
            w0[dst, z] = smoothed(a0, lambda k: w0[src, k], z, z - 1, z + 1)

        return body

    each(3, Z0 - 3, sweep0(0, 1))
    each(4, Z0 - 4, sweep0(1, 0))

    for z in range(8):
        final[z] = w0[0, z + H, 0:16, 0:128]
    copies = [
        pltpu.make_async_copy(final, pressure, sems.at[0]),
        pltpu.make_async_copy(rest.at[0:4], left.at[0:4], sems.at[1]),
        pltpu.make_async_copy(rest.at[4:8], left.at[4:8], sems.at[2]),
    ]
    copies[0].start()
    for z in range(8):
        v, beside = around(a0, lambda k: w0[0, k], z + H, z + H - 1, z + H + 1)
        r = W / a0[RD, z + H] * (1.5 * a0[C, z + H] - v) + beside
        rest[z] = r[0:16, 0:128]
        if z % 4 == 3:
            copies[1 + z // 4].start()
    for copy in copies:
        copy.wait()


def shift(value, axis, by):
    count = lax.axis_size(axis)
    return lax.ppermute(value, axis, [((i + by) % count, i) for i in range(count)])


def local(facies, boundary, hc, vc, source, density):
    tables = jnp.broadcast_to(jnp.concatenate([hc, vc])[:, None], (16, 128))
    lo, hi, own = call(
        pack_z,
        [(4 * H - 2, 16, 128)] * 2 + [(4, 8, 16, 128)],
        facies, boundary, source, density,
        spaces=[HBM] * 4,
        scratch=[
            pltpu.VMEM((8, 16, 128), jnp.int32), pltpu.VMEM((8, 16, 128), jnp.int32),
            pltpu.SemaphoreType.DMA((4,)),
        ],
        limit=60,
        pin=True,
    )
    above, below = shift(lo, "gz", 1), shift(hi, "gz", -1)
    xl, xh, lo, hi = call(
        pack_x, [(4, Z0, 8, 128)] * 2 + [(XTILES, 8, 128)] * 2, own, above, below
    )
    ml, mh = shift(lo, "gx", 1), shift(hi, "gx", -1)
    rl, rh, lo, hi = call(
        pack_y, [(4, Z0, 8, 128)] * 2 + [(YTILES, 8, 128)] * 2, xl, xh, ml, mh
    )
    yl, yh = shift(lo, "gy", 1), shift(hi, "gy", -1)
    (main,) = call(
        main0, [(5, Z0, 32, 128)], tables, xl, xh, rl, rh, scratch=[(Z0, 32, 128)],
    )
    a0, packed = call(
        level0,
        [(6, Z0, 32, 256), (5, 2, 8, 128)],
        tables, main, yl, yh,
        scratch=[
            (4, Z0, 32, 128), (5, Z0, 32, 128), (Z0, 32, 128), (8, 16, 128), (8, 16, 128),
            (8, 16, 128), (6, 4, 16, 128), (6, 4, 8, 128),
        ],
    )
    (v0,) = call(
        outer0, [(4, 32, 256)], tables, main, yl, yh, a0,
        scratch=[(4, Z0, 32, 128), (5, Z0, 32, 128), (Z0, 32, 128), (6, Z0, 32, 256)],
    )
    blocks = [shift(packed, "gz", n) for n in (1, 2, 3)]
    stack, lo, hi = call(pack_y1, [(40, 8, 128)] + [(8, 8, 128)] * 2, packed, *blocks)
    right, left = shift(lo, "gy", 1), shift(hi, "gy", -1)
    full, lo, hi = call(pack_x1, [(56, 8, 128)] + [(28, 8, 128)] * 2, stack, right, left)
    near = (shift(full, "gx", 1), shift(full, "gx", -1), shift(lo, "gx", 2), shift(hi, "gx", -2))
    a1, a2, sent = call(
        level12,
        [(6, 16, 32, 128), (6, 8, 16, 128), (320, 128)],
        full, *near, v0,
        scratch=[
            (16, 32, 128), (16, 32, 128), (5, 8, 32, 128), (4, 2, 8, 128),
            (8, 16, 128), (8, 16, 128), (16, 32, 128), (8, 16, 128), (8, 16, 128),
        ],
    )
    got = lax.all_to_all(sent.reshape(64, 1, 640), ("gy", "gx"), 0, 0).reshape(320, 128)
    return tuple(
        call(
            solve,
            [(8, 16, 128), (8, 16, 128)],
            got, a0, v0, a1, a2,
            scratch=[
                (5, 4, 32, 128), (5, 2, 32, 128), (2, 16, 24, 128),
                (16, 128), (2, 32, 128), (4, 16, 128), (8, 32, 128), (2, 8, 32, 128),
                (4, 48, 128), (2, Z0, 32, 256),
                (8, 16, 128), (8, 16, 128), pltpu.SemaphoreType.DMA((3,)),
            ],
            out_space=HBM,
        )
    )


def solution(mesh):
    split = P("gz", "gx", "gy")
    return jax.shard_map(
        local,
        mesh=mesh,
        in_specs=(split, split, P(), P(), split, split),
        out_specs=(split, split),
        check_vma=False,
    )
```

```python
import jax
import jax.numpy as jnp
from jax import lax
from jax.experimental import pallas as pl
from jax.experimental.pallas import tpu as pltpu
from jax.sharding import PartitionSpec as P

COARSE_SWEEPS = 8
W = 2.0 / 3.0
F32 = jnp.float32
UX, UY, UZ, RD, C, V = range(6)
SINK = RD
H = 5
Z0 = 8 + 2 * H

VMEM = pl.BlockSpec(memory_space=pltpu.VMEM)
HBM = pl.BlockSpec(memory_space=pltpu.HBM)


def call(kernel, outs, *args, scratch=(), spaces=None, limit=24, pin=False):
    return pl.pallas_call(
        kernel,
        out_shape=[(pltpu.VMEM if pin else jax.ShapeDtypeStruct)(s, F32) for s in outs],
        in_specs=spaces or [VMEM] * len(args),
        out_specs=[VMEM] * len(outs),
        scratch_shapes=[pltpu.VMEM(s, F32) if isinstance(s, tuple) else s for s in scratch],
        compiler_params=pltpu.CompilerParams(vmem_limit_bytes=limit * 2**20),
    )(*args)


def position():
    return [lax.axis_index(name) for name in ("gx", "gy", "gz")]


def iota(shape, dim):
    return lax.broadcasted_iota(jnp.int32, shape, dim)


def up(a, dim):
    return pltpu.roll(a, a.shape[dim] - 1, dim)


def down(a, dim):
    return pltpu.roll(a, 1, dim)


def turn(a, by):
    by %= 128
    return pltpu.roll(a, by, a.ndim - 1) if by else a


def pick(a, index):
    return jnp.take_along_axis(a, index, axis=1, mode="promise_in_bounds")


def fold_lanes(a):
    return pick(a + up(a, 1), (2 * iota(a.shape, 1)) % 128)


def spread_lanes(a, first=0):
    return pick(a, first + iota(a.shape, 1) // 2)


def each(start, stop, body):
    for z in range(start, stop):
        body(z)


def wrap(z, n):
    return z % n


class Held:
    def __init__(self):
        self.values = {}

    def __getitem__(self, at):
        return self.values[at]

    def __setitem__(self, at, value):
        self.values[at] = value


class Field:
    def __init__(self, held, k):
        self.held, self.k = held, k

    def __getitem__(self, z):
        return self.held[self.k, z]


def around(a, field, z, zm, zp):
    v = field(z)
    ux, uy = a[UX, z], a[UY, z]
    out = ux * up(v, 0) + down(ux * v, 0)
    out = out + (uy * up(v, 1) + down(uy * v, 1))
    return v, out + (a[UZ, z] * field(zp) + a[UZ, zm] * field(zm))


def smoothed(a, field, z, zm, zp):
    v, beside = around(a, field, z, zm, zp)
    return v * (1.0 / 3.0) + a[C, z] + a[RD, z] * beside


def finish(a, d, r, z, zm):
    ux, uy = a[UX, z], a[UY, z]
    diag = a[SINK, z] + a[UZ, z] + a[UZ, zm] + ux + down(ux, 0) + uy + down(uy, 1)
    d[z] = diag
    rd = jnp.where(diag > 0.0, W / jnp.where(diag > 0.0, diag, 1.0), 0.0)
    a[RD, z] = rd
    if r is not None:
        a[C, z] = rd * r[z]


def circ(n):
    return lambda z: (z, wrap(z - 1, n), wrap(z + 1, n))


def pre(a, d, r, res, n):
    c3 = circ(n)
    each(0, n, lambda z: finish(a, d, r, z, wrap(z - 1, n)))

    def one(z):
        a[V, z] = smoothed(a, lambda k: a[C, k], *c3(z))

    each(0, n, one)

    def two(z):
        v, beside = around(a, lambda k: a[V, k], *c3(z))
        res[z] = d[z] * (1.5 * a[C, z] - v) + beside

    each(0, n, two)


def halve(a, sink, r, t, store, n, rows):
    odd_row = iota((rows, 128), 0) % 2 == 1
    odd_lane = iota((rows, 128), 1) % 2 == 1

    def body(z):
        lo, hi = 2 * z, 2 * z + 1
        parts = (
            jnp.where(odd_row, a[UX, lo] + a[UX, hi], 0.0),
            jnp.where(odd_lane, a[UY, lo] + a[UY, hi], 0.0),
            a[UZ, hi],
            sink[lo] + sink[hi],
            r[lo] + r[hi],
        )
        for k, part in enumerate(parts):
            t[k, z] = part
        for k in range(5):
            store(k, z, fold_rows(t.at[k, z], rows // 2))

    each(0, n // 2, body)


def fold_rows(t, n):
    return t[pl.ds(0, n, stride=2), :] + t[pl.ds(1, n, stride=2), :]


def spread_rows(t, value):
    n = value.shape[0]
    t[pl.ds(0, n, stride=2), :] = value
    t[pl.ds(1, n, stride=2), :] = value
    return t[...]


def pack_z(f, b, s, d, lo, hi, own, fi, bi, sems):
    copies = [
        pltpu.make_async_copy(src, dst, sems.at[k])
        for k, (src, dst) in enumerate(((f, fi), (b, bi), (s, own.at[2]), (d, own.at[3])))
    ]
    for copy in copies:
        copy.start()
    for k, (at, n) in enumerate(((0, H), (2 * H, H - 1), (3 * H - 1, H - 1), (H, H))):
        copies[k].wait()
        if k < 2:
            own[k] = (fi, bi)[k][...].astype(F32)
        lo[at : at + n] = own[k, 0:n]
        hi[at : at + n] = own[k, 8 - n : 8]


FACIES, BOUNDARY, SOURCE, DENSITY = range(4)
XTILES = 2 * Z0 + 3


def pack_x(own, above, below, xl, xh, lo, hi):
    for out, row in ((xl, 0), (xh, 8)):
        rows = slice(row, row + 8)
        out[:, H : H + 8] = own[:, :, rows]
        for k, at in ((FACIES, 0), (DENSITY, H)):
            out[k, 0:H] = below[at : at + H, rows]
            out[k, H + 8 : Z0] = above[at : at + H, rows]
        for k, at in ((BOUNDARY, 2 * H), (SOURCE, 3 * H - 1)):
            out[k, 1:H] = below[at : at + H - 1, rows]
            out[k, H + 8 : Z0 - 1] = above[at : at + H - 1, rows]
            out[k, 0] = out[k, Z0 - 1] = jnp.zeros((8, 128), F32)
    first = iota((8, 128), 0) < 4
    lo[XTILES - 1] = hi[XTILES - 1] = jnp.zeros((8, 128), F32)
    for z in range(Z0):
        fifth = 2 * Z0 + z // 8, slice(z % 8, z % 8 + 1)
        f, b, s, d = (xl[k, z] for k in range(4))
        lo[2 * z] = jnp.where(first, b, pltpu.roll(s, 4, 0))
        lo[2 * z + 1] = jnp.where(first, d, pltpu.roll(f, 4, 0))
        lo[fifth] = f[4:5]
        f, b, s, d = (xh[k, z] for k in range(4))
        hi[2 * z] = jnp.where(first, pltpu.roll(b, 4, 0), s)
        hi[2 * z + 1] = jnp.where(first, pltpu.roll(d, 4, 0), f)
        hi[fifth] = f[3:4]


SMALL = 7
YTILES = SMALL + 5


def block_of(k, z, tile):
    if k == FACIES:
        return SMALL + z // 4, 8 * (4 * (z % 4) + tile), 8
    layer = (k - 1) * Z0 + z
    return layer // 8, 4 * (4 * (layer % 8) + tile), 4


def pack_y(xl, xh, ml, mh, rl, rh, lo, hi):
    row, lane = iota((8, 128), 0), iota((8, 128), 1)
    for z in range(Z0):
        fifth = 2 * Z0 + z // 8, slice(z % 8, z % 8 + 1)
        bs, df = ml[2 * z], ml[2 * z + 1]
        rl[BOUNDARY, z] = bs
        rl[SOURCE, z] = pltpu.roll(bs, 4, 0)
        rl[DENSITY, z] = df
        rl[FACIES, z] = jnp.where(row == 4, ml[fifth], pltpu.roll(df, 4, 0))
        bs, df = mh[2 * z], mh[2 * z + 1]
        rh[BOUNDARY, z] = pltpu.roll(bs, 4, 0)
        rh[SOURCE, z] = bs
        rh[DENSITY, z] = pltpu.roll(df, 4, 0)
        rh[FACIES, z] = jnp.where(row == 3, mh[fifth], df)
    left, right = [None] * YTILES, [None] * YTILES
    for k in range(4):
        for z in range(Z0):
            for tile, ref in enumerate((xl, xh, rl, rh)):
                g, at, width = block_of(k, z, tile)
                v = ref[k, z]
                v = turn(v, at)
                left[g] = v if at == 0 else jnp.where(lane // width == at // width, v, left[g])
                before = (at // width - 1) % (128 // width)
                right[g] = v if at == 0 else jnp.where(lane // width == before, v, right[g])
    for g in range(YTILES):
        lo[g] = left[g]
        hi[g] = right[g]


PART = PUX, PUZ, PSINK, PB, PH = range(5)


def tile0(tables, raw, first_lane, part, vs, start=0, stop=Z0):
    pos = position()
    table = [jnp.broadcast_to(tables[n : n + 1], (32, 128)) for n in range(16)]
    row, lane = iota((32, 128), 0), iota((32, 128), 1)
    x = pos[0] * 16 + jnp.where(row < 24, row, row - 32)
    y = pos[1] * 128 + first_lane + (lane if first_lane == 0 else jnp.where(lane < 64, lane, lane - 256))
    inside = (x >= 0) & (x < 256) & (y >= 0) & (y < 512)
    for z in range(start, stop):
        zg = pos[2] * 8 + z - H
        here = inside & ((zg >= 0) & (zg < 32))
        kind = raw(FACIES, z)
        h = table[0]
        v = table[8]
        for n in range(1, 8):
            is_n = kind == float(n)
            h = jnp.where(is_n, table[n], h)
            v = jnp.where(is_n, table[8 + n], v)
        part[PH, z] = jnp.where(here, h, 0.0)
        vs[z] = jnp.where(here, v, 0.0)
    for z in range(start, stop - 1):
        h, v = part[PH, z], vs[z]
        hn, vn = up(h, 0), vs[z + 1]
        hsum, vsum = h + hn, v + vn
        hsum = jnp.where(hsum > 0.0, hsum, 1.0)
        vsum = jnp.where(vsum > 0.0, vsum, 1.0)
        twice = 2.0 / (hsum * vsum)
        part[PUX, z] = (h * hn) * (twice * vsum)
        part[PUZ, z] = (v * vn) * (twice * hsum)
    for z in range(start + 1, stop - 1):
        kind = raw(BOUNDARY, z)
        part[PSINK, z] = jnp.where(
            kind == 1.0, 2.0 * vs[z], jnp.where(kind == 2.0, 0.5 * part[PH, z], 0.0)
        )
        dens = raw(DENSITY, z)
        part[PB, z] = (
            raw(SOURCE, z)
            + 0.5 * part[PUZ, z] * (dens + raw(DENSITY, z + 1))
            - 0.5 * part[PUZ, z - 1] * (raw(DENSITY, z - 1) + dens)
        )


def main0(tables, xl, xh, rl, rh, part, vs):
    def raw(k, z):
        return jnp.concatenate([ref[k, z] for ref in (xl, xh, rl, rh)], axis=0)

    tile0(tables, raw, 0, part, vs)


def y_sides(yl, yh, raw, layers):
    lane = iota((8, 128), 1)
    for k in range(4):
        for z in layers:
            for tile in range(4):
                g, at, width = block_of(k, z, tile)
                both = jnp.where(lane // width == at // width, yl[g], yh[g])
                raw[k, z, 8 * tile : 8 * tile + 8] = turn(both, -at)


def setup0(a, main, side, z):
    def both(k):
        return jnp.concatenate([main[k, z], side[k, z]], axis=1)

    h, sink, ux, uz, lz = both(PH), both(PSINK), both(PUX), both(PUZ), a[UZ, z - 1]
    hn = up(h, 1)
    hsum = h + hn
    uy = 2.0 * h * hn / jnp.where(hsum > 0.0, hsum, 1.0)
    a[UX, z], a[UY, z], a[UZ, z] = ux, uy, uz
    lx, ly = down(ux, 0), down(uy, 1)
    diag = sink + lz + uz + lx + ux + ly + uy
    rd = jnp.where(diag > 0.0, W / jnp.where(diag > 0.0, diag, 1.0), 0.0)
    a[RD, z] = rd
    a[C, z] = rd * both(PB)
    return diag, sink, ux, uy, uz, lx, ly, lz


def level0(tables, main, yl, yh, a, packed, raw, side, vs, hs, dd, res, t, m):
    lane8 = iota((8, 128), 1)
    y_sides(yl, yh, raw, range(2, Z0 - 2))
    tile0(tables, lambda k, z: raw[k, z], 128, side, vs, 2, Z0 - 2)
    row, lane = iota((32, 256), 0), iota((32, 256), 1)
    odd_row, odd_lane = row % 2 == 1, lane % 2 == 1
    a[UZ, 2] = jnp.concatenate([main[PUZ, 2], side[PUZ, 2]], axis=1)
    for z in range(3, Z0 - 3):
        diag, sink, ux, uy, uz, lx, ly, lz = setup0(a, main, side, z)
        if H <= z < H + 8:
            dd[z - H] = diag[0:16, 0:128]
            outer = sink + jnp.where(odd_row, ux, lx) + jnp.where(odd_lane, uy, ly)
            hs[z - H] = (outer + (uz if (z - H) % 2 == 1 else lz))[0:16, 0:128]

    def first(z):
        a[V, z] = smoothed(a, lambda k: a[C, k], z, z - 1, z + 1)

    each(4, Z0 - 4, first)

    def residual(z):
        v, beside = around(a, lambda k: a[V, k], z, z - 1, z + 1)
        res[z - H] = dd[z - H] * (1.5 * a[C, z] - v)[0:16, 0:128] + beside[0:16, 0:128]

    each(H, H + 8, residual)

    o_row = iota((16, 128), 0) % 2 == 1
    o_lane = iota((16, 128), 1) % 2 == 1

    def coarsen(z):
        lo, hi = H + 2 * z, H + 2 * z + 1

        def pair(ref):
            return ref[lo, 0:16, 0:128] + ref[hi, 0:16, 0:128]

        parts = (
            jnp.where(o_row, pair(a.at[UX]), 0.0),
            jnp.where(o_lane, pair(a.at[UY]), 0.0),
            a[UZ, hi, 0:16, 0:128],
            pair(main.at[PSINK]),
            res[2 * z] + res[2 * z + 1],
            hs[2 * z] + hs[2 * z + 1],
        )
        for k, part in enumerate(parts):
            t[k, z] = part
        for k in range(6):
            m[k, z] = fold_rows(t.at[k, z], 8)

    each(0, 4, coarsen)
    lower = lane8 < 64
    for s in range(2):
        parts = [jnp.where(lower, fold_lanes(m[k, s]), fold_lanes(m[k, 2 + s])) for k in range(6)]
        for k in range(4):
            packed[k, s] = parts[k]
        packed[4, s] = W * parts[4] / parts[5]


OUTER = (2, 3, Z0 - 4, Z0 - 3)


def outer0(tables, main, yl, yh, a0, field, raw, side, vs, a):
    for start, stop in ((0, 4), (Z0 - 4, Z0)):
        y_sides(yl, yh, raw, range(start, stop))
        tile0(tables, lambda k, z: raw[k, z], 128, side, vs, start, stop)
        a[UZ, start] = jnp.concatenate([main[PUZ, start], side[PUZ, start]], axis=1)
        for z in range(start + 1, stop - 1):
            setup0(a, main, side, z)
    for z in (3, 4, Z0 - 5, Z0 - 4):
        for k in (UX, UY, UZ, RD, C):
            a[k, z] = a0[k, z]
    for n, z in enumerate(OUTER):
        field[n] = smoothed(a, lambda k: a[C, k], z, z - 1, z + 1)


def pack_y1(own, b1, b3, b2, stack, lo, hi):
    lane = iota((8, 128), 1)
    block, last = (lane % 64) // 12, ((lane + 12) % 64) // 12
    blocks = (own, b1, b2, b3)
    for g in range(8):
        left = right = None
        for at in range(5):
            k, n = divmod(5 * g + at, 8)
            v = blocks[n // 2][k, n % 2]
            stack[5 * g + at] = v
            v = turn(v, 12 * at)
            left = v if at == 0 else jnp.where(block == at, v, left)
            right = v if at == 0 else jnp.where(last == at, v, right)
        lo[g] = left
        hi[g] = right


def pack_x1(stack, right, left, full, lo, hi):
    first = iota((8, 128), 0) < 4
    full[0:40] = stack[...]
    full[40:48] = right[...]
    full[48:56] = left[...]
    for n in range(28):
        a, b = full[2 * n], pltpu.roll(full[2 * n + 1], 4, 0)
        lo[n] = jnp.where(first, a, b)
        hi[n] = jnp.where(first, b, a)


def level12(full, xr, xl, xr2, xl2, before, a, b, sent, d1, r1, t1, m1, d2, r2, s1, s2, q2):
    gx, gy, gz = position()
    row, lane = iota((8, 128), 0), iota((8, 128), 1)
    y = gy * 64 + jnp.where(lane < 96, lane, lane - 128)
    in_y = (y >= 0) & (y < 256)
    first = row < 4

    def middle(i):
        near, far = xr2[i // 2], xl2[i // 2]
        if i % 2 == 0:
            return jnp.where(first, near, far)
        return pltpu.roll(jnp.where(first, far, near), 4, 0)

    for tile, tiles in enumerate((full, xr, None, xl)):
        of = middle if tiles is None else lambda i, tiles=tiles: tiles[i]
        edges = [(of(40 + g), of(48 + g)) for g in range(8)]
        x = gx * 8 + jnp.where(8 * tile + row < 20, 8 * tile + row, 8 * tile + row - 32)
        inside = in_y & (x >= 0) & (x < 128)
        rows = slice(8 * tile, 8 * tile + 8)
        for k in range(5):
            for n in range(8):
                g, at = divmod(8 * k + n, 5)
                v = of(8 * k + n)
                near = jnp.where((lane % 64) // 12 == at, *edges[g])
                for part in range(2):
                    own = turn(v, 64 * part)
                    beyond = turn(near, 64 - 64 * part - 12 * at)
                    value = jnp.where(inside, jnp.where(lane < 64, own, beyond), 0.0)
                    z = 4 * (n // 2) + 2 * part + n % 2
                    a[k, z, rows] = value
                    if k == SINK:
                        s1[z, rows] = value
    pre(a, d1, None, r1, 16)

    def keep1(k, z, value):
        value = fold_lanes(value)
        if k < 4:
            b[k, z] = value
        if k == SINK:
            s2[z] = value
        if k == 4:
            q2[z] = value

    halve(a, s1, r1, t1, keep1, 16, 32)
    pre(b, d2, q2, r2, 8)

    def keep2(k, z, value):
        m1[z, 0, k : k + 1] = value[0:1]
        m1[z, 1, k : k + 1] = value[1:2]

    m1[...] = jnp.zeros((4, 2, 8, 128), F32)
    halve(b, s2, r2, t1.at[:, :, 0:16], keep2, 8, 16)
    total = jnp.zeros((8, 128), F32)
    for z in range(4):
        zg = lax.rem(z + gz, 4)
        for s in range(2):
            v = m1[z, s]
            v = pick(v + up(v, 1), 2 * (lane % 16))
            total = jnp.where(lane // 16 == lax.rem(2 * zg + s + gy, 8), v, total)
    for tile in range(5):
        value = total
        for i in range(8):
            value = jnp.where(row == i, total[(8 * tile + i) % 5 : (8 * tile + i) % 5 + 1], value)
        for i in range(8):
            sent[40 * i + 8 * tile : 40 * i + 8 * tile + 8] = value


def cut(v):
    return jnp.concatenate([v[0:16], v[24:32]], axis=0)


class Cut:
    def __init__(self, ref):
        self.ref = ref

    def __getitem__(self, at):
        return cut(self.ref[at])


def sweep(a, src, dst, n, layers=None):
    for z in layers or range(n):
        dst[z % n] = smoothed(a, lambda k: src[k], z % n, (z - 1) % n, (z + 1) % n)


def solve(
    got, a0, v0, a1, a2, pressure, left,
    got3, t3, e1, g4, g3, g2, g1, g0, b3, w0,
):
    a3, a4, d3, d4, r3, r4, s3, s4, e2, e3, e4, f2, q5 = (Held() for _ in range(13))
    gx, gy, gz = position()
    lane = iota((16, 128), 1)
    for k in range(5):
        rows = [got[pl.ds(80 * g + k, 16, stride=5), :] for g in range(4)]
        rows = rows + [turn(value, 64) for value in rows]
        for z in range(4):
            for s in range(2):
                at = 2 * z + s
                value = rows[0]
                for g in range(1, 8):
                    value = jnp.where(lane // 16 == (at + g) % 8, rows[g], value)
                value = turn(value, -16 * at)
                got3[k, z, pl.ds(s, 16, stride=2), :] = value
    for z in range(4):
        for k in range(4):
            a3[k, z] = got3[k, z]
        s3[z], r3[z] = got3[SINK, z], got3[4, z]
    pre(a3, d3, r3, e3, 4)

    def keep3(k, z, value):
        value = fold_lanes(value)
        if k < 4:
            a4[k, z] = value
        if k == SINK:
            s4[z] = value
        if k == 4:
            r4[z] = value

    halve(a3, s3, e3, t3, keep3, 4, 32)
    pre(a4, d4, r4, e4, 2)

    def keep4(k, z, value):
        q5[k] = fold_lanes(value)

    halve(a4, s4, e4, t3.at[:, :, 0:16], keep4, 2, 16)
    ux, uy, uz, sink, r = q5[0], q5[1], q5[2], q5[3], q5[4]
    lx, ly = down(ux, 0), down(uy, 1)
    diag = sink + uz + uz + ux + lx + uy + ly
    rd = W / diag
    c = rd * r
    ux, lx, uy, ly = rd * ux, rd * lx, rd * uy, rd * ly
    v = c
    for _ in range(COARSE_SWEEPS - 1):
        beside = (ux * up(v, 0) + lx * down(v, 0)) + (uy * up(v, 1) + ly * down(v, 1))
        v = (v * (1.0 / 3.0) + c) + beside

    e = spread_rows(g4, spread_lanes(v))
    for z in range(2):
        a4[V, z] = a4[V, z] + e
    sweep(a4, Field(a4, V), e4, 2)
    sweep(a4, e4, r4, 2)
    for z in range(2):
        e = spread_rows(g3.at[z], spread_lanes(r4[z]))
        a3[V, 2 * z] = a3[V, 2 * z] + e
        a3[V, 2 * z + 1] = a3[V, 2 * z + 1] + e
    sweep(a3, Field(a3, V), e3, 4)
    sweep(a3, e3, r3, 4)
    for z in range(4):
        b3[z, 8:40] = r3[z]
        b3[z, 0:8] = r3[z][24:32]
        b3[z, 40:48] = r3[z][0:8]
    lane = iota((8, 128), 1) % 64
    index = jnp.where(lane < 40, lane // 2, lane // 2 - 32) + 16 * gy
    index = lax.rem(index + 64, 64)
    for z in range(4):
        e = b3[lax.rem(z + gz, 4), pl.ds(2 * gx + 5, 8), :]
        e = pick(pltpu.roll(e, 5, 0), index)
        e = spread_rows(g2.at[z], e)
        e2[2 * z] = a2[V, 2 * z] + e
        e2[2 * z + 1] = a2[V, 2 * z + 1] + e
    sweep(a2, e2, f2, 8)
    sweep(a2, f2, e2, 8, range(-2, 4))
    for z in range(-2, 4):
        e = cut(spread_rows(g1.at[z % 8], spread_lanes(e2[z % 8])))
        for zf in (2 * z % 16, 2 * z % 16 + 1):
            e1[0, zf] = cut(a1[V, zf]) + e
    sweep(Cut(a1), e1.at[0], e1.at[1], 16, range(-3, 7))
    sweep(Cut(a1), e1.at[1], e1.at[0], 16, range(-2, 6))
    upper = iota((8, 128), 0) < 4
    for zc in range(-2, 6):
        v = e1[0, zc % 16]
        v = jnp.concatenate([v[0:8], jnp.where(upper, v[8:16], v[16:24])], axis=0)
        for half in range(2):
            e = spread_rows(g0.at[half, zc + 2], spread_lanes(v, 64 * half))
            lanes = slice(128 * half, 128 * half + 128)
            for z in (2 * zc, 2 * zc + 1):
                if -3 <= z <= 10:
                    old = v0.at[OUTER.index(z + H)] if z + H in OUTER else a0.at[V, z + H]
                    w0[0, z + H, :, lanes] = old[:, lanes] + e

    def sweep0(src, dst):
        def body(z):
            w0[dst, z] = smoothed(a0, lambda k: w0[src, k], z, z - 1, z + 1)

        return body

    each(3, Z0 - 3, sweep0(0, 1))
    each(4, Z0 - 4, sweep0(1, 0))

    def last(z):
        v, beside = around(a0, lambda k: w0[0, k], z, z - 1, z + 1)
        r = W / a0[RD, z] * (1.5 * a0[C, z] - v) + beside
        pressure[z - H] = v[0:16, 0:128]
        left[z - H] = r[0:16, 0:128]

    each(H, H + 8, last)


def shift(value, axis, by):
    count = lax.axis_size(axis)
    return lax.ppermute(value, axis, [((i + by) % count, i) for i in range(count)])


def local(facies, boundary, hc, vc, source, density):
    tables = jnp.broadcast_to(jnp.concatenate([hc, vc])[:, None], (16, 128))
    lo, hi, own = call(
        pack_z,
        [(4 * H - 2, 16, 128)] * 2 + [(4, 8, 16, 128)],
        facies, boundary, source, density,
        spaces=[HBM] * 4,
        scratch=[
            pltpu.VMEM((8, 16, 128), jnp.int32), pltpu.VMEM((8, 16, 128), jnp.int32),
            pltpu.SemaphoreType.DMA((4,)),
        ],
        limit=60,
        pin=True,
    )
    above, below = shift(lo, "gz", 1), shift(hi, "gz", -1)
    xl, xh, lo, hi = call(
        pack_x, [(4, Z0, 8, 128)] * 2 + [(XTILES, 8, 128)] * 2, own, above, below
    )
    ml, mh = shift(lo, "gx", 1), shift(hi, "gx", -1)
    rl, rh, lo, hi = call(
        pack_y, [(4, Z0, 8, 128)] * 2 + [(YTILES, 8, 128)] * 2, xl, xh, ml, mh
    )
    yl, yh = shift(lo, "gy", 1), shift(hi, "gy", -1)
    (main,) = call(
        main0, [(5, Z0, 32, 128)], tables, xl, xh, rl, rh, scratch=[(Z0, 32, 128)],
    )
    a0, packed = call(
        level0,
        [(6, Z0, 32, 256), (5, 2, 8, 128)],
        tables, main, yl, yh,
        scratch=[
            (4, Z0, 32, 128), (5, Z0, 32, 128), (Z0, 32, 128), (8, 16, 128), (8, 16, 128),
            (8, 16, 128), (6, 4, 16, 128), (6, 4, 8, 128),
        ],
    )
    (v0,) = call(
        outer0, [(4, 32, 256)], tables, main, yl, yh, a0,
        scratch=[(4, Z0, 32, 128), (5, Z0, 32, 128), (Z0, 32, 128), (6, Z0, 32, 256)],
    )
    blocks = [shift(packed, "gz", n) for n in (1, 3, 2)]
    stack, lo, hi = call(pack_y1, [(40, 8, 128)] + [(8, 8, 128)] * 2, packed, *blocks)
    right, left = shift(lo, "gy", 1), shift(hi, "gy", -1)
    full, lo, hi = call(pack_x1, [(56, 8, 128)] + [(28, 8, 128)] * 2, stack, right, left)
    near = (shift(full, "gx", 1), shift(full, "gx", -1), shift(lo, "gx", 2), shift(hi, "gx", -2))
    a1, a2, sent = call(
        level12,
        [(6, 16, 32, 128), (6, 8, 16, 128), (320, 128)],
        full, *near, v0,
        scratch=[
            (16, 32, 128), (16, 32, 128), (5, 8, 32, 128), (4, 2, 8, 128),
            (8, 16, 128), (8, 16, 128), (16, 32, 128), (8, 16, 128), (8, 16, 128),
        ],
    )
    got = lax.all_to_all(sent.reshape(64, 1, 640), ("gy", "gx"), 0, 0).reshape(320, 128)
    return tuple(
        call(
            solve,
            [(8, 16, 128), (8, 16, 128)],
            got, a0, v0, a1, a2,
            scratch=[
                (5, 4, 32, 128), (5, 2, 32, 128), (2, 16, 24, 128),
                (16, 128), (2, 32, 128), (4, 16, 128), (8, 32, 128), (2, 8, 32, 128),
                (4, 48, 128), (2, Z0, 32, 256),
            ],
        )
    )


def solution(mesh):
    split = P("gz", "gx", "gy")
    return jax.shard_map(
        local,
        mesh=mesh,
        in_specs=(split, split, P(), P(), split, split),
        out_specs=(split, split),
        check_vma=False,
    )
```
